32 devices in a mesh: rep: 4 (over x, core), fsdp: 8 (over z, y).
Axes of the slice: x: 2, y: 2, z: 4, core: 2. Of those that a mesh axis runs over, the one named last changes fastest.
Arguments:
- layer_in: bfloat16 [2, 8192, 1024], P(None, ('rep', 'fsdp')), may hold values from -6 to 6
- segments: int32 [2, 8192], P(None, ('rep', 'fsdp')), may hold values from 0 to 7, never falling along the last dimension, each value on 1 to 2000 neighbouring positions
- w_in: bfloat16 [1024, 3072], P(None, 'fsdp'), may hold values from -0.1875 to 0.1875
- w_out: bfloat16 [1024, 1024], P(None, 'fsdp'), may hold values from -0.1875 to 0.1875
- w_gate: bfloat16 [1024, 4608], P(None, 'fsdp'), may hold values from -0.1875 to 0.1875
- w_up: bfloat16 [1024, 4608], P(None, 'fsdp'), may hold values from -0.1875 to 0.1875
- w_down: bfloat16 [4608, 1024], P(None, 'fsdp'), may hold values from -0.09375 to 0.09375
- conv_taps: bfloat16 [3, 1024], P(None, 'fsdp'), may hold values from -3 to 3
- gain_one: bfloat16 [1024], P('fsdp'), may hold values from 0.099609375 to 1.8984375
- gain_two: bfloat16 [1024], P('fsdp'), may hold values from 0.099609375 to 1.8984375
- cotangent: bfloat16 [2, 8192, 1024], P(None, ('rep', 'fsdp')), may hold values from -6 to 6
Outputs:
- layer_out: float32 [2, 8192, 1024], P(None, ('rep', 'fsdp'))
- grad_layer_in: float32 [2, 8192, 1024], P(None, ('rep', 'fsdp'))
- grad_w_in: float32 [1024, 3072], P(None, 'fsdp')
- grad_w_out: float32 [1024, 1024], P(None, 'fsdp')
- grad_w_gate: float32 [1024, 4608], P(None, 'fsdp')
- grad_w_up: float32 [1024, 4608], P(None, 'fsdp')
- grad_w_down: float32 [4608, 1024], P(None, 'fsdp')
- grad_conv_taps: float32 [3, 1024], P(None, 'fsdp')
- grad_gain_one: float32 [1024], P('fsdp')
- grad_gain_two: float32 [1024], P('fsdp')
The draws below stay inside these ranges and needn't reach their ends.
Inputs may be any that keep to these rules, and one draw needn't show every extreme that they name: `segments`: document numbers never fall along a micro-batch's 8192 tokens; a document holds at most 2000 tokens.
All inputs are finite; a program needn't handle non-finite values.
Results may differ from the reference program's by a relative error of at most 0.013.
Values may be sent and summed in bfloat16 or wider, within the bound.
A program may use at most 256 MiB of HBM per device.

```python
import math
import jax
import jax.numpy as jnp
import numpy as np
from jax import lax

D = 1024
FF = 4608
KERNEL = 3
MICRO = 2
DOC_MOST = 2000
ROWS = 8192
DOCS = 8
N_REP = 4


def spiked(drawn, own_key, source, target, parts, factor):
    owner, partner = [(jnp.arange(drawn.shape[position]) // (drawn.shape[position] // parts)).reshape([-1 if axis == position else 1 for axis in range(drawn.ndim)]) for position in (source, target)]
    chosen = jax.random.permutation(own_key, parts)[partner]
    strong = (owner == chosen) | (owner == (partner + parts // 2) % parts)
    return jnp.where(strong, factor * drawn, drawn)


def block_levels(rng, extent, shards, smallest, top_value):
    def one(position, blocks):
        steps = jax.random.uniform(jax.random.fold_in(jax.random.fold_in(rng, 6), position), (blocks,), jnp.float32, smallest / len(shards), top_value / len(shards))
        return jnp.repeat(jnp.exp(steps), extent[position] // blocks).reshape((-1,) + (1,) * (len(extent) - position - 1))

    level = one(*shards[0])
    for cut in shards[1:]:
        level = level * one(*cut)
    return level


def length_profile(number_of, total, most, skew):
    loads = [(1 << 20) // math.isqrt(standing ** skew) + 1 for standing in range(2, number_of + 1)]
    spare, holding = total - most - (number_of - 1), [1] * (number_of - 1)
    while spare > 0:
        movable = [i for i in range(number_of - 1) if holding[i] < most]
        pool, remaining = sum([loads[i] for i in movable]), spare
        for i in movable:
            more = min(most - holding[i], max(1, remaining * loads[i] // pool), spare)
            holding[i] = holding[i] + more
            spare = spare - more
    return np.array([most] + holding)


def ragged(key, count, total, limit, slope):
    if count == 2:
        one = jax.random.randint(key, (), max(1, total - limit), min(limit, total - 1) + 1)
        return jnp.stack([one, total - one])
    tallies = jnp.asarray(length_profile(count, total, limit, slope), jnp.int32)
    pairs = (count - 1) // 2
    donor, taker = tallies[1:1 + 2 * pairs:2], tallies[2:2 + 2 * pairs:2]
    room = jnp.minimum(donor - 1, limit - taker)
    shifted = jax.random.randint(jax.random.fold_in(key, 1), (pairs,), 0, 1 << 20) % (room + 1)
    tallies = tallies.at[1:1 + 2 * pairs:2].set(donor - shifted).at[2:2 + 2 * pairs:2].set(taker + shifted)
    return tallies[jax.random.permutation(jax.random.fold_in(key, 2), count)]


def gaussian(stream_key, extent, width, most, split=(), dtype=jnp.bfloat16):
    entries = width * jax.random.normal(stream_key, extent, jnp.float32)
    if split:
        entries = entries * block_levels(stream_key, extent, split, -0.22, 0.18)
    return jnp.clip(entries, -most, most).astype(dtype)


def gaussian_with(stream_key, extent, spread, most, cuts, heavy, dtype=jnp.bfloat16):
    array = spread * jax.random.normal(stream_key, extent, jnp.float32)
    if cuts:
        array = array * block_levels(stream_key, extent, cuts, -0.22, 0.18)
    return jnp.clip(spiked(array, jax.random.fold_in(stream_key, 3), *heavy), -most, most).astype(dtype)


def setup_inputs(seed: int = 0) -> dict:
    key_list = jax.random.split(jax.random.key(seed), 12)
    layer_in = gaussian(key_list[0], (MICRO, ROWS, D), 1.0, 6.0, ((1, 32),))
    segments = jax.vmap(lambda own: jnp.searchsorted(jnp.cumsum(ragged(own, DOCS, ROWS, DOC_MOST, 0)), jnp.arange(ROWS), side="right"))(jax.random.split(key_list[1], MICRO)).reshape((MICRO, ROWS)).astype(jnp.int32)
    w_in = gaussian(key_list[2], (D, 3 * D), D ** -0.5, 0.1875, ((1, 8),))
    w_out = gaussian(key_list[3], (D, D), D ** -0.5, 0.1875, ((1, 8),))
    w_gate = gaussian(key_list[4], (D, FF), D ** -0.5, 0.1875, ((1, 8),))
    w_up = gaussian(key_list[5], (D, FF), D ** -0.5, 0.1875, ((1, 8),))
    w_down = gaussian(key_list[6], (FF, D), FF ** -0.5, 0.09375, ((1, 8),))
    conv_taps = gaussian(key_list[7], (KERNEL, D), 0.7, 3.0, ((1, 8),))
    gain_one = jnp.clip(1.0 + 0.18 * jax.random.normal(key_list[8], (D,), jnp.float32), 0.099609375, 1.8984375).astype(jnp.bfloat16)
    gain_two = jnp.clip(1.0 + 0.18 * jax.random.normal(key_list[9], (D,), jnp.float32), 0.099609375, 1.8984375).astype(jnp.bfloat16)
    cotangent = gaussian_with(key_list[10], (MICRO, ROWS, D), 1.0, 6.0, ((1, 32),), (1, 2, 32, 2.75))
    return dict(layer_in=layer_in, segments=segments, w_in=w_in, w_out=w_out, w_gate=w_gate, w_up=w_up, w_down=w_down, conv_taps=conv_taps, gain_one=gain_one, gain_two=gain_two, cotangent=cotangent)


@jax.custom_vjp
def low(v):
    return lax.optimization_barrier(v.astype(jnp.bfloat16)).astype(jnp.float32)

@jax.custom_vjp
def low_back(v):
    return v

def low_keep(v):
    return (low(v), None)

def low_pass(kept, grad):
    return (grad,)

def back_keep(v):
    return (v, None)

def back_low(kept, grad):
    return (low(grad),)
low.defvjp(low_keep, low_pass)
low_back.defvjp(back_keep, back_low)
epsilon = 1e-05

def matmul(left_side, right_side):
    return jnp.dot(left_side, right_side, precision=lax.Precision.HIGHEST, preferred_element_type=jnp.float32)

def rms_scale(values):
    return lax.rsqrt(lax.optimization_barrier(jnp.mean(values * values, axis=-1, keepdims=True)) + epsilon)

def causal_taps(product_bx, doc_ids, tap_values):
    model_width = product_bx.shape[1]
    conv_out = tap_values[0] * product_bx
    for offset in (1, 2):
        earlier = jnp.concatenate([jnp.zeros((offset, model_width), jnp.float32), product_bx[:-offset]], 0)
        earlier_ids = jnp.concatenate([jnp.full((offset,), -1, jnp.int32), doc_ids[:-offset]], 0)
        matching = (earlier_ids == doc_ids).astype(jnp.float32)[:, None]
        conv_out = conv_out + tap_values[offset] * matching * earlier
    return conv_out

def layer_block(residual, doc_ids, params):
    w_in, w_out, w_gate, w_up, w_down, conv_taps, gain_one, gain_two = params
    model_width = residual.shape[1]
    normed_one = low(residual * rms_scale(residual) * gain_one)
    projected = low_back(matmul(normed_one, w_in))
    b_part = projected[:, :model_width]
    c_part = projected[:, model_width:2 * model_width]
    x_part = projected[:, 2 * model_width:]
    conv_out = causal_taps(b_part * x_part, doc_ids, conv_taps)
    gated = low(c_part * conv_out)
    middle = residual + low_back(matmul(gated, w_out))
    normed_two = low(middle * rms_scale(middle) * gain_two)
    gate_pre = low_back(matmul(normed_two, w_gate))
    up_pre = low_back(matmul(normed_two, w_up))
    hidden = low(jax.nn.silu(gate_pre) * up_pre)
    return middle + low_back(matmul(hidden, w_down))

def reference(layer_in, segments, w_in, w_out, w_gate, w_up, w_down, conv_taps, gain_one, gain_two, cotangent):
    micro_count, row_count, model_width = layer_in.shape
    seq_count = micro_count * N_REP
    seq_length = row_count // N_REP
    inputs = layer_in.astype(jnp.float32).reshape(seq_count, seq_length, model_width)
    doc_ids = segments.reshape(seq_count, seq_length)
    cotangents = cotangent.astype(jnp.float32).reshape(seq_count, seq_length, model_width)
    params = tuple((weight.astype(jnp.float32) for weight in (w_in, w_out, w_gate, w_up, w_down, conv_taps, gain_one, gain_two)))
    checked_block = jax.checkpoint(layer_block)

    def whole_layer(inputs, params):

        def scan_step(scan_carry, scan_item):
            return (scan_carry, checked_block(scan_item[0], scan_item[1], params))
        _, outputs = lax.scan(scan_step, jnp.zeros((), jnp.float32), (inputs, doc_ids))
        return outputs
    outputs, pullback = jax.vjp(whole_layer, inputs, params)
    grad_inputs, grad_params = pullback(cotangents)
    return (outputs.reshape(micro_count, row_count, model_width), grad_inputs.reshape(micro_count, row_count, model_width), grad_params[0], grad_params[1], grad_params[2], grad_params[3], grad_params[4], grad_params[5], grad_params[6], grad_params[7])
```

```python
import jax
import jax.numpy as jnp
from jax import lax
from jax.sharding import PartitionSpec as P

epsilon = 1e-05


def shifted(block, axis, distance):
    devices = range(lax.axis_size(axis))
    route = [(i - distance, i) for i in devices if i - distance in devices]
    return lax.ppermute(block, axis, route)


def rms_scale(values):
    return lax.rsqrt(jnp.mean(values * values, axis=-1, keepdims=True) + epsilon)


def matmul(left_side, right_side):
    return jnp.dot(left_side, right_side, preferred_element_type=jnp.float32)


def contract_rows(left_side, right_side):
    return lax.dot_general(
        left_side, right_side, (((0,), (0,)), ((), ())), preferred_element_type=jnp.float32
    )


def against_rows(left_side, right_side):
    return lax.dot_general(
        left_side, right_side, (((1,), (1,)), ((), ())), preferred_element_type=jnp.float32
    )


def forward_pass(layer_rows, doc_rows, weights):
    w_in, w_out, w_gate, w_up, w_down, conv_taps, gain_one, gain_two = weights
    residual = layer_rows.astype(jnp.float32)
    model_width = residual.shape[1]
    seq_rows = residual.shape[0]
    tap_values = conv_taps.astype(jnp.float32)
    scale_one = rms_scale(residual)
    normed_one = (residual * scale_one * gain_one.astype(jnp.float32)).astype(jnp.bfloat16)
    projected = matmul(normed_one, w_in)
    b_part = projected[:, :model_width]
    c_part = projected[:, model_width : 2 * model_width]
    x_part = projected[:, 2 * model_width :]
    product_bx = b_part * x_part
    doc_float = doc_rows.astype(jnp.float32)
    rim_values, rim_ids = shifted((product_bx[-2:], doc_float[-2:]), "fsdp", 1)
    extended = jnp.concatenate([rim_values, product_bx], 0)
    extended_ids = jnp.concatenate([rim_ids, doc_float], 0)
    conv_out = tap_values[0] * product_bx
    doc_masks = []
    for offset in (1, 2):
        matching = (extended_ids[2 - offset : 2 - offset + seq_rows] == doc_float).astype(
            jnp.float32
        )[:, None]
        doc_masks.append(matching)
        conv_out = (
            conv_out + tap_values[offset] * matching * extended[2 - offset : 2 - offset + seq_rows]
        )
    gated_rows = (c_part * conv_out).astype(jnp.bfloat16)
    middle = residual + matmul(gated_rows, w_out)
    scale_two = rms_scale(middle)
    normed_two = (middle * scale_two * gain_two.astype(jnp.float32)).astype(jnp.bfloat16)
    gate_pre = matmul(normed_two, w_gate)
    up_pre = matmul(normed_two, w_up)
    hidden = (jax.nn.silu(gate_pre) * up_pre).astype(jnp.bfloat16)
    output = middle + matmul(hidden, w_down)
    saved_state = (
        residual,
        scale_one,
        normed_one,
        projected,
        extended,
        doc_masks,
        conv_out,
        gated_rows,
        middle,
        scale_two,
        normed_two,
        gate_pre,
        up_pre,
        hidden,
    )
    return (output, saved_state)


def backward_pass(cotan_rows, weights, saved_state):
    w_in, w_out, w_gate, w_up, w_down, conv_taps, gain_one, gain_two = weights
    (
        residual,
        scale_one,
        normed_one,
        projected,
        extended,
        doc_masks,
        conv_out,
        gated_rows,
        middle,
        scale_two,
        normed_two,
        gate_pre,
        up_pre,
        hidden,
    ) = saved_state
    model_width = residual.shape[1]
    seq_rows = residual.shape[0]
    tap_values = conv_taps.astype(jnp.float32)
    b_part = projected[:, :model_width]
    c_part = projected[:, model_width : 2 * model_width]
    x_part = projected[:, 2 * model_width :]
    grad_out = cotan_rows.astype(jnp.float32)
    grad_down = contract_rows(hidden, cotan_rows)
    grad_hidden = against_rows(cotan_rows, w_down)
    gate_prob = jax.nn.sigmoid(gate_pre)
    grad_gate = (grad_hidden * up_pre * gate_prob * (1.0 + gate_pre * (1.0 - gate_prob))).astype(
        jnp.bfloat16
    )
    grad_up = (grad_hidden * gate_pre * gate_prob).astype(jnp.bfloat16)
    grad_wgate = contract_rows(normed_two, grad_gate)
    grad_wup = contract_rows(normed_two, grad_up)
    grad_normed_two = against_rows(grad_gate, w_gate) + against_rows(grad_up, w_up)
    grad_gtwo = jnp.sum(grad_normed_two * middle * scale_two, axis=0)
    weighted = grad_normed_two * gain_two.astype(jnp.float32)
    grad_middle = (
        grad_out
        + scale_two * weighted
        - middle * scale_two**3 * jnp.mean(weighted * middle, axis=-1, keepdims=True)
    )
    grad_branch = grad_middle.astype(jnp.bfloat16)
    grad_wout = contract_rows(gated_rows, grad_branch)
    grad_gated = against_rows(grad_branch, w_out)
    grad_c = grad_gated * conv_out
    grad_conv = grad_gated * c_part
    grad_ext = jnp.pad(tap_values[0] * grad_conv, ((2, 0), (0, 0)))
    tap_rows = [jnp.sum(grad_conv * extended[2:], axis=0)]
    for offset, matching in zip((1, 2), doc_masks):
        masked_grad = matching * grad_conv
        grad_ext = grad_ext + jnp.pad(
            tap_values[offset] * masked_grad, ((2 - offset, offset), (0, 0))
        )
        tap_rows.append(jnp.sum(masked_grad * extended[2 - offset : 2 - offset + seq_rows], axis=0))
    rim_back = shifted(grad_ext[:2], "fsdp", -1)
    grad_bx = grad_ext[2:] + jnp.pad(rim_back, ((seq_rows - 2, 0), (0, 0)))
    grad_taps = jnp.stack(tap_rows)
    grad_proj = jnp.concatenate([grad_bx * x_part, grad_c, grad_bx * b_part], 1).astype(
        jnp.bfloat16
    )
    grad_win = contract_rows(normed_one, grad_proj)
    grad_normed_one = against_rows(grad_proj, w_in)
    grad_gone = jnp.sum(grad_normed_one * residual * scale_one, axis=0)
    weighted_one = grad_normed_one * gain_one.astype(jnp.float32)
    grad_input = (
        grad_middle
        + scale_one * weighted_one
        - residual * scale_one**3 * jnp.mean(weighted_one * residual, axis=-1, keepdims=True)
    )
    local_grads = (
        grad_win,
        grad_wout,
        grad_wgate,
        grad_wup,
        grad_down,
        grad_taps,
        grad_gone,
        grad_gtwo,
    )
    return (grad_input, local_grads)


def per_device(
    layer_in, segments, w_in, w_out, w_gate, w_up, w_down, conv_taps, gain_one, gain_two, cotangent
):
    outputs = []
    input_grads = []
    totals = None
    owned_grads = None
    for batch_index in range(layer_in.shape[0]):
        weights_now = (
            lax.all_gather(w_in, "fsdp", axis=1, tiled=True),
            lax.all_gather(w_out, "fsdp", axis=1, tiled=True),
            lax.all_gather(w_gate, "fsdp", axis=1, tiled=True),
            lax.all_gather(w_up, "fsdp", axis=1, tiled=True),
            lax.all_gather(w_down, "fsdp", axis=1, tiled=True),
            lax.all_gather(conv_taps, "fsdp", axis=1, tiled=True),
            lax.all_gather(gain_one, "fsdp", axis=0, tiled=True),
            lax.all_gather(gain_two, "fsdp", axis=0, tiled=True),
        )
        output, saved_state = forward_pass(
            layer_in[batch_index], segments[batch_index], weights_now
        )
        outputs.append(output)
        grad_input, local_grads = backward_pass(cotangent[batch_index], weights_now, saved_state)
        input_grads.append(grad_input)
        totals = local_grads if batch_index == 0 else jax.tree.map(jnp.add, totals, local_grads)
    owned_grads = tuple(
        lax.psum_scatter(
            total.astype(jnp.bfloat16), "fsdp", scatter_dimension=total.ndim - 1, tiled=True
        )
        for total in totals
    )
    summed = (
        lax.psum(owned_grads[0].astype(jnp.bfloat16), "rep").astype(jnp.float32),
        lax.psum(owned_grads[1].astype(jnp.bfloat16), "rep").astype(jnp.float32),
        lax.psum(owned_grads[2].astype(jnp.bfloat16), "rep").astype(jnp.float32),
        lax.psum(owned_grads[3].astype(jnp.bfloat16), "rep").astype(jnp.float32),
        lax.psum(owned_grads[4].astype(jnp.bfloat16), "rep").astype(jnp.float32),
        lax.psum(owned_grads[5].astype(jnp.bfloat16), "rep").astype(jnp.float32),
        lax.psum(owned_grads[6].astype(jnp.bfloat16), "rep").astype(jnp.float32),
        lax.psum(owned_grads[7].astype(jnp.bfloat16), "rep").astype(jnp.float32),
    )
    return (
        jnp.stack(outputs),
        jnp.stack(input_grads),
        summed[0],
        summed[1],
        summed[2],
        summed[3],
        summed[4],
        summed[5],
        summed[6],
        summed[7],
    )


def solution(mesh):
    return jax.shard_map(
        per_device,
        mesh=mesh,
        in_specs=(
            P(None, ("rep", "fsdp"), None),
            P(None, ("rep", "fsdp")),
            P(None, "fsdp"),
            P(None, "fsdp"),
            P(None, "fsdp"),
            P(None, "fsdp"),
            P(None, "fsdp"),
            P(None, "fsdp"),
            P("fsdp"),
            P("fsdp"),
            P(None, ("rep", "fsdp"), None),
        ),
        out_specs=(
            P(None, ("rep", "fsdp"), None),
            P(None, ("rep", "fsdp"), None),
            P(None, "fsdp"),
            P(None, "fsdp"),
            P(None, "fsdp"),
            P(None, "fsdp"),
            P(None, "fsdp"),
            P(None, "fsdp"),
            P("fsdp"),
            P("fsdp"),
        ),
        check_vma=False,
    )
```

```python
import jax
import jax.numpy as jnp
from jax import lax
from jax.experimental import pallas as pl
from jax.experimental.pallas import tpu as pltpu
from jax.sharding import PartitionSpec as P

epsilon = 1e-05
VMEM_BYTES = 65000 << 10


def shifted(block, axis, distance):
    devices = range(lax.axis_size(axis))
    route = [(i - distance, i) for i in devices if i - distance in devices]
    return lax.ppermute(block, axis, route)


def rms_scale(values):
    return lax.rsqrt(jnp.mean(values * values, axis=-1, keepdims=True) + epsilon)


def matmul(left_side, right_side):
    return jnp.dot(left_side, right_side, preferred_element_type=jnp.float32)


def contract_rows(left_side, right_side):
    return lax.dot_general(
        left_side, right_side, (((0,), (0,)), ((), ())), preferred_element_type=jnp.float32
    )


def against_rows(left_side, right_side):
    return lax.dot_general(
        left_side, right_side, (((1,), (1,)), ((), ())), preferred_element_type=jnp.float32
    )


def forward_pass(layer_rows, doc_rows, weights):
    w_in, w_out, w_gate, w_up, w_down, conv_taps, gain_one, gain_two = weights
    residual = layer_rows.astype(jnp.float32)
    model_width = residual.shape[1]
    seq_rows = residual.shape[0]
    tap_values = conv_taps.astype(jnp.float32)
    scale_one = rms_scale(residual)
    normed_one = (residual * scale_one * gain_one.astype(jnp.float32)).astype(jnp.bfloat16)
    projected = matmul(normed_one, w_in)
    b_part = projected[:, :model_width]
    c_part = projected[:, model_width : 2 * model_width]
    x_part = projected[:, 2 * model_width :]
    product_bx = b_part * x_part
    doc_float = doc_rows.astype(jnp.float32)
    rim_values, rim_ids = shifted((product_bx[-2:], doc_float[-2:]), "fsdp", 1)
    extended = jnp.concatenate([rim_values, product_bx], 0)
    extended_ids = jnp.concatenate([rim_ids, doc_float], 0)
    conv_out = tap_values[0] * product_bx
    doc_masks = []
    for offset in (1, 2):
        matching = (extended_ids[2 - offset : 2 - offset + seq_rows] == doc_float).astype(
            jnp.float32
        )[:, None]
        doc_masks.append(matching)
        conv_out = (
            conv_out + tap_values[offset] * matching * extended[2 - offset : 2 - offset + seq_rows]
        )
    gated_rows = (c_part * conv_out).astype(jnp.bfloat16)
    middle = residual + matmul(gated_rows, w_out)
    scale_two = rms_scale(middle)
    normed_two = (middle * scale_two * gain_two.astype(jnp.float32)).astype(jnp.bfloat16)
    gate_pre = matmul(normed_two, w_gate)
    up_pre = matmul(normed_two, w_up)
    hidden = (jax.nn.silu(gate_pre) * up_pre).astype(jnp.bfloat16)
    output = middle + matmul(hidden, w_down)
    saved_state = (
        residual,
        scale_one,
        normed_one,
        projected,
        extended,
        doc_masks,
        conv_out,
        gated_rows,
        middle,
        scale_two,
        normed_two,
        gate_pre,
        up_pre,
        hidden,
    )
    return (output, saved_state)


def backward_pass(cotan_rows, weights, saved_state):
    w_in, w_out, w_gate, w_up, w_down, conv_taps, gain_one, gain_two = weights
    (
        residual,
        scale_one,
        normed_one,
        projected,
        extended,
        doc_masks,
        conv_out,
        gated_rows,
        middle,
        scale_two,
        normed_two,
        gate_pre,
        up_pre,
        hidden,
    ) = saved_state
    model_width = residual.shape[1]
    seq_rows = residual.shape[0]
    tap_values = conv_taps.astype(jnp.float32)
    b_part = projected[:, :model_width]
    c_part = projected[:, model_width : 2 * model_width]
    x_part = projected[:, 2 * model_width :]
    grad_out = cotan_rows.astype(jnp.float32)
    grad_down = contract_rows(hidden, cotan_rows)
    grad_hidden = against_rows(cotan_rows, w_down)
    gate_prob = jax.nn.sigmoid(gate_pre)
    grad_gate = (grad_hidden * up_pre * gate_prob * (1.0 + gate_pre * (1.0 - gate_prob))).astype(
        jnp.bfloat16
    )
    grad_up = (grad_hidden * gate_pre * gate_prob).astype(jnp.bfloat16)
    grad_wgate = contract_rows(normed_two, grad_gate)
    grad_wup = contract_rows(normed_two, grad_up)
    grad_normed_two = against_rows(grad_gate, w_gate) + against_rows(grad_up, w_up)
    grad_gtwo = jnp.sum(grad_normed_two * middle * scale_two, axis=0)
    weighted = grad_normed_two * gain_two.astype(jnp.float32)
    grad_middle = (
        grad_out
        + scale_two * weighted
        - middle * scale_two**3 * jnp.mean(weighted * middle, axis=-1, keepdims=True)
    )
    grad_branch = grad_middle.astype(jnp.bfloat16)
    grad_wout = contract_rows(gated_rows, grad_branch)
    grad_gated = against_rows(grad_branch, w_out)
    grad_c = grad_gated * conv_out
    grad_conv = grad_gated * c_part
    grad_ext = jnp.pad(tap_values[0] * grad_conv, ((2, 0), (0, 0)))
    tap_rows = [jnp.sum(grad_conv * extended[2:], axis=0)]
    for offset, matching in zip((1, 2), doc_masks):
        masked_grad = matching * grad_conv
        grad_ext = grad_ext + jnp.pad(
            tap_values[offset] * masked_grad, ((2 - offset, offset), (0, 0))
        )
        tap_rows.append(jnp.sum(masked_grad * extended[2 - offset : 2 - offset + seq_rows], axis=0))
    rim_back = shifted(grad_ext[:2], "fsdp", -1)
    grad_bx = grad_ext[2:] + jnp.pad(rim_back, ((seq_rows - 2, 0), (0, 0)))
    grad_taps = jnp.stack(tap_rows)
    grad_proj = jnp.concatenate([grad_bx * x_part, grad_c, grad_bx * b_part], 1).astype(
        jnp.bfloat16
    )
    grad_win = contract_rows(normed_one, grad_proj)
    grad_normed_one = against_rows(grad_proj, w_in)
    grad_gone = jnp.sum(grad_normed_one * residual * scale_one, axis=0)
    weighted_one = grad_normed_one * gain_one.astype(jnp.float32)
    grad_input = (
        grad_middle
        + scale_one * weighted_one
        - residual * scale_one**3 * jnp.mean(weighted_one * residual, axis=-1, keepdims=True)
    )
    local_grads = (
        grad_win,
        grad_wout,
        grad_wgate,
        grad_wup,
        grad_down,
        grad_taps,
        grad_gone,
        grad_gtwo,
    )
    return (grad_input, local_grads)


def per_device(
    layer_in, segments, w_in, w_out, w_gate, w_up, w_down, conv_taps, gain_one, gain_two, cotangent
):
    outputs = []
    input_grads = []
    totals = None
    owned_grads = None
    for batch_index in range(layer_in.shape[0]):
        weights_now = (
            lax.all_gather(w_in, "fsdp", axis=1, tiled=True),
            lax.all_gather(w_out, "fsdp", axis=1, tiled=True),
            lax.all_gather(w_gate, "fsdp", axis=1, tiled=True),
            lax.all_gather(w_up, "fsdp", axis=1, tiled=True),
            lax.all_gather(w_down, "fsdp", axis=1, tiled=True),
            lax.all_gather(conv_taps, "fsdp", axis=1, tiled=True),
            lax.all_gather(gain_one, "fsdp", axis=0, tiled=True),
            lax.all_gather(gain_two, "fsdp", axis=0, tiled=True),
        )
        output, saved_state = forward_pass(
            layer_in[batch_index], segments[batch_index], weights_now
        )
        outputs.append(output)
        grad_input, local_grads = backward_pass(cotangent[batch_index], weights_now, saved_state)
        input_grads.append(grad_input)
        totals = local_grads if batch_index == 0 else jax.tree.map(jnp.add, totals, local_grads)
    owned_grads = tuple(
        lax.psum_scatter(
            total.astype(jnp.bfloat16), "fsdp", scatter_dimension=total.ndim - 1, tiled=True
        )
        for total in totals
    )
    summed = (
        lax.psum(owned_grads[0].astype(jnp.bfloat16), "rep").astype(jnp.float32),
        lax.psum(owned_grads[1].astype(jnp.bfloat16), "rep").astype(jnp.float32),
        lax.psum(owned_grads[2].astype(jnp.bfloat16), "rep").astype(jnp.float32),
        lax.psum(owned_grads[3].astype(jnp.bfloat16), "rep").astype(jnp.float32),
        lax.psum(owned_grads[4].astype(jnp.bfloat16), "rep").astype(jnp.float32),
        lax.psum(owned_grads[5].astype(jnp.bfloat16), "rep").astype(jnp.float32),
        lax.psum(owned_grads[6].astype(jnp.bfloat16), "rep").astype(jnp.float32),
        lax.psum(owned_grads[7].astype(jnp.bfloat16), "rep").astype(jnp.float32),
    )
    return (
        jnp.stack(outputs),
        jnp.stack(input_grads),
        summed[0],
        summed[1],
        summed[2],
        summed[3],
        summed[4],
        summed[5],
        summed[6],
        summed[7],
    )


MESH_ID = pl.DeviceIdType.MESH
BF16 = jnp.bfloat16
F32 = jnp.float32
CW, CCW = 0, 1
WIN, WO, WG, WU, WD = range(5)


def dot_nn(a, b):
    return lax.dot_general(a, b, (((1,), (0,)), ((), ())), preferred_element_type=F32)


def dot_nt(a, b):
    return lax.dot_general(a, b, (((1,), (1,)), ((), ())), preferred_element_type=F32)


def dot_tn(a, b):
    return lax.dot_general(a, b, (((0,), (0,)), ((), ())), preferred_element_type=F32)


def span(start, size, step):
    return pl.ds(pl.multiple_of(start, step), size)


def layer_kernel(
    li, cot_in, win_in, wo_in, wg_in, wu_in, wd_in, hal, gains_in, masks_in,
    o_lo, o_gi, o_d, o_g, o_u, o_i, o_o, o_s,
    win, wo, wg, wu, wd, n1, n2, cot, proj, gated, gate, up, hidden, dwd,
    slots_d, slots_g, slots_u, part, rsib, rxn, middle, gmid,
    gains, masks, taps, hbx, halo_out, halo_in, dtap, dgain, small_r, small_x,
    loc_sem, ag_s, ag_r, rs_s, rs_r, gain_s, gain_r, mask_s, mask_r, n1_s, n1_r,
    cot_s, cot_r, n2_s, n2_r, ex_s, ex_r, gb_s, gb_r, halo_s, halo_r, fin_s, fin_r, mx_s, mx_r,
    ms_s, ms_r, sm_s, sm_r, sx_s, sx_r, out_sem, sib_credit, xn_credit, oi_ready,
):
    r = lax.axis_index("rep")
    f = lax.axis_index("fsdp")
    x = lax.div(r, 2)
    c = lax.rem(r, 2)
    oc = 1 - c
    sib = 2 * x + oc
    xn = 2 * (1 - x) + c
    far = 2 * (1 - x) + oc
    y = lax.rem(f, 2)
    z = lax.div(f, 2)
    p = z + y * (7 - 2 * z)

    def f_at(place):
        place = lax.rem(place + 16, 8)
        yy = lax.div(place, 4)
        return 2 * (place + yy * (7 - 2 * place)) + yy

    right, left = f_at(p + 1), f_at(p - 1)
    toward = (right, left)

    def remote(src, dst, send, recv, device):
        return pltpu.make_async_remote_copy(
            src_ref=src, dst_ref=dst, send_sem=send, recv_sem=recv, device_id=device,
            device_id_type=MESH_ID,
        )

    def weight_slot(k, g):
        if k == WIN:
            return win.at[span(g * 192, 192, 64), :]
        if k == WO:
            return wo.at[:, span(g * 128, 128, 128)]
        if k == WG:
            return wg.at[span(g * 144, 144, 16), :]
        if k == WU:
            return wu.at[span(g * 144, 144, 16), :]
        return wd.at[:, span(g * 128, 128, 128)]

    reach = {WIN: (4, 3), WO: (3, 4), WG: (3, 4), WU: (3, 4), WD: (4, 3)}

    def ag_copy(k, s, way, g):
        return remote(
            weight_slot(k, g), weight_slot(k, g), ag_s.at[k, way, s], ag_r.at[k, way, s],
            (r, toward[way]),
        )

    def ag_send(k, s, way):
        ag_copy(k, s, way, f_at(p - s) if way == CW else f_at(p + s)).start()

    def ag_start(k):
        ag_send(k, 0, CW)
        ag_send(k, 0, CCW)

    def ag_event(k, s):
        for way in (CW, CCW):
            if s < reach[k][way]:
                g = f_at(p - 1 - s) if way == CW else f_at(p + 1 + s)
                ag_copy(k, s, way, g).wait_recv()
                if s + 1 < reach[k][way]:
                    ag_send(k, s + 1, way)

    def ag_drain(k):
        for way in (CW, CCW):
            for s in range(reach[k][way]):
                ag_copy(k, s, way, f).wait_send()

    def grad_piece(k, g, way):
        if k == WD:
            return dwd.at[pl.ds(576 * way, 576), span(g * 128, 128, 128)]
        if k == WG:
            return hidden.at[span(g * 144, 144, 16), pl.ds(512 * way, 512)]
        if k == WU:
            return hidden.at[span(g * 144, 144, 16), pl.ds(1024 + 512 * way, 512)]
        if k == WO:
            return gate.at[pl.ds(512 + 256 * way, 256), span(1024 + g * 128, 128, 128)]
        return gate.at[
            span(192 * lax.rem(g, 6), 192, 64), span(1024 * lax.div(g, 6) + 512 * way, 512, 128)
        ]

    def sum_slot(k, way, s):
        if k == WD:
            return slots_d.at[way, s]
        if k == WG:
            return slots_g.at[way, s]
        if k == WU:
            return slots_u.at[way, s]
        i = way * 7 + s
        if k == WO:
            return up.at[pl.ds(768, 256), pl.ds(128 * i, 128)]
        return up.at[pl.ds(192 * (i // 4), 192), pl.ds(512 * (i % 4), 512)]

    def rs_copy(k, way, s):
        src = sum_slot(k, way, s - 1) if s else grad_piece(
            k, f_at(p - 1) if way == CW else f_at(p + 1), way
        )
        return remote(
            src, sum_slot(k, way, s), rs_s.at[k, way, s], rs_r.at[k, way, s], (r, toward[way])
        )

    def rs_start(k):
        rs_copy(k, CW, 0).start()
        rs_copy(k, CCW, 0).start()

    def rs_event(k, s):
        for way in (CW, CCW):
            g = f_at(p - 2 - s) if way == CW else f_at(p + 2 + s)
            rs_copy(k, way, s).wait_recv()
            slot = sum_slot(k, way, s)
            slot[...] = (slot[...].astype(F32) + grad_piece(k, g, way)[...].astype(F32)).astype(BF16)
            if s < 6:
                rs_copy(k, way, s + 1).start()

    def rs_drain(k):
        for way in (CW, CCW):
            for s in range(7):
                rs_copy(k, way, s).wait_send()

    ffn_out = {WD: (0, o_d), WG: (1, o_g), WU: (2, o_u)}
    peers = (sib, xn, far)

    def final_view(k, owner, way):
        out = ffn_out[k][1]
        if k == WD:
            return out.at[owner, pl.ds(576 * way, 576), :]
        return out.at[owner, :, pl.ds(512 * way, 512)]

    def final_copy(k, way, j):
        i = ffn_out[k][0]
        src = sum_slot(k, way, 6)
        if j == 3:
            return pltpu.make_async_copy(src, final_view(k, r, way), fin_s.at[i, way, 3])
        return remote(
            src, final_view(k, r, way), fin_s.at[i, way, j], fin_r.at[i, way, j], (peers[j], f)
        )

    def final_start(k):
        for way in (CW, CCW):
            for j in range(4):
                final_copy(k, way, j).start()

    def final_drain(k):
        i = ffn_out[k][0]
        for way in (CW, CCW):
            final_copy(k, way, 3).wait()
            for j in range(3):
                final_copy(k, way, j).wait_send()
                view = final_view(k, peers[j], way)
                remote(view, view, fin_s.at[i, way, j], fin_r.at[i, way, j], (r, left)).wait_recv()

    loads = [
        pltpu.make_async_copy(win_in, weight_slot(WIN, f), loc_sem.at[0]),
        pltpu.make_async_copy(wo_in, weight_slot(WO, f), loc_sem.at[1]),
        pltpu.make_async_copy(li, part.at[0], loc_sem.at[2]),
        pltpu.make_async_copy(cot_in, cot.at[span(r * 512, 512, 512), :], loc_sem.at[3]),
        pltpu.make_async_copy(wg_in, weight_slot(WG, f), loc_sem.at[4]),
        pltpu.make_async_copy(wu_in, weight_slot(WU, f), loc_sem.at[5]),
        pltpu.make_async_copy(wd_in, weight_slot(WD, f), loc_sem.at[6]),
        pltpu.make_async_copy(gains_in, gains.at[:, span(f * 128, 128, 128)], loc_sem.at[7]),
        pltpu.make_async_copy(masks_in, masks.at[c], loc_sem.at[8]),
    ]
    for load in loads:
        load.start()
    barrier = pltpu.get_barrier_semaphore()
    for j in range(1, 8):
        pl.semaphore_signal(
            barrier, inc=1, device_id=(r, lax.rem(f + j, 8)), device_id_type=MESH_ID
        )
    for peer in peers:
        pl.semaphore_signal(barrier, inc=1, device_id=(peer, f), device_id_type=MESH_ID)
    dtap[...] = jnp.zeros_like(dtap)
    dgain[...] = jnp.zeros_like(dgain)
    pl.semaphore_wait(barrier, 10)

    def gain_copy(j):
        return remote(
            gains_in, gains.at[:, span(f * 128, 128, 128)], gain_s.at[j - 1], gain_r.at[j - 1],
            (r, lax.rem(f + j, 8)),
        )

    def cot_copy(m, j):
        rows = span((xn if j == 2 else r) * 512 + m * 256, 256, 256)
        return remote(
            cot.at[rows, :], cot.at[rows, :], cot_s.at[m, j], cot_r.at[m, j],
            (xn if j == 1 else sib, f),
        )

    def cot_arrive(m, j):
        rows = span((sib, xn, far)[j] * 512 + m * 256, 256, 256)
        remote(
            cot.at[rows, :], cot.at[rows, :], cot_s.at[m, j], cot_r.at[m, j], (sib, f)
        ).wait_recv()

    def n2_copy(m, j):
        rows = span((xn if j == 2 else r) * 512 + m * 256, 256, 256)
        return remote(
            n2.at[rows, :], n2.at[rows, :], n2_s.at[m, j], n2_r.at[m, j],
            (xn if j == 1 else sib, f),
        )

    def n2_arrive(m, j):
        rows = span((sib, xn, far)[j] * 512 + m * 256, 256, 256)
        remote(
            n2.at[rows, :], n2.at[rows, :], n2_s.at[m, j], n2_r.at[m, j], (sib, f)
        ).wait_recv()

    for j in range(1, 8):
        gain_copy(j).start()
    loads[0].wait()
    loads[1].wait()
    ag_start(WIN)
    ag_start(WO)
    loads[8].wait()
    mask_copy = remote(masks.at[c], masks.at[c], mask_s, mask_r, (sib, f))
    mask_copy.start()
    loads[3].wait()
    for m in (0, 1):
        cot_copy(m, 0).start()
        cot_copy(m, 1).start()
    loads[2].wait()
    loads[7].wait()
    for j in range(1, 8):
        gain_copy(j).wait_recv()

    gain_one = gains[0:1, :]
    gain_two = gains[1:2, :]

    def norm_rows(rows):
        rows = rows.astype(F32)
        scale = lax.rsqrt(jnp.mean(rows * rows, axis=1, keepdims=True) + epsilon)
        return (rows * scale * gain_one).astype(BF16)

    def norm_step(i, carry):
        rows = span(i * 64, 64, 64)
        n1[c, rows, :] = norm_rows(part[0, rows, :])
        return carry

    lax.fori_loop(0, 8, norm_step, 0)
    n1[c, 512:544, :] = norm_rows(hal[...])
    n1_copy = remote(n1.at[c], n1.at[c], n1_s, n1_r, (sib, f))
    n1_copy.start()

    ag_event(WIN, 0)
    ag_event(WO, 0)
    ag_event(WIN, 1)
    ag_event(WO, 1)
    for load in loads[4:7]:
        load.wait()
    ag_start(WG)
    ag_event(WIN, 2)
    ag_event(WO, 2)
    for m in (0, 1):
        cot_arrive(m, 1)
        cot_copy(m, 2).start()
    ag_event(WIN, 3)
    ag_event(WO, 3)

    for g in range(8):
        taps[64 * g : 64 * g + 64, :] = wo[512:576, 128 * g : 128 * g + 128]
    remote(n1.at[oc], n1.at[oc], n1_s, n1_r, (sib, f)).wait_recv()
    remote(masks.at[oc], masks.at[oc], mask_s, mask_r, (sib, f)).wait_recv()
    lane256 = lax.broadcasted_iota(jnp.int32, (64, 256), 1)

    def halo_product(qc):
        rows = n1[qc, 512:544, :]
        return dot_nt(win[0:512, :], rows) * dot_nt(win[1024:1536, :], rows)

    hbx[:, 0:32] = halo_product(0)
    hbx[:, 32:64] = halo_product(1)

    def earlier(bx, qc, rows, m):
        held = hbx[rows, 0:64]
        place = 32 * qc + 16 * m
        spot = lax.broadcasted_iota(jnp.int32, (64, 64), 1) - place
        one = jnp.sum(jnp.where(spot == 15, held, 0.0), axis=1, keepdims=True)
        two = jnp.sum(jnp.where(spot == 14, held, 0.0), axis=1, keepdims=True)
        prev_one = jnp.where(lane256 == 0, one, pltpu.roll(bx, 1, 1))
        prev_two = jnp.where(
            lane256 == 0, two, jnp.where(lane256 == 1, one, pltpu.roll(bx, 2, 1))
        )
        return prev_one, prev_two

    def tap_columns(rows):
        held = taps[rows, :].astype(F32)
        return held[:, 0:1], held[:, 1:2], held[:, 2:3]

    def mix_fwd(qc, m):
        tokens = n1[qc, 256 * m : 256 * m + 256, :]
        lanes = span(qc * 512 + m * 256, 256, 256)
        mask_one = masks[qc, 2 * m : 2 * m + 1, :]
        mask_two = masks[qc, 2 * m + 1 : 2 * m + 2, :]
        for i in range(3):
            gmid[:, 256 * i : 256 * i + 256] = dot_nt(win[512 * i : 512 * i + 512, :], tokens)

        def step(i, carry):
            rows = span(64 * i, 64, 64)
            b, cc, xx = gmid[rows, 0:256], gmid[rows, 256:512], gmid[rows, 512:768]
            proj[rows, lanes] = b.astype(BF16)
            proj[span(512 + 64 * i, 64, 64), lanes] = cc.astype(BF16)
            proj[span(1024 + 64 * i, 64, 64), lanes] = xx.astype(BF16)
            bx = b * xx
            prev_one, prev_two = earlier(bx, qc, rows, m)
            t0, t1, t2 = tap_columns(rows)
            conv = (
                t0 * bx + t1 * (mask_one * prev_one) + t2 * (mask_two * prev_two)
            )
            gated[rows, lanes] = (cc * conv).astype(BF16)
            return carry

        lax.fori_loop(0, 8, step, 0)
        return dot_tn(gated[:, lanes], wo[0:512, :])

    def ex_copy(op, kind, m):
        rows = span(256 * m, 256, 256)
        src = part.at[{0: 1, 1: 0, 2: 2}[kind], rows, :]
        dst = rxn.at[rows, :] if kind == 2 else rsib.at[kind, rows, :]
        return remote(
            src, dst, ex_s.at[op, kind, m], ex_r.at[op, kind, m], (xn if kind == 2 else sib, f)
        )

    for m in (0, 1):
        part[1, 256 * m : 256 * m + 256, :] = mix_fwd(oc, m).astype(BF16)
        ex_copy(0, 0, m).start()
        ag_event(WG, m)
        if m == 1:
            ag_start(WU)
    for m in (0, 1):
        middle[256 * m : 256 * m + 256, :] = mix_fwd(c, m)
        if m == 0:
            ag_event(WG, 2)
    for m in (0, 1):
        ex_copy(0, 0, m).wait_recv()

        def norm_two_step(i, carry):
            rows = span(256 * m + i * 64, 64, 64)
            mid = middle[rows, :] + rsib[0, rows, :].astype(F32) + part[0, rows, :].astype(F32)
            middle[rows, :] = mid
            scale = lax.rsqrt(jnp.mean(mid * mid, axis=1, keepdims=True) + epsilon)
            n2[span(r * 512 + 256 * m + i * 64, 64, 64), :] = (mid * scale * gain_two).astype(BF16)
            return carry

        lax.fori_loop(0, 4, norm_two_step, 0)
        n2_copy(m, 1).start()
        n2_copy(m, 0).start()
    pl.semaphore_signal(sib_credit, inc=1, device_id=(sib, f), device_id_type=MESH_ID)
    for m in (0, 1):
        ex_copy(0, 0, m).wait_send()
    ag_event(WG, 3)
    ag_event(WU, 0)
    ag_event(WU, 1)
    ag_start(WD)
    for m in (0, 1):
        n2_arrive(m, 1)
        n2_copy(m, 2).start()
    ag_event(WU, 2)
    ag_event(WU, 3)

    def gate_up(q):
        def step(i, carry):
            rows = span(lax.rem(i, 3) * 384, 384, 128)
            tokens = span(q * 512 + lax.div(i, 3) * 256, 256, 256)
            g = dot_nt(wg[rows, :], n2[tokens, :])
            u = dot_nt(wu[rows, :], n2[tokens, :])
            gate[rows, tokens] = g.astype(BF16)
            up[rows, tokens] = u.astype(BF16)
            hidden[rows, tokens] = (g * jax.nn.sigmoid(g) * u).astype(BF16)
            return carry

        lax.fori_loop(0, 6, step, 0)

    gate_up(r)
    ag_event(WD, 0)
    for m in (0, 1):
        n2_arrive(m, 0)
    gate_up(sib)
    ag_event(WD, 1)
    gate_up(xn)
    for m in (0, 1):
        n2_arrive(m, 2)
    gate_up(far)
    ag_event(WD, 2)
    for m in (0, 1):
        cot_arrive(m, 0)
        cot_arrive(m, 2)

    def dwd_step(i, carry):
        rows = span(i * 384, 384, 128)
        for n in (0, 512):
            dwd[rows, n : 512 + n] = dot_nn(hidden[rows, :], cot[:, n : n + 512]).astype(BF16)
        return carry

    lax.fori_loop(0, 3, dwd_step, 0)
    rs_start(WD)
    ag_event(WD, 3)

    pending = []

    def tick(count=1):
        for _ in range(count):
            if pending:
                k, s = pending.pop(0)
                rs_event(k, s)
                if s == 6 and k in ffn_out:
                    final_start(k)

    def four_way(op, partial, ticks):
        pl.semaphore_wait(sib_credit, 1)
        if op == 2:
            pl.semaphore_wait(xn_credit, 1)

        def to_part(slot, q, kind):
            def step(m, carry):
                part[slot, span(256 * m, 256, 256), :] = partial(q, m).astype(BF16)
                if kind is not None:
                    ex_copy(op, kind, m).start()
                return carry

            lax.fori_loop(0, 2, step, 0)

        to_part(0, far, 1)
        to_part(2, xn, None)
        tick(ticks[0])
        for m in (0, 1):
            ex_copy(op, 1, m).wait_recv()

            def add_step(i, carry):
                rows = span(256 * m + i * 64, 64, 64)
                part[2, rows, :] = (
                    part[2, rows, :].astype(F32) + rsib[1, rows, :].astype(F32)
                ).astype(BF16)
                return carry

            lax.fori_loop(0, 4, add_step, 0)
            ex_copy(op, 2, m).start()
        to_part(1, sib, 0)
        tick(ticks[1])

        def own_step(m, carry):
            gmid[span(256 * m, 256, 256), :] = partial(r, m)
            return carry

        lax.fori_loop(0, 2, own_step, 0)

    def four_way_sent(op):
        for m in (0, 1):
            for kind in range(3):
                ex_copy(op, kind, m).wait_send()

    def down_part(q, m):
        return dot_tn(hidden[:, span(q * 512 + m * 256, 256, 256)], wd[...])

    for m in (0, 1):
        for j in range(3):
            cot_copy(m, j).wait_send()
            n2_copy(m, j).wait_send()
    pending += [(WD, s) for s in range(7)]
    four_way(1, down_part, (1, 1))

    def grad_hidden(q):
        def step(i, carry):
            rows = span(lax.rem(i, 3) * 384, 384, 128)
            tokens = span(q * 512 + lax.div(i, 3) * 256, 256, 256)
            gh = dot_nt(wd[rows, :], cot[tokens, :])
            g = gate[rows, tokens].astype(F32)
            u = up[rows, tokens].astype(F32)
            s = jax.nn.sigmoid(g)
            gate[rows, tokens] = (gh * u * s * (1.0 + g * (1.0 - s))).astype(BF16)
            up[rows, tokens] = (gh * g * s).astype(BF16)
            return carry

        lax.fori_loop(0, 6, step, 0)

    for i, q in enumerate((r, sib, xn, far)):
        grad_hidden(q)
        if i % 2:
            tick()

    def dwg_step(i, carry):
        rows = span(i * 384, 384, 128)
        for n in (0, 512):
            hidden[rows, n : 512 + n] = dot_nn(gate[rows, :], n2[:, n : n + 512]).astype(BF16)
        return carry

    def dwu_step(i, carry):
        rows = span(i * 384, 384, 128)
        for n in (0, 512):
            hidden[rows, 1024 + n : 1536 + n] = dot_nn(up[rows, :], n2[:, n : n + 512]).astype(BF16)
        return carry

    lax.fori_loop(0, 3, dwg_step, 0)
    rs_start(WG)
    tick()
    lax.fori_loop(0, 3, dwu_step, 0)
    rs_start(WU)
    pending[:] = [(WD, s) for s in range(5, 7)] + pending[2:]
    pending[:] = [(WD, 5), (WG, 0), (WD, 6), (WG, 1), (WU, 0)] + [
        e for s in range(2, 7) for e in ((WG, s), (WU, s - 1))
    ] + [(WU, 6)]
    tick(2)

    for m in (0, 1):
        ex_copy(1, 0, m).wait_recv()
        ex_copy(1, 2, m).wait_recv()

    def out_step(i, carry):
        rows = span(i * 64, 64, 64)
        gmid[rows, :] = (
            gmid[rows, :] + middle[rows, :] + rsib[0, rows, :].astype(F32) + rxn[rows, :].astype(F32)
        )
        return carry

    lax.fori_loop(0, 8, out_step, 0)
    four_way_sent(1)
    lo_copy = pltpu.make_async_copy(gmid, o_lo, out_sem.at[0])
    lo_copy.start()
    pl.semaphore_signal(sib_credit, inc=1, device_id=(sib, f), device_id_type=MESH_ID)
    pl.semaphore_signal(xn_credit, inc=1, device_id=(xn, f), device_id_type=MESH_ID)
    lo_copy.wait()

    def gn2_part(q, m):
        tokens = span(q * 512 + m * 256, 256, 256)
        return dot_tn(gate[:, tokens], wg[...]) + dot_tn(up[:, tokens], wu[...])

    four_way(2, gn2_part, (1, 2))
    pl.semaphore_signal(oi_ready, inc=1, device_id=(r, right), device_id_type=MESH_ID)
    pl.semaphore_signal(oi_ready, inc=1, device_id=(r, left), device_id_type=MESH_ID)
    tick(2)
    gb_copies = []
    for m in (0, 1):
        ex_copy(2, 0, m).wait_recv()
        ex_copy(2, 2, m).wait_recv()

        def grad_middle_step(i, carry):
            rows = span(256 * m + i * 64, 64, 64)
            gn = gmid[rows, :] + rsib[0, rows, :].astype(F32) + rxn[rows, :].astype(F32)
            mid = middle[rows, :]
            scale = lax.rsqrt(jnp.mean(mid * mid, axis=1, keepdims=True) + epsilon)
            dgain[1:2, :] += jnp.sum(gn * (mid * scale), axis=0, keepdims=True)
            weighted = gn * gain_two
            inner = jnp.mean(weighted * mid, axis=1, keepdims=True)
            gm = (
                cot[span(r * 512 + 256 * m + i * 64, 64, 64), :].astype(F32)
                + scale * weighted
                - mid * (scale * scale * scale * inner)
            )
            gmid[rows, :] = gm
            n2[span(c * 512 + 256 * m + i * 64, 64, 64), :] = gm.astype(BF16)
            return carry

        lax.fori_loop(0, 4, grad_middle_step, 0)
        rows = span(c * 512 + 256 * m, 256, 256)
        copy = remote(n2.at[rows, :], n2.at[rows, :], gb_s.at[m], gb_r.at[m], (sib, f))
        copy.start()
        gb_copies.append(copy)
    pl.semaphore_signal(sib_credit, inc=1, device_id=(sib, f), device_id_type=MESH_ID)
    four_way_sent(2)
    tick(2)
    for m in (0, 1):
        rows = span(oc * 512 + 256 * m, 256, 256)
        remote(n2.at[rows, :], n2.at[rows, :], gb_s.at[m], gb_r.at[m], (sib, f)).wait_recv()

    lane128 = lax.broadcasted_iota(jnp.int32, (512, 128), 1)
    rim = jnp.zeros((512, 128), F32)
    taps_one, taps_two = tap_columns(slice(None))[1:]
    for qc in (0, 1):
        for m in (0, 1):
            at = qc * 512 + m * 256
            gg = dot_nt(wo[0:512, :], n2[at : at + 16, :])
            gc = gg * proj[512:1024, at : at + 128].astype(F32)[:, 0:16]
            masked_one = masks[qc, 2 * m : 2 * m + 1, 0:16] * gc
            masked_two = masks[qc, 2 * m + 1 : 2 * m + 2, 0:16] * gc
            first = taps_two * masked_two[:, 0:1]
            second = taps_one * masked_one[:, 0:1] + taps_two * masked_two[:, 1:2]
            b = 2 * (2 * qc + m)
            rim = jnp.where(lane128 == b, first, jnp.where(lane128 == b + 1, second, rim))
    halo_out[...] = rim.astype(BF16)
    halo_copy = remote(halo_out, halo_in, halo_s, halo_r, (r, lax.rem(f + 7, 8)))
    halo_copy.start()

    for n in (0, 512):
        gate[512:1024, 1024 + n : 1536 + n] = dot_nn(gated[...], n2[0:1024, n : n + 512]).astype(BF16)
    pl.semaphore_wait(oi_ready, 2)
    rs_start(WO)
    tick()
    halo_copy.wait_recv()
    inside = jnp.where(f < 7, 1.0, 0.0).astype(F32)
    lane_tap = lax.broadcasted_iota(jnp.int32, (64, 128), 1)

    def mix_bwd(qc, m):
        lanes = pl.ds(qc * 512 + m * 256, 256)
        tokens = n2[qc * 512 + m * 256 : qc * 512 + m * 256 + 256, :]
        mask_one = masks[qc, 2 * m : 2 * m + 1, :]
        mask_two = masks[qc, 2 * m + 1 : 2 * m + 2, :]
        b2 = 2 * (2 * qc + m)
        middle[:, 0:256] = dot_nt(wo[0:512, :], tokens)

        def step(i, carry):
            rows = span(64 * i, 64, 64)
            c_rows, x_rows = span(512 + 64 * i, 64, 64), span(1024 + 64 * i, 64, 64)
            gg = middle[rows, 0:256]
            b = proj[rows, lanes].astype(F32)
            cc = proj[c_rows, lanes].astype(F32)
            xx = proj[x_rows, lanes].astype(F32)
            bx = b * xx
            prev_one, prev_two = earlier(bx, qc, rows, m)
            prev_one = mask_one * prev_one
            prev_two = mask_two * prev_two
            t0, t1, t2 = tap_columns(rows)
            conv = t0 * bx + t1 * prev_one + t2 * prev_two
            gc = gg * cc
            sum0 = jnp.sum(gc * bx, axis=1, keepdims=True)
            sum1 = jnp.sum(gc * prev_one, axis=1, keepdims=True)
            sum2 = jnp.sum(gc * prev_two, axis=1, keepdims=True)
            dtap[rows, :] += jnp.where(
                lane_tap == 0, sum0, jnp.where(lane_tap == 1, sum1, jnp.where(lane_tap == 2, sum2, 0.0))
            )
            back_one = jnp.where(lane256 < 255, pltpu.roll(mask_one * gc, 255, 1), 0.0)
            back_two = jnp.where(lane256 < 254, pltpu.roll(mask_two * gc, 254, 1), 0.0)
            edge = halo_in[rows, :].astype(F32) * inside
            back = jnp.where(
                lane256 == 254, edge[:, b2 : b2 + 1],
                jnp.where(lane256 == 255, edge[:, b2 + 1 : b2 + 2], 0.0),
            )
            gbx = t0 * gc + t1 * back_one + t2 * back_two + back
            proj[rows, lanes] = (gbx * xx).astype(BF16)
            proj[c_rows, lanes] = (gg * conv).astype(BF16)
            proj[x_rows, lanes] = (gbx * b).astype(BF16)
            return carry

        lax.fori_loop(0, 8, step, 0)

    for qc in (0, 1):
        for m in (0, 1):
            mix_bwd(qc, m)
            if m:
                tick()

    def dwin(t, n):
        rows = span(384 * t, 384, 128)
        return (
            dot_nn(proj[rows, 0:512], n1[0, 0:512, n : n + 512])
            + dot_nn(proj[rows, 512:1024], n1[1, 0:512, n : n + 512])
        ).astype(BF16)

    def dwin_step(t, carry):
        for n in (0, 512):
            gate[span(384 * t, 384, 128), n : n + 512] = dwin(t, n)
        return carry

    lax.fori_loop(0, 3, dwin_step, 0)
    for n in (0, 512):
        gate[0:384, 1024 + n : 1536 + n] = dwin(3, n)
    rs_start(WIN)
    pending += [e for s in range(7) for e in ((WO, s), (WIN, s))]
    tick(2)

    def gn1_part(qc, m):
        return dot_tn(proj[:, span(qc * 512 + m * 256, 256, 256)], win[...])

    pl.semaphore_wait(sib_credit, 1)
    li_again = pltpu.make_async_copy(li, part.at[0], loc_sem.at[2])
    li_again.start()
    for m in (0, 1):
        part[1, 256 * m : 256 * m + 256, :] = gn1_part(oc, m).astype(BF16)
        ex_copy(3, 0, m).start()
    tick(2)
    for m in (0, 1):
        middle[256 * m : 256 * m + 256, :] = gn1_part(c, m)
    tick(2)
    li_again.wait()
    for m in (0, 1):
        ex_copy(3, 0, m).wait_recv()

        def grad_in_step(i, carry):
            rows = span(256 * m + i * 64, 64, 64)
            gn = middle[rows, :] + rsib[0, rows, :].astype(F32)
            res = part[0, rows, :].astype(F32)
            scale = lax.rsqrt(jnp.mean(res * res, axis=1, keepdims=True) + epsilon)
            dgain[0:1, :] += jnp.sum(gn * (res * scale), axis=0, keepdims=True)
            weighted = gn * gain_one
            inner = jnp.mean(weighted * res, axis=1, keepdims=True)
            middle[rows, :] = gmid[rows, :] + scale * weighted - res * (scale * scale * scale * inner)
            return carry

        lax.fori_loop(0, 4, grad_in_step, 0)
    gi_copy = pltpu.make_async_copy(middle, o_gi, out_sem.at[1])
    gi_copy.start()
    for m in (0, 1):
        ex_copy(3, 0, m).wait_send()

    for g in range(8):
        gmid[0:64, 128 * g : 128 * g + 128] = dtap[64 * g : 64 * g + 64, :]
        gmid[64:72, 128 * g : 128 * g + 128] = dgain[:, 128 * g : 128 * g + 128]

    def small_p(g):
        return gmid.at[pl.ds(0, 72), span(g * 128, 128, 128)]

    def small_copy(j):
        g = lax.rem(f + j, 8)
        return remote(small_p(g), small_r.at[j], sm_s.at[j - 1], sm_r.at[j - 1], (r, g))

    for j in range(1, 8):
        small_copy(j).start()
    tick(2)
    total = small_p(f)[...]
    for j in range(1, 8):
        small_copy(j).wait_recv()
        total = total + small_r[j]
    small_x[0] = total
    sx_copy = remote(small_x.at[0], small_x.at[1], sx_s.at[0], sx_r.at[0], (xn, f))
    sx_copy.start()
    tick(2)
    sx_copy.wait_recv()
    small_x[2] = small_x[0] + small_x[1]
    ss_copy = remote(small_x.at[2], o_s.at[c], sx_s.at[1], sx_r.at[1], (sib, f))
    ss_copy.start()
    so_copy = pltpu.make_async_copy(small_x.at[2], o_s.at[c], out_sem.at[2])
    so_copy.start()
    tick(len(pending))

    def mix_sum(k, way):
        if k == WIN:
            return cot.at[pl.ds(0, 192), pl.ds(512 * way, 512)]
        return cot.at[pl.ds(192 + 256 * way, 256), pl.ds(0, 128)]

    def mx_copy(k, way):
        i = 0 if k == WIN else 1
        return remote(
            sum_slot(k, way, 6), mix_sum(k, way), mx_s.at[i, way], mx_r.at[i, way], (xn, f)
        )

    def mix_view(k, owner, way):
        if k == WIN:
            return o_i.at[owner, :, pl.ds(512 * way, 512)]
        return o_o.at[owner, pl.ds(256 * way, 256), :]

    def mix_copies(k, way):
        i = 0 if k == WIN else 1
        dst = mix_sum(k, way)
        return (
            remote(dst, mix_view(k, c, way), ms_s.at[i, way], ms_r.at[i, way], (sib, f)),
            pltpu.make_async_copy(dst, mix_view(k, c, way), out_sem.at[3 + 2 * i + way]),
        )

    for k in (WO, WIN):
        for way in (CW, CCW):
            mx_copy(k, way).start()
    for k in (WO, WIN):
        for way in (CW, CCW):
            mx_copy(k, way).wait_recv()
            dst = mix_sum(k, way)
            dst[...] = (dst[...].astype(F32) + sum_slot(k, way, 6)[...].astype(F32)).astype(BF16)
            for out in mix_copies(k, way):
                out.start()

    for k in range(5):
        ag_drain(k)
        rs_drain(k)
    for k in (WD, WG, WU):
        final_drain(k)
    for j in range(1, 8):
        gain_copy(j).wait_send()
        small_copy(j).wait_send()
    mask_copy.wait_send()
    n1_copy.wait_send()
    for m in (0, 1):
        gb_copies[m].wait_send()
    halo_copy.wait_send()
    lo_gi = (gi_copy, so_copy)
    for copy in lo_gi:
        copy.wait()
    sx_copy.wait_send()
    ss_copy.wait_send()
    other = o_s.at[oc]
    remote(other, other, sx_s.at[1], sx_r.at[1], (sib, f)).wait_recv()
    for k in (WO, WIN):
        i = 0 if k == WIN else 1
        for way in (CW, CCW):
            mx_copy(k, way).wait_send()
            out, local = mix_copies(k, way)
            out.wait_send()
            local.wait()
            view = mix_view(k, oc, way)
            remote(view, view, ms_s.at[i, way], ms_r.at[i, way], (sib, f)).wait_recv()


def grouped_device(
    layer_in, segments, w_in, w_out, w_gate, w_up, w_down, conv_taps, gain_one, gain_two, cotangent
):
    r = lax.axis_index("rep")
    c = lax.rem(r, 2)
    width = layer_in.shape[2]

    def pick(array, axis, index):
        return lax.dynamic_index_in_dim(array, index, axis, keepdims=False)

    packed = jnp.concatenate(
        [
            layer_in[:, 254:256, :],
            jnp.broadcast_to(segments[:, 254:256, None].astype(BF16), (2, 2, 128)),
        ],
        2,
    )
    rim = shifted(packed, "fsdp", 1)
    halo = jnp.pad(rim[:, :, :width], ((0, 0), (14, 0), (0, 0))).reshape(32, width)
    ids = jnp.concatenate([rim[:, :, width].astype(jnp.int32), segments], 1)
    masks = jnp.stack([ids[:, 1:257] == segments, ids[:, 0:256] == segments], 1)
    masks = jnp.pad(masks.reshape(4, 256).astype(F32), ((0, 4), (0, 0)))
    own_in = pick(w_in.reshape(width, 3, 2, 64), 2, c).reshape(width, 192).T
    own_out = pick(w_out.reshape(8, 2, 64, 128), 1, c).reshape(512, 128)
    tap_half = pick(conv_taps.reshape(3, 2, 64), 1, c)
    tap_cols = jnp.pad(tap_half.T, ((0, 0), (0, 125)))
    own_out = jnp.concatenate([own_out, tap_cols], 0)
    own_gate = pick(w_gate.reshape(width, 4, 144), 1, r).T
    own_up = pick(w_up.reshape(width, 4, 144), 1, r).T
    own_down = pick(w_down.reshape(8, 4, 144, 128), 1, r).reshape(1152, 128)
    gains = jnp.pad(jnp.stack([gain_one, gain_two]).astype(F32), ((0, 6), (0, 0)))

    hbm = pl.BlockSpec(memory_space=pl.ANY)
    vmem = pl.BlockSpec(memory_space=pltpu.VMEM)
    dma = pltpu.SemaphoreType.DMA
    regular = pltpu.SemaphoreType.REGULAR

    def big(*shape, dtype=BF16):
        return pltpu.VMEM(shape, dtype)

    outs = pl.pallas_call(
        layer_kernel,
        out_shape=(
            jax.ShapeDtypeStruct((512, 1024), F32),
            jax.ShapeDtypeStruct((512, 1024), F32),
            jax.ShapeDtypeStruct((4, 1152, 128), BF16),
            jax.ShapeDtypeStruct((4, 144, 1024), BF16),
            jax.ShapeDtypeStruct((4, 144, 1024), BF16),
            jax.ShapeDtypeStruct((2, 192, 1024), BF16),
            jax.ShapeDtypeStruct((2, 512, 128), BF16),
            jax.ShapeDtypeStruct((2, 72, 128), F32),
        ),
        in_specs=[hbm] * 7 + [vmem, hbm, hbm],
        out_specs=[hbm] * 8,
        scratch_shapes=[
            big(1536, 1024), big(576, 1024), big(1152, 1024), big(1152, 1024), big(1152, 1024),
            big(2, 544, 1024), big(2048, 1024), big(2048, 1024), big(1536, 1024), big(512, 1024),
            big(1152, 2048), big(1152, 2048), big(1152, 2048), big(1152, 1024),
            big(2, 7, 576, 128), big(2, 7, 144, 512), big(2, 7, 144, 512),
            big(3, 512, 1024), big(2, 512, 1024), big(512, 1024),
            big(512, 1024, dtype=F32), big(512, 1024, dtype=F32),
            big(8, 1024, dtype=F32), big(2, 8, 256, dtype=F32), big(512, 128),
            big(512, 128, dtype=F32), big(512, 128), big(512, 128),
            big(512, 128, dtype=F32), big(8, 1024, dtype=F32),
            big(8, 72, 128, dtype=F32), big(3, 72, 128, dtype=F32),
            dma((9,)), dma((5, 2, 4)), dma((5, 2, 4)), dma((5, 2, 7)), dma((5, 2, 7)),
            dma((7,)), dma((7,)), dma, dma, dma, dma,
            dma((2, 3)), dma((2, 3)), dma((2, 3)), dma((2, 3)),
            dma((4, 3, 2)), dma((4, 3, 2)), dma((2,)), dma((2,)), dma, dma,
            dma((3, 2, 4)), dma((3, 2, 3)), dma((2, 2)), dma((2, 2)),
            dma((2, 2)), dma((2, 2)), dma((7,)), dma((7,)), dma((2,)), dma((2,)), dma((7,)),
            regular, regular, regular,
        ],
        compiler_params=pltpu.CompilerParams(
            collective_id=0, has_side_effects=True, vmem_limit_bytes=VMEM_BYTES
        ),
        name="layer",
    )(
        layer_in.reshape(512, width), cotangent.reshape(512, width),
        own_in, own_out, own_gate, own_up, own_down, halo, gains, masks,
    )
    lo, gi, od, og, ou, oi, oo, small = outs
    back = lambda a: a.astype(F32)
    grad_in = back(oi).reshape(2, 3, 64, width).transpose(3, 1, 0, 2).reshape(width, 384)
    grad_out = back(oo).reshape(2, 8, 64, 128).transpose(1, 0, 2, 3).reshape(width, 128)
    grad_gate = back(og).reshape(576, width).T
    grad_up = back(ou).reshape(576, width).T
    grad_down = back(od).reshape(4, 8, 144, 128).transpose(1, 0, 2, 3).reshape(4608, 128)
    grad_taps = small[:, 0:64, 0:3].reshape(128, 3).T
    return (
        lo.reshape(2, 256, width), gi.reshape(2, 256, width),
        grad_in, grad_out, grad_gate, grad_up, grad_down, grad_taps,
        small[0, 64] + small[1, 64], small[0, 65] + small[1, 65],
    )


def solution(mesh):
    grouped = mesh.shape["rep"] == 4 and mesh.shape["fsdp"] == 8
    return jax.shard_map(
        grouped_device if grouped else per_device,
        mesh=mesh,
        in_specs=(
            P(None, ("rep", "fsdp"), None),
            P(None, ("rep", "fsdp")),
            P(None, "fsdp"),
            P(None, "fsdp"),
            P(None, "fsdp"),
            P(None, "fsdp"),
            P(None, "fsdp"),
            P(None, "fsdp"),
            P("fsdp"),
            P("fsdp"),
            P(None, ("rep", "fsdp"), None),
        ),
        out_specs=(
            P(None, ("rep", "fsdp"), None),
            P(None, ("rep", "fsdp"), None),
            P(None, "fsdp"),
            P(None, "fsdp"),
            P(None, "fsdp"),
            P(None, "fsdp"),
            P(None, "fsdp"),
            P(None, "fsdp"),
            P("fsdp"),
            P("fsdp"),
        ),
        check_vma=False,
    )
```

```python
import jax
import jax.numpy as jnp
from jax import lax
from jax.experimental import pallas as pl
from jax.experimental.pallas import tpu as pltpu
from jax.sharding import PartitionSpec as P

epsilon = 1e-05
VMEM_BYTES = 65000 << 10


def shifted(block, axis, distance):
    devices = range(lax.axis_size(axis))
    route = [(i - distance, i) for i in devices if i - distance in devices]
    return lax.ppermute(block, axis, route)


def rms_scale(values):
    return lax.rsqrt(jnp.mean(values * values, axis=-1, keepdims=True) + epsilon)


def matmul(left_side, right_side):
    return jnp.dot(left_side, right_side, preferred_element_type=jnp.float32)


def contract_rows(left_side, right_side):
    return lax.dot_general(
        left_side, right_side, (((0,), (0,)), ((), ())), preferred_element_type=jnp.float32
    )


def against_rows(left_side, right_side):
    return lax.dot_general(
        left_side, right_side, (((1,), (1,)), ((), ())), preferred_element_type=jnp.float32
    )


def forward_pass(layer_rows, doc_rows, weights):
    w_in, w_out, w_gate, w_up, w_down, conv_taps, gain_one, gain_two = weights
    residual = layer_rows.astype(jnp.float32)
    model_width = residual.shape[1]
    seq_rows = residual.shape[0]
    tap_values = conv_taps.astype(jnp.float32)
    scale_one = rms_scale(residual)
    normed_one = (residual * scale_one * gain_one.astype(jnp.float32)).astype(jnp.bfloat16)
    projected = matmul(normed_one, w_in)
    b_part = projected[:, :model_width]
    c_part = projected[:, model_width : 2 * model_width]
    x_part = projected[:, 2 * model_width :]
    product_bx = b_part * x_part
    doc_float = doc_rows.astype(jnp.float32)
    rim_values, rim_ids = shifted((product_bx[-2:], doc_float[-2:]), "fsdp", 1)
    extended = jnp.concatenate([rim_values, product_bx], 0)
    extended_ids = jnp.concatenate([rim_ids, doc_float], 0)
    conv_out = tap_values[0] * product_bx
    doc_masks = []
    for offset in (1, 2):
        matching = (extended_ids[2 - offset : 2 - offset + seq_rows] == doc_float).astype(
            jnp.float32
        )[:, None]
        doc_masks.append(matching)
        conv_out = (
            conv_out + tap_values[offset] * matching * extended[2 - offset : 2 - offset + seq_rows]
        )
    gated_rows = (c_part * conv_out).astype(jnp.bfloat16)
    middle = residual + matmul(gated_rows, w_out)
    scale_two = rms_scale(middle)
    normed_two = (middle * scale_two * gain_two.astype(jnp.float32)).astype(jnp.bfloat16)
    gate_pre = matmul(normed_two, w_gate)
    up_pre = matmul(normed_two, w_up)
    hidden = (jax.nn.silu(gate_pre) * up_pre).astype(jnp.bfloat16)
    output = middle + matmul(hidden, w_down)
    saved_state = (
        residual,
        scale_one,
        normed_one,
        projected,
        extended,
        doc_masks,
        conv_out,
        gated_rows,
        middle,
        scale_two,
        normed_two,
        gate_pre,
        up_pre,
        hidden,
    )
    return (output, saved_state)


def backward_pass(cotan_rows, weights, saved_state):
    w_in, w_out, w_gate, w_up, w_down, conv_taps, gain_one, gain_two = weights
    (
        residual,
        scale_one,
        normed_one,
        projected,
        extended,
        doc_masks,
        conv_out,
        gated_rows,
        middle,
        scale_two,
        normed_two,
        gate_pre,
        up_pre,
        hidden,
    ) = saved_state
    model_width = residual.shape[1]
    seq_rows = residual.shape[0]
    tap_values = conv_taps.astype(jnp.float32)
    b_part = projected[:, :model_width]
    c_part = projected[:, model_width : 2 * model_width]
    x_part = projected[:, 2 * model_width :]
    grad_out = cotan_rows.astype(jnp.float32)
    grad_down = contract_rows(hidden, cotan_rows)
    grad_hidden = against_rows(cotan_rows, w_down)
    gate_prob = jax.nn.sigmoid(gate_pre)
    grad_gate = (grad_hidden * up_pre * gate_prob * (1.0 + gate_pre * (1.0 - gate_prob))).astype(
        jnp.bfloat16
    )
    grad_up = (grad_hidden * gate_pre * gate_prob).astype(jnp.bfloat16)
    grad_wgate = contract_rows(normed_two, grad_gate)
    grad_wup = contract_rows(normed_two, grad_up)
    grad_normed_two = against_rows(grad_gate, w_gate) + against_rows(grad_up, w_up)
    grad_gtwo = jnp.sum(grad_normed_two * middle * scale_two, axis=0)
    weighted = grad_normed_two * gain_two.astype(jnp.float32)
    grad_middle = (
        grad_out
        + scale_two * weighted
        - middle * scale_two**3 * jnp.mean(weighted * middle, axis=-1, keepdims=True)
    )
    grad_branch = grad_middle.astype(jnp.bfloat16)
    grad_wout = contract_rows(gated_rows, grad_branch)
    grad_gated = against_rows(grad_branch, w_out)
    grad_c = grad_gated * conv_out
    grad_conv = grad_gated * c_part
    grad_ext = jnp.pad(tap_values[0] * grad_conv, ((2, 0), (0, 0)))
    tap_rows = [jnp.sum(grad_conv * extended[2:], axis=0)]
    for offset, matching in zip((1, 2), doc_masks):
        masked_grad = matching * grad_conv
        grad_ext = grad_ext + jnp.pad(
            tap_values[offset] * masked_grad, ((2 - offset, offset), (0, 0))
        )
        tap_rows.append(jnp.sum(masked_grad * extended[2 - offset : 2 - offset + seq_rows], axis=0))
    rim_back = shifted(grad_ext[:2], "fsdp", -1)
    grad_bx = grad_ext[2:] + jnp.pad(rim_back, ((seq_rows - 2, 0), (0, 0)))
    grad_taps = jnp.stack(tap_rows)
    grad_proj = jnp.concatenate([grad_bx * x_part, grad_c, grad_bx * b_part], 1).astype(
        jnp.bfloat16
    )
    grad_win = contract_rows(normed_one, grad_proj)
    grad_normed_one = against_rows(grad_proj, w_in)
    grad_gone = jnp.sum(grad_normed_one * residual * scale_one, axis=0)
    weighted_one = grad_normed_one * gain_one.astype(jnp.float32)
    grad_input = (
        grad_middle
        + scale_one * weighted_one
        - residual * scale_one**3 * jnp.mean(weighted_one * residual, axis=-1, keepdims=True)
    )
    local_grads = (
        grad_win,
        grad_wout,
        grad_wgate,
        grad_wup,
        grad_down,
        grad_taps,
        grad_gone,
        grad_gtwo,
    )
    return (grad_input, local_grads)


def per_device(
    layer_in, segments, w_in, w_out, w_gate, w_up, w_down, conv_taps, gain_one, gain_two, cotangent
):
    outputs = []
    input_grads = []
    totals = None
    owned_grads = None
    for batch_index in range(layer_in.shape[0]):
        weights_now = (
            lax.all_gather(w_in, "fsdp", axis=1, tiled=True),
            lax.all_gather(w_out, "fsdp", axis=1, tiled=True),
            lax.all_gather(w_gate, "fsdp", axis=1, tiled=True),
            lax.all_gather(w_up, "fsdp", axis=1, tiled=True),
            lax.all_gather(w_down, "fsdp", axis=1, tiled=True),
            lax.all_gather(conv_taps, "fsdp", axis=1, tiled=True),
            lax.all_gather(gain_one, "fsdp", axis=0, tiled=True),
            lax.all_gather(gain_two, "fsdp", axis=0, tiled=True),
        )
        output, saved_state = forward_pass(
            layer_in[batch_index], segments[batch_index], weights_now
        )
        outputs.append(output)
        grad_input, local_grads = backward_pass(cotangent[batch_index], weights_now, saved_state)
        input_grads.append(grad_input)
        totals = local_grads if batch_index == 0 else jax.tree.map(jnp.add, totals, local_grads)
    owned_grads = tuple(
        lax.psum_scatter(
            total.astype(jnp.bfloat16), "fsdp", scatter_dimension=total.ndim - 1, tiled=True
        )
        for total in totals
    )
    summed = (
        lax.psum(owned_grads[0].astype(jnp.bfloat16), "rep").astype(jnp.float32),
        lax.psum(owned_grads[1].astype(jnp.bfloat16), "rep").astype(jnp.float32),
        lax.psum(owned_grads[2].astype(jnp.bfloat16), "rep").astype(jnp.float32),
        lax.psum(owned_grads[3].astype(jnp.bfloat16), "rep").astype(jnp.float32),
        lax.psum(owned_grads[4].astype(jnp.bfloat16), "rep").astype(jnp.float32),
        lax.psum(owned_grads[5].astype(jnp.bfloat16), "rep").astype(jnp.float32),
        lax.psum(owned_grads[6].astype(jnp.bfloat16), "rep").astype(jnp.float32),
        lax.psum(owned_grads[7].astype(jnp.bfloat16), "rep").astype(jnp.float32),
    )
    return (
        jnp.stack(outputs),
        jnp.stack(input_grads),
        summed[0],
        summed[1],
        summed[2],
        summed[3],
        summed[4],
        summed[5],
        summed[6],
        summed[7],
    )


MESH_ID = pl.DeviceIdType.MESH
BF16 = jnp.bfloat16
F32 = jnp.float32
CW, CCW = 0, 1
OUT, GN2, DOWN, GN1 = range(4)
WIN, WO, WG, WU, WD, WIN2 = range(6)


def dot_nn(a, b):
    return lax.dot_general(a, b, (((1,), (0,)), ((), ())), preferred_element_type=F32)


def dot_nt(a, b):
    return lax.dot_general(a, b, (((1,), (1,)), ((), ())), preferred_element_type=F32)


def dot_tn(a, b):
    return lax.dot_general(a, b, (((0,), (0,)), ((), ())), preferred_element_type=F32)


def span(start, size, step):
    return pl.ds(pl.multiple_of(start, step), size)


def layer_kernel(
    li, cot_in, win_in, wo_in, taps_in, wg_in, wu_in, wd_in, gains_in, ids_in,
    o_lo, o_gi, o_d, o_g, o_u, o_i, o_o, o_s,
    win, wo, wg, wu, wd, n1, n2, cot, proj, gated, gate, up, hidden, dwd,
    slots_d, slots_g, slots_u, part, rsib, rxn, middle, gmid,
    gains, masks, ids, hal, taps, hbx, halo_out, halo_in, dtap, dgain, mix_o, small_r, small_x,
    loc_sem, ag_s, ag_r, rs_s, rs_r, gain_s, gain_r, mask_s, mask_r, n1_s, n1_r,
    rim_s, rim_r, cot_s, cot_r, n2_s, n2_r, ex_s, ex_r, gb_s, gb_r, halo_s, halo_r, fin_s, fin_r, mx_s, mx_r,
    ms_s, ms_r, sm_s, sm_r, sx_s, sx_r, out_sem, sib_credit, xn_credit, oi_ready,
):
    r = lax.axis_index("rep")
    f = lax.axis_index("fsdp")
    x = lax.div(r, 2)
    c = lax.rem(r, 2)
    oc = 1 - c
    sib = 2 * x + oc
    xn = 2 * (1 - x) + c
    far = 2 * (1 - x) + oc
    y = lax.rem(f, 2)
    z = lax.div(f, 2)
    p = z + y * (7 - 2 * z)

    def f_at(place):
        place = lax.rem(place + 16, 8)
        yy = lax.div(place, 4)
        return 2 * (place + yy * (7 - 2 * place)) + yy

    right, left = f_at(p + 1), f_at(p - 1)
    toward = (right, left)

    def remote(src, dst, send, recv, device):
        return pltpu.make_async_remote_copy(
            src_ref=src, dst_ref=dst, send_sem=send, recv_sem=recv, device_id=device,
            device_id_type=MESH_ID,
        )

    def weight_slot(k, g):
        if k == WIN:
            return win.at[span(g * 192, 192, 64), :]
        if k == WO:
            return wo.at[:, span(g * 128, 128, 128)]
        if k == WG:
            return wg.at[span(g * 144, 144, 16), :]
        if k == WU:
            return wu.at[span(g * 144, 144, 16), :]
        return wd.at[:, span(g * 128, 128, 128)]

    def weight_part(k, g, h):
        if k == WIN:
            return win.at[span(g * 192, 192, 64), pl.ds(512 * h, 512)]
        if k == WO:
            return wo.at[pl.ds(288 * h, 288), span(g * 128, 128, 128)]
        if k == WG:
            return wg.at[span(g * 144, 144, 16), pl.ds(512 * h, 512)]
        if k == WU:
            return wu.at[span(g * 144, 144, 16), pl.ds(512 * h, 512)]
        return wd.at[pl.ds(576 * h, 576), span(g * 128, 128, 128)]

    reach = {WIN: (4, 3), WO: (3, 4), WG: (3, 4), WU: (3, 4), WD: (4, 3)}

    def ag_copy(k, s, way, g, h):
        view = weight_part(k, g, h)
        return remote(
            view, view, ag_s.at[k, way, s, h], ag_r.at[k, way, s, h], (r, toward[way])
        )

    def ag_send(k, s, way, h):
        ag_copy(k, s, way, f_at(p - s) if way == CW else f_at(p + s), h).start()

    def ag_start(k):
        for h in (0, 1):
            for way in (CW, CCW):
                ag_send(k, 0, way, h)

    def ag_event(k, s):
        for h in (0, 1):
            for way in (CW, CCW):
                if s < reach[k][way]:
                    g = f_at(p - 1 - s) if way == CW else f_at(p + 1 + s)
                    ag_copy(k, s, way, g, h).wait_recv()
                    if s + 1 < reach[k][way]:
                        ag_send(k, s + 1, way, h)

    def ag_drain(k):
        for way in (CW, CCW):
            for s in range(reach[k][way]):
                for h in (0, 1):
                    ag_copy(k, s, way, f, h).wait_send()

    def grad_piece(k, g, way):
        if k == WD:
            return dwd.at[pl.ds(576 * way, 576), span(g * 128, 128, 128)]
        if k == WG:
            return cot.at[span(g * 144, 144, 16), pl.ds(512 * way, 512)]
        if k == WU:
            return wu.at[span(g * 144, 144, 16), pl.ds(512 * way, 512)]
        if k == WO:
            return gate.at[pl.ds(512 + 256 * way, 256), span(1024 + g * 128, 128, 128)]
        return gate.at[
            span(192 * lax.rem(g, 6), 192, 64), span(1024 * lax.div(g, 6) + 512 * way + 256 * (k == WIN2), 256, 128)
        ]

    def sum_slot(k, way, s):
        if k == WD:
            return slots_d.at[way, s]
        if k == WG:
            return slots_g.at[way, s]
        if k == WU:
            return slots_u.at[way, s]
        i = way * 7 + s
        if k == WO:
            return up.at[pl.ds(768, 256), pl.ds(128 * i, 128)]
        return up.at[pl.ds(192 * (i // 4), 192), pl.ds(512 * (i % 4) + 256 * (k == WIN2), 256)]

    def rs_copy(k, way, s):
        src = sum_slot(k, way, s - 1) if s else grad_piece(
            k, f_at(p - 1) if way == CW else f_at(p + 1), way
        )
        return remote(
            src, sum_slot(k, way, s), rs_s.at[k, way, s], rs_r.at[k, way, s], (r, toward[way])
        )

    def rs_start(k):
        rs_copy(k, CW, 0).start()
        rs_copy(k, CCW, 0).start()

    def rs_event(k, s):
        for way in (CW, CCW):
            g = f_at(p - 2 - s) if way == CW else f_at(p + 2 + s)
            rs_copy(k, way, s).wait_recv()
            slot = sum_slot(k, way, s)
            slot[...] = (slot[...].astype(F32) + grad_piece(k, g, way)[...].astype(F32)).astype(BF16)
            if s < 6:
                rs_copy(k, way, s + 1).start()

    def rs_drain(k):
        for way in (CW, CCW):
            for s in range(7):
                rs_copy(k, way, s).wait_send()

    ffn_out = {WD: (0, o_d), WG: (1, o_g), WU: (2, o_u)}
    peers = (sib, xn, far)

    def final_view(k, owner, way):
        out = ffn_out[k][1]
        if k == WD:
            return out.at[owner, pl.ds(576 * way, 576), :]
        return out.at[owner, :, pl.ds(512 * way, 512)]

    def final_copy(k, way, j):
        i = ffn_out[k][0]
        src = final_view(k, xn, way) if j == 2 else sum_slot(k, way, 6)
        dst = final_view(k, xn if j == 2 else r, way)
        if j == 3:
            return pltpu.make_async_copy(src, dst, fin_s.at[i, way, 3])
        return remote(
            src, dst, fin_s.at[i, way, j], fin_r.at[i, way, j], (xn if j == 1 else sib, f)
        )

    def final_start(k):
        for way in (CW, CCW):
            for j in (1, 0, 3):
                final_copy(k, way, j).start()

    def final_arrive(k, way, j):
        i = ffn_out[k][0]
        view = final_view(k, peers[j], way)
        remote(view, view, fin_s.at[i, way, j], fin_r.at[i, way, j], (sib, f)).wait_recv()

    def final_forward(k):
        for way in (CW, CCW):
            final_arrive(k, way, 1)
            final_copy(k, way, 2).start()

    def final_drain(k):
        for way in (CW, CCW):
            final_copy(k, way, 3).wait()
            for j in range(3):
                final_copy(k, way, j).wait_send()
            final_arrive(k, way, 0)
            final_arrive(k, way, 2)

    loads = [
        pltpu.make_async_copy(win_in, weight_slot(WIN, f), loc_sem.at[0]),
        pltpu.make_async_copy(
            taps_in, wo.at[pl.ds(512, 64), span(f * 128, 128, 128)], loc_sem.at[1]
        ),
        pltpu.make_async_copy(li, part.at[0], loc_sem.at[2]),
        pltpu.make_async_copy(cot_in, cot.at[span(r * 512, 512, 512), :], loc_sem.at[3]),
        pltpu.make_async_copy(wg_in, weight_slot(WG, f), loc_sem.at[4]),
        pltpu.make_async_copy(wu_in, weight_slot(WU, f), loc_sem.at[5]),
        pltpu.make_async_copy(ids_in, ids.at[0], loc_sem.at[6]),
        pltpu.make_async_copy(gains_in, gains.at[:, span(f * 128, 128, 128)], loc_sem.at[7]),
    ]
    loads_out = [
        pltpu.make_async_copy(
            wo_in.at[g, c], wo.at[pl.ds(64 * g, 64), span(f * 128, 128, 128)], loc_sem.at[8 + g]
        )
        for g in range(8)
    ]
    loads_down = [
        pltpu.make_async_copy(
            wd_in.at[g, r], wd.at[pl.ds(144 * g, 144), span(f * 128, 128, 128)], loc_sem.at[16 + g]
        )
        for g in range(8)
    ]
    for load in loads[:2] + loads_out + loads[2:] + loads_down:
        load.start()
    barrier = pltpu.get_barrier_semaphore()
    for j in range(1, 8):
        pl.semaphore_signal(
            barrier, inc=1, device_id=(r, lax.rem(f + j, 8)), device_id_type=MESH_ID
        )
    for peer in peers:
        pl.semaphore_signal(barrier, inc=1, device_id=(peer, f), device_id_type=MESH_ID)
    dtap[...] = jnp.zeros_like(dtap)
    dgain[...] = jnp.zeros_like(dgain)
    pl.semaphore_wait(barrier, 10)

    def gain_copy(j):
        return remote(
            gains_in, gains.at[:, span(f * 128, 128, 128)], gain_s.at[j - 1], gain_r.at[j - 1],
            (r, lax.rem(f + j, 8)),
        )

    def cot_copy(m, j):
        rows = span((xn if j == 2 else r) * 512 + m * 256, 256, 256)
        return remote(
            cot.at[rows, :], cot.at[rows, :], cot_s.at[m, j], cot_r.at[m, j],
            (xn if j == 1 else sib, f),
        )

    def cot_arrive(m, j):
        rows = span((sib, xn, far)[j] * 512 + m * 256, 256, 256)
        remote(
            cot.at[rows, :], cot.at[rows, :], cot_s.at[m, j], cot_r.at[m, j], (sib, f)
        ).wait_recv()

    def n2_copy(m, j):
        rows = span((xn if j == 2 else r) * 512 + m * 256, 256, 256)
        return remote(
            n2.at[rows, :], n2.at[rows, :], n2_s.at[m, j], n2_r.at[m, j],
            (xn if j == 1 else sib, f),
        )

    def n2_arrive(m, j):
        rows = span((sib, xn, far)[j] * 512 + m * 256, 256, 256)
        remote(
            n2.at[rows, :], n2.at[rows, :], n2_s.at[m, j], n2_r.at[m, j], (sib, f)
        ).wait_recv()

    def rim_copy(j):
        if j == 2:
            src, dst = ids_in, ids.at[1]
        else:
            src, dst = li.at[pl.ds(240 + 256 * j, 16), :], hal.at[pl.ds(16 * j, 16), :]
        return remote(src, dst, rim_s.at[j], rim_r.at[j], (r, lax.rem(f + 1, 8)))

    for j in range(1, 8):
        gain_copy(j).start()
    for j in range(3):
        rim_copy(j).start()
    for load in loads[:2] + loads_out:
        load.wait()
    ag_start(WIN)
    ag_start(WO)
    loads[3].wait()
    for m in (0, 1):
        cot_copy(m, 0).start()
        cot_copy(m, 1).start()
    loads[2].wait()
    loads[7].wait()
    for j in range(1, 8):
        gain_copy(j).wait_recv()

    gain_one = gains[0:1, :]
    gain_two = gains[1:2, :]

    def norm_rows(rows):
        rows = rows.astype(F32)
        scale = lax.rsqrt(jnp.mean(rows * rows, axis=1, keepdims=True) + epsilon)
        return (rows * scale * gain_one).astype(BF16)

    def norm_step(i, carry):
        rows = span(i * 64, 64, 64)
        n1[c, rows, :] = norm_rows(part[0, rows, :])
        return carry

    lax.fori_loop(0, 8, norm_step, 0)
    for j in range(3):
        rim_copy(j).wait_recv()
    started = jnp.where(f > 0, 1.0, 0.0).astype(F32)
    n1[c, 512:544, :] = norm_rows(hal[...].astype(F32) * started)
    n1_copy = remote(n1.at[c], n1.at[c], n1_s, n1_r, (sib, f))
    n1_copy.start()
    loads[6].wait()
    here, before = ids[0], ids[1]
    lane_ids = lax.broadcasted_iota(jnp.int32, (8, 256), 1)
    last = before[:, 255:256]
    prev = jnp.where(lane_ids == 0, last, pltpu.roll(here, 1, 1))
    masks[c, 0:8, :] = jnp.where(prev == here, 1.0, 0.0)
    prev = jnp.where(
        lane_ids == 0, before[:, 254:255], jnp.where(lane_ids == 1, last, pltpu.roll(here, 2, 1))
    )
    masks[c, 8:16, :] = jnp.where(prev == here, 1.0, 0.0)
    mask_copy = remote(masks.at[c], masks.at[c], mask_s, mask_r, (sib, f))
    mask_copy.start()

    pending = []

    def tick(count=1):
        for _ in range(count):
            if pending:
                job, *rest = pending.pop(0)
                job(*rest)

    for s in (0, 1):
        ag_event(WIN, s)
        ag_event(WO, s)
    for load in loads[4:6] + loads_down:
        load.wait()
    ag_start(WG)
    ag_event(WIN, 2)
    ag_event(WO, 2)
    ag_event(WG, 0)
    for m in (0, 1):
        cot_arrive(m, 1)
        cot_copy(m, 2).start()
    ag_event(WIN, 3)
    ag_event(WO, 3)
    ag_start(WU)
    ag_start(WD)
    pending += [
        (ag_event, WG, 1), (ag_event, WU, 0), (ag_event, WG, 2), (ag_event, WU, 1), (ag_event, WD, 0),
        (ag_event, WG, 3), (ag_event, WU, 2), (ag_event, WD, 1), (ag_event, WU, 3),
        (ag_event, WD, 2), (ag_event, WD, 3),
    ]

    for g in range(8):
        taps[64 * g : 64 * g + 64, :] = wo[512:576, 128 * g : 128 * g + 128]
    remote(n1.at[oc], n1.at[oc], n1_s, n1_r, (sib, f)).wait_recv()
    remote(masks.at[oc], masks.at[oc], mask_s, mask_r, (sib, f)).wait_recv()
    lane256 = lax.broadcasted_iota(jnp.int32, (64, 256), 1)

    def halo_product(qc):
        rows = n1[qc, 512:544, :]
        return dot_nt(win[0:512, :], rows) * dot_nt(win[1024:1536, :], rows)

    hbx[:, 0:32] = halo_product(0)
    hbx[:, 32:64] = halo_product(1)

    def earlier(bx, qc, rows, m):
        held = hbx[rows, 0:64]
        place = 32 * qc + 16 * m
        spot = lax.broadcasted_iota(jnp.int32, (64, 64), 1) - place
        one = jnp.sum(jnp.where(spot == 15, held, 0.0), axis=1, keepdims=True)
        two = jnp.sum(jnp.where(spot == 14, held, 0.0), axis=1, keepdims=True)
        prev_one = jnp.where(lane256 == 0, one, pltpu.roll(bx, 1, 1))
        prev_two = jnp.where(
            lane256 == 0, two, jnp.where(lane256 == 1, one, pltpu.roll(bx, 2, 1))
        )
        return prev_one, prev_two

    def tap_columns(rows):
        held = taps[rows, :].astype(F32)
        return held[:, 0:1], held[:, 1:2], held[:, 2:3]

    def mix_fwd(qc, m):
        tokens = n1[qc, 256 * m : 256 * m + 256, :]
        lanes = span(qc * 512 + m * 256, 256, 256)
        mask_one = masks[qc, m : m + 1, :]
        mask_two = masks[qc, 8 + m : 9 + m, :]
        for i in range(3):
            gmid[:, 256 * i : 256 * i + 256] = dot_nt(win[512 * i : 512 * i + 512, :], tokens)

        def step(i, carry):
            rows = span(64 * i, 64, 64)
            b, cc, xx = gmid[rows, 0:256], gmid[rows, 256:512], gmid[rows, 512:768]
            proj[rows, lanes] = b.astype(BF16)
            proj[span(512 + 64 * i, 64, 64), lanes] = cc.astype(BF16)
            proj[span(1024 + 64 * i, 64, 64), lanes] = xx.astype(BF16)
            bx = b * xx
            prev_one, prev_two = earlier(bx, qc, rows, m)
            t0, t1, t2 = tap_columns(rows)
            conv = (
                t0 * bx + t1 * (mask_one * prev_one) + t2 * (mask_two * prev_two)
            )
            gated[rows, lanes] = (cc * conv).astype(BF16)
            return carry

        lax.fori_loop(0, 8, step, 0)
        return dot_tn(gated[:, lanes], wo[0:512, :])

    def ex_copy(op, kind, m):
        rows = span(256 * m, 256, 256)
        src = part.at[{0: 1, 1: 0, 2: 2}[kind], rows, :]
        if op == DOWN and kind == 2:
            src = cot.at[span(1152 + 256 * m, 256, 128), :]
        dst = rxn.at[rows, :] if kind == 2 else rsib.at[kind, rows, :]
        return remote(
            src, dst, ex_s.at[op, kind, m], ex_r.at[op, kind, m], (xn if kind == 2 else sib, f)
        )

    for m in (0, 1):
        part[1, 256 * m : 256 * m + 256, :] = mix_fwd(oc, m).astype(BF16)
        ex_copy(OUT, 0, m).start()
        middle[256 * m : 256 * m + 256, :] = mix_fwd(c, m)
        ex_copy(OUT, 0, m).wait_recv()

        def norm_two_step(i, carry):
            rows = span(256 * m + i * 64, 64, 64)
            mid = middle[rows, :] + rsib[0, rows, :].astype(F32) + part[0, rows, :].astype(F32)
            middle[rows, :] = mid
            scale = lax.rsqrt(jnp.mean(mid * mid, axis=1, keepdims=True) + epsilon)
            n2[span(r * 512 + 256 * m + i * 64, 64, 64), :] = (mid * scale * gain_two).astype(BF16)
            return carry

        lax.fori_loop(0, 4, norm_two_step, 0)
        n2_copy(m, 1).start()
        n2_copy(m, 0).start()
        tick(2)
    pl.semaphore_signal(sib_credit, inc=1, device_id=(sib, f), device_id_type=MESH_ID)
    mid_copy = pltpu.make_async_copy(middle, o_lo, out_sem.at[0])
    mid_copy.start()
    for m in (0, 1):
        ex_copy(OUT, 0, m).wait_send()
    tick(3)
    for m in (0, 1):
        n2_arrive(m, 1)
        n2_copy(m, 2).start()
        tick()
    assert pending[0] == (ag_event, WD, 2)

    def gate_up(q):
        def step(i, carry):
            rows = span(lax.rem(i, 3) * 384, 384, 128)
            tokens = span(q * 512 + lax.div(i, 3) * 256, 256, 256)
            g = dot_nt(wg[rows, :], n2[tokens, :])
            u = dot_nt(wu[rows, :], n2[tokens, :])
            gate[rows, tokens] = g.astype(BF16)
            up[rows, tokens] = u.astype(BF16)
            hidden[rows, tokens] = (g * jax.nn.sigmoid(g) * u).astype(BF16)
            return carry

        lax.fori_loop(0, 6, step, 0)

    gate_up(r)
    for m in (0, 1):
        n2_arrive(m, 0)
    gate_up(sib)
    tick()
    gate_up(xn)
    for m in (0, 1):
        n2_arrive(m, 2)
    gate_up(far)
    for m in (0, 1):
        cot_arrive(m, 0)
        cot_arrive(m, 2)

    def dwd_step(i, carry):
        rows = span(i * 384, 384, 128)
        for n in (0, 512):
            dwd[rows, n : n + 512] = dot_nn(hidden[rows, :], cot[:, n : n + 512]).astype(BF16)
        return carry

    lax.fori_loop(0, 3, dwd_step, 0)
    rs_start(WD)
    tick(len(pending))

    def ring(*events):
        for k, s in events:
            rs_event(k, s)

    def grad_hidden(q):
        def step(i, carry):
            rows = span(lax.rem(i, 3) * 384, 384, 128)
            tokens = span(q * 512 + lax.div(i, 3) * 256, 256, 256)
            gh = dot_nt(wd[rows, :], cot[tokens, :])
            g = gate[rows, tokens].astype(F32)
            u = up[rows, tokens].astype(F32)
            s = jax.nn.sigmoid(g)
            gate[rows, tokens] = (gh * u * s * (1.0 + g * (1.0 - s))).astype(BF16)
            up[rows, tokens] = (gh * g * s).astype(BF16)
            return carry

        lax.fori_loop(0, 6, step, 0)

    for i, q in enumerate((r, sib, xn, far)):
        grad_hidden(q)
        if i % 2:
            ring((WD, i // 2))
    for m in (0, 1):
        for j in range(3):
            cot_copy(m, j).wait_send()
            n2_copy(m, j).wait_send()
    ag_drain(WG)
    ag_drain(WU)

    def dwg_step(i, carry):
        rows = span(i * 384, 384, 128)
        for n in (0, 512):
            cot[rows, n : n + 512] = dot_nn(gate[rows, :], n2[:, n : n + 512]).astype(BF16)
        return carry


    def gn2_part(q, m):
        tokens = span(q * 512 + m * 256, 256, 256)
        return dot_tn(gate[:, tokens], wg[...]) + dot_tn(up[:, tokens], wu[...])

    def down_part(q, m):
        return dot_tn(hidden[:, span(q * 512 + m * 256, 256, 256)], wd[...])

    def to_part(partial, q, dst, op=None, kind=None):
        def step(m, carry):
            dst(m)[...] = partial(q, m).astype(BF16)
            if op is not None:
                ex_copy(op, kind, m).start()
            return carry

        lax.fori_loop(0, 2, step, 0)

    def part_rows(slot):
        return lambda m: part.at[slot, span(256 * m, 256, 256), :]

    def core_sum(op, dst):
        for m in (0, 1):
            ex_copy(op, 1, m).wait_recv()

            def add_step(i, carry):
                rows = span(256 * m + i * 64, 64, 64)
                view = dst(256 * m + i * 64)
                view[...] = (view[...].astype(F32) + rsib[1, rows, :].astype(F32)).astype(BF16)
                return carry

            lax.fori_loop(0, 4, add_step, 0)
            ex_copy(op, 2, m).start()

    pl.semaphore_wait(sib_credit, 1)
    to_part(gn2_part, far, part_rows(0), GN2, 1)
    to_part(gn2_part, xn, part_rows(2))
    core_sum(GN2, lambda at: part.at[2, span(at, 64, 64), :])
    ring((WD, 2))
    lax.fori_loop(0, 3, dwg_step, 0)
    rs_start(WG)
    ring((WD, 3))

    def own_step(m, carry):
        gmid[span(256 * m, 256, 256), :] = gn2_part(r, m)
        return carry

    lax.fori_loop(0, 2, own_step, 0)
    to_part(gn2_part, sib, part_rows(1))
    for m in (0, 1):
        ex_copy(GN2, 0, m).start()
    ring((WD, 4), (WG, 0))
    cot_again = pltpu.make_async_copy(
        cot_in, gate.at[pl.ds(0, 512), pl.ds(0, 1024)], loc_sem.at[3]
    )
    cot_again.start()

    def dwu_step(i, carry):
        rows = span(i * 384, 384, 128)
        for n in (0, 512):
            wu[rows, n : n + 512] = dot_nn(up[rows, :], n2[:, n : n + 512]).astype(BF16)
        return carry

    lax.fori_loop(0, 3, dwu_step, 0)
    rs_start(WU)
    pl.semaphore_signal(oi_ready, inc=1, device_id=(r, right), device_id_type=MESH_ID)
    pl.semaphore_signal(oi_ready, inc=1, device_id=(r, left), device_id_type=MESH_ID)
    ring((WD, 5), (WG, 1))

    for m in (0, 1):
        ex_copy(GN2, 0, m).wait_send()
        ex_copy(GN2, 1, m).wait_send()
    to_part(down_part, far, part_rows(0))
    to_part(down_part, sib, part_rows(1))
    ring((WD, 6), (WG, 2), (WU, 0))
    to_part(down_part, xn, lambda m: cot.at[span(1152 + 256 * m, 256, 128), :])
    cot_again.wait()
    gb_copies = []
    for m in (0, 1):
        ex_copy(GN2, 0, m).wait_recv()
        ex_copy(GN2, 2, m).wait_recv()

        def grad_middle_step(i, carry):
            rows = span(256 * m + i * 64, 64, 64)
            gn = gmid[rows, :] + rsib[0, rows, :].astype(F32) + rxn[rows, :].astype(F32)
            mid = middle[rows, :]
            scale = lax.rsqrt(jnp.mean(mid * mid, axis=1, keepdims=True) + epsilon)
            dgain[1:2, :] += jnp.sum(gn * (mid * scale), axis=0, keepdims=True)
            weighted = gn * gain_two
            inner = jnp.mean(weighted * mid, axis=1, keepdims=True)
            gm = (
                gate[rows, 0:1024].astype(F32)
                + scale * weighted
                - mid * (scale * scale * scale * inner)
            )
            gmid[rows, :] = gm
            wg[span(c * 512 + 256 * m + i * 64, 64, 64), :] = gm.astype(BF16)
            return carry

        lax.fori_loop(0, 4, grad_middle_step, 0)
        rows = span(c * 512 + 256 * m, 256, 256)
        copy = remote(wg.at[rows, :], wg.at[rows, :], gb_s.at[m], gb_r.at[m], (sib, f))
        copy.start()
        gb_copies.append(copy)
    pl.semaphore_signal(sib_credit, inc=1, device_id=(sib, f), device_id_type=MESH_ID)
    pl.semaphore_signal(xn_credit, inc=1, device_id=(xn, f), device_id_type=MESH_ID)
    mid_copy.wait()
    pl.semaphore_wait(sib_credit, 1)
    for m in (0, 1):
        ex_copy(DOWN, 1, m).start()
        ex_copy(DOWN, 0, m).start()
    for m in (0, 1):
        ex_copy(GN2, 2, m).wait_send()
        rows = span(oc * 512 + 256 * m, 256, 256)
        remote(wg.at[rows, :], wg.at[rows, :], gb_s.at[m], gb_r.at[m], (sib, f)).wait_recv()

    mix_place = {WIN: 0, WIN2: 1, WO: 2}

    def mix_sum(k, way):
        if k == WO:
            return mix_o.at[pl.ds(256 * way, 256), :]
        return cot.at[pl.ds(1664, 192), pl.ds(512 * way + 256 * (k == WIN2), 256)]

    def mx_copy(k, way):
        i = mix_place[k]
        return remote(
            sum_slot(k, way, 6), mix_sum(k, way), mx_s.at[i, way], mx_r.at[i, way], (xn, f)
        )

    def mix_start(k):
        for way in (CW, CCW):
            mx_copy(k, way).start()

    def mix_view(k, owner, way):
        if k == WO:
            return o_o.at[owner, pl.ds(256 * way, 256), :]
        return o_i.at[owner, :, pl.ds(512 * way + 256 * (k == WIN2), 256)]

    def mix_copies(k, way):
        i = mix_place[k]
        dst = mix_sum(k, way)
        return (
            remote(dst, mix_view(k, c, way), ms_s.at[i, way], ms_r.at[i, way], (sib, f)),
            pltpu.make_async_copy(dst, mix_view(k, c, way), out_sem.at[3 + 2 * i + way]),
        )

    lane128 = lax.broadcasted_iota(jnp.int32, (512, 128), 1)
    rim = jnp.zeros((512, 128), F32)
    taps_one, taps_two = tap_columns(slice(None))[1:]
    for qc in (0, 1):
        for m in (0, 1):
            at = qc * 512 + m * 256
            gg = dot_nt(wo[0:512, :], wg[at : at + 16, :])
            gc = gg * proj[512:1024, at : at + 128].astype(F32)[:, 0:16]
            masked_one = masks[qc, m : m + 1, 0:16] * gc
            masked_two = masks[qc, 8 + m : 9 + m, 0:16] * gc
            first = taps_two * masked_two[:, 0:1]
            second = taps_one * masked_one[:, 0:1] + taps_two * masked_two[:, 1:2]
            b = 2 * (2 * qc + m)
            rim = jnp.where(lane128 == b, first, jnp.where(lane128 == b + 1, second, rim))
    halo_out[...] = rim.astype(BF16)
    halo_copy = remote(halo_out, halo_in, halo_s, halo_r, (r, lax.rem(f + 7, 8)))
    halo_copy.start()

    for n in (0, 512):
        gate[512:1024, 1024 + n : 1536 + n] = dot_nn(gated[...], wg[0:1024, n : n + 512]).astype(BF16)
    pl.semaphore_wait(oi_ready, 2)
    rs_start(WO)
    ring((WG, 3), (WU, 1))
    halo_copy.wait_recv()
    inside = jnp.where(f < 7, 1.0, 0.0).astype(F32)
    lane_tap = lax.broadcasted_iota(jnp.int32, (64, 128), 1)

    def mix_bwd(qc, m):
        lanes = pl.ds(qc * 512 + m * 256, 256)
        tokens = wg[qc * 512 + m * 256 : qc * 512 + m * 256 + 256, :]
        mask_one = masks[qc, m : m + 1, :]
        mask_two = masks[qc, 8 + m : 9 + m, :]
        b2 = 2 * (2 * qc + m)
        middle[:, 0:256] = dot_nt(wo[0:512, :], tokens)

        def step(i, carry):
            rows = span(64 * i, 64, 64)
            c_rows, x_rows = span(512 + 64 * i, 64, 64), span(1024 + 64 * i, 64, 64)
            gg = middle[rows, 0:256]
            b = proj[rows, lanes].astype(F32)
            cc = proj[c_rows, lanes].astype(F32)
            xx = proj[x_rows, lanes].astype(F32)
            bx = b * xx
            prev_one, prev_two = earlier(bx, qc, rows, m)
            prev_one = mask_one * prev_one
            prev_two = mask_two * prev_two
            t0, t1, t2 = tap_columns(rows)
            conv = t0 * bx + t1 * prev_one + t2 * prev_two
            gc = gg * cc
            sum0 = jnp.sum(gc * bx, axis=1, keepdims=True)
            sum1 = jnp.sum(gc * prev_one, axis=1, keepdims=True)
            sum2 = jnp.sum(gc * prev_two, axis=1, keepdims=True)
            dtap[rows, :] += jnp.where(
                lane_tap == 0, sum0, jnp.where(lane_tap == 1, sum1, jnp.where(lane_tap == 2, sum2, 0.0))
            )
            back_one = jnp.where(lane256 < 255, pltpu.roll(mask_one * gc, 255, 1), 0.0)
            back_two = jnp.where(lane256 < 254, pltpu.roll(mask_two * gc, 254, 1), 0.0)
            edge = halo_in[rows, :].astype(F32) * inside
            back = jnp.where(
                lane256 == 254, edge[:, b2 : b2 + 1],
                jnp.where(lane256 == 255, edge[:, b2 + 1 : b2 + 2], 0.0),
            )
            gbx = t0 * gc + t1 * back_one + t2 * back_two + back
            proj[rows, lanes] = (gbx * xx).astype(BF16)
            proj[c_rows, lanes] = (gg * conv).astype(BF16)
            proj[x_rows, lanes] = (gbx * b).astype(BF16)
            return carry

        lax.fori_loop(0, 8, step, 0)

    for qc in (0, 1):
        for m in (0, 1):
            mix_bwd(qc, m)
        if qc == 0:
            ring((WG, 4), (WU, 2), (WO, 0))
            pl.semaphore_wait(xn_credit, 1)
            core_sum(DOWN, lambda at: cot.at[span(1152 + at, 64, 64), :])
            pl.semaphore_signal(sib_credit, inc=1, device_id=(sib, f), device_id_type=MESH_ID)
            final_start(WD)
    ring((WG, 5), (WU, 3), (WO, 1))

    def dwin(t, n):
        rows = span(384 * t, 384, 128)
        return (
            dot_nn(proj[rows, 0:512], n1[0, 0:512, n : n + 512])
            + dot_nn(proj[rows, 512:1024], n1[1, 0:512, n : n + 512])
        ).astype(BF16)

    def dwin_step(t, carry):
        for n in (0, 512):
            gate[span(384 * t, 384, 128), n : n + 512] = dwin(t, n)
        return carry

    lax.fori_loop(0, 3, dwin_step, 0)
    for n in (0, 512):
        gate[0:384, 1024 + n : 1536 + n] = dwin(3, n)
    rs_start(WIN)
    rs_start(WIN2)
    ring((WG, 6), (WU, 4), (WO, 2))
    final_start(WG)

    def gn1_part(qc, m):
        return dot_tn(proj[:, span(qc * 512 + m * 256, 256, 256)], win[...])

    pl.semaphore_wait(sib_credit, 1)
    for m in (0, 1):
        ex_copy(DOWN, 0, m).wait_send()
        ex_copy(DOWN, 1, m).wait_send()
    li_again = pltpu.make_async_copy(li, part.at[1], loc_sem.at[2])
    li_again.start()
    to_part(gn1_part, oc, part_rows(0), GN1, 1)
    ring((WU, 5), (WO, 3), (WIN, 0), (WIN2, 0))
    for m in (0, 1):
        middle[256 * m : 256 * m + 256, :] = gn1_part(c, m)
    ring((WU, 6), (WO, 4), (WIN, 1), (WIN2, 1))
    final_start(WU)
    li_again.wait()
    for m in (0, 1):
        ex_copy(GN1, 1, m).wait_recv()

        def grad_in_step(i, carry):
            rows = span(256 * m + i * 64, 64, 64)
            gn = middle[rows, :] + rsib[1, rows, :].astype(F32)
            res = part[1, rows, :].astype(F32)
            scale = lax.rsqrt(jnp.mean(res * res, axis=1, keepdims=True) + epsilon)
            dgain[0:1, :] += jnp.sum(gn * (res * scale), axis=0, keepdims=True)
            weighted = gn * gain_one
            inner = jnp.mean(weighted * res, axis=1, keepdims=True)
            middle[rows, :] = gmid[rows, :] + scale * weighted - res * (scale * scale * scale * inner)
            return carry

        lax.fori_loop(0, 4, grad_in_step, 0)
    gi_copy = pltpu.make_async_copy(middle, o_gi, out_sem.at[1])
    gi_copy.start()
    for m in (0, 1):
        ex_copy(GN1, 1, m).wait_send()

    for g in range(8):
        gmid[0:64, 128 * g : 128 * g + 128] = dtap[64 * g : 64 * g + 64, :]
        gmid[64:72, 128 * g : 128 * g + 128] = dgain[:, 128 * g : 128 * g + 128]

    def small_p(g):
        return gmid.at[pl.ds(0, 72), span(g * 128, 128, 128)]

    def small_copy(j):
        g = lax.rem(f + j, 8)
        return remote(small_p(g), small_r.at[j], sm_s.at[j - 1], sm_r.at[j - 1], (r, g))

    for j in range(1, 8):
        small_copy(j).start()
    ring((WO, 5), (WIN, 2), (WIN2, 2))
    total = small_p(f)[...]
    for j in range(1, 8):
        small_copy(j).wait_recv()
        total = total + small_r[j]
    small_x[0] = total
    sx_copy = remote(small_x.at[0], small_x.at[1], sx_s.at[0], sx_r.at[0], (xn, f))
    sx_copy.start()
    gi_copy.wait()
    mid_again = pltpu.make_async_copy(o_lo, middle, out_sem.at[0])
    mid_again.start()
    ring((WO, 6), (WIN, 3), (WIN2, 3))
    final_forward(WD)
    sx_copy.wait_recv()
    small_x[2] = small_x[0] + small_x[1]
    ss_copy = remote(small_x.at[2], o_s.at[c], sx_s.at[1], sx_r.at[1], (sib, f))
    ss_copy.start()
    so_copy = pltpu.make_async_copy(small_x.at[2], o_s.at[c], out_sem.at[2])
    so_copy.start()
    for way in (CW, CCW):
        mx_copy(WO, way).start()

    mid_again.wait()
    for m in (0, 1):
        ex_copy(DOWN, 0, m).wait_recv()
        ex_copy(DOWN, 2, m).wait_recv()
        middle[256 * m : 256 * m + 256, :] += down_part(r, m)

        def out_step(i, carry):
            rows = span(256 * m + i * 64, 64, 64)
            middle[rows, :] += rsib[0, rows, :].astype(F32) + rxn[rows, :].astype(F32)
            return carry

        lax.fori_loop(0, 4, out_step, 0)
        ring((WIN, 4 + m), (WIN2, 4 + m))
    lo_copy = pltpu.make_async_copy(middle, o_lo, out_sem.at[0])
    lo_copy.start()
    final_forward(WG)
    ring((WIN, 6))
    mix_start(WIN)
    ring((WIN2, 6))
    mix_start(WIN2)
    final_forward(WU)

    for k in (WO, WIN, WIN2):
        for way in (CW, CCW):
            mx_copy(k, way).wait_recv()
            dst = mix_sum(k, way)
            dst[...] = (dst[...].astype(F32) + sum_slot(k, way, 6)[...].astype(F32)).astype(BF16)
            for out in mix_copies(k, way):
                out.start()

    for k in (WIN, WO, WD):
        ag_drain(k)
    for k in range(6):
        rs_drain(k)
    for k in (WD, WG, WU):
        final_drain(k)
    for j in range(1, 8):
        gain_copy(j).wait_send()
        small_copy(j).wait_send()
    mask_copy.wait_send()
    for j in range(3):
        rim_copy(j).wait_send()
    n1_copy.wait_send()
    for m in (0, 1):
        gb_copies[m].wait_send()
    halo_copy.wait_send()
    lo_copy.wait()
    so_copy.wait()
    for m in (0, 1):
        ex_copy(DOWN, 2, m).wait_send()
    sx_copy.wait_send()
    ss_copy.wait_send()
    other = o_s.at[oc]
    remote(other, other, sx_s.at[1], sx_r.at[1], (sib, f)).wait_recv()
    for k in (WO, WIN, WIN2):
        i = mix_place[k]
        for way in (CW, CCW):
            mx_copy(k, way).wait_send()
            out, local = mix_copies(k, way)
            out.wait_send()
            local.wait()
            view = mix_view(k, oc, way)
            remote(view, view, ms_s.at[i, way], ms_r.at[i, way], (sib, f)).wait_recv()


def grouped_device(
    layer_in, segments, w_in, w_out, w_gate, w_up, w_down, conv_taps, gain_one, gain_two, cotangent
):
    r = lax.axis_index("rep")
    c = lax.rem(r, 2)
    width = layer_in.shape[2]

    def pick(array, axis, index):
        return lax.dynamic_index_in_dim(array, index, axis, keepdims=False)

    ids = jnp.pad(segments.astype(F32), ((0, 6), (0, 0)))
    own_in = pick(w_in.reshape(width, 3, 2, 64), 2, c).reshape(width, 192).T
    tap_half = pick(conv_taps.reshape(3, 2, 64), 1, c)
    tap_cols = jnp.pad(tap_half.T, ((0, 0), (0, 125)))
    own_gate = pick(w_gate.reshape(width, 4, 144), 1, r).T
    own_up = pick(w_up.reshape(width, 4, 144), 1, r).T
    gains = jnp.pad(jnp.stack([gain_one, gain_two]).astype(F32), ((0, 6), (0, 0)))

    hbm = pl.BlockSpec(memory_space=pl.ANY)
    dma = pltpu.SemaphoreType.DMA
    regular = pltpu.SemaphoreType.REGULAR

    def big(*shape, dtype=BF16):
        return pltpu.VMEM(shape, dtype)

    outs = pl.pallas_call(
        layer_kernel,
        out_shape=(
            jax.ShapeDtypeStruct((512, 1024), F32),
            jax.ShapeDtypeStruct((512, 1024), F32),
            jax.ShapeDtypeStruct((4, 1152, 128), BF16),
            jax.ShapeDtypeStruct((4, 144, 1024), BF16),
            jax.ShapeDtypeStruct((4, 144, 1024), BF16),
            jax.ShapeDtypeStruct((2, 192, 1024), BF16),
            jax.ShapeDtypeStruct((2, 512, 128), BF16),
            jax.ShapeDtypeStruct((2, 72, 128), F32),
        ),
        in_specs=[hbm] * 10,
        out_specs=[hbm] * 8,
        scratch_shapes=[
            big(1536, 1024), big(576, 1024), big(1152, 1024), big(1152, 1024), big(1152, 1024),
            big(2, 544, 1024), big(2048, 1024), big(2048, 1024), big(1536, 1024), big(512, 1024),
            big(1152, 2048), big(1152, 2048), big(1152, 2048), big(1152, 1024),
            big(2, 7, 576, 128), big(2, 7, 144, 512), big(2, 7, 144, 512),
            big(3, 512, 1024), big(2, 512, 1024), big(512, 1024),
            big(512, 1024, dtype=F32), big(512, 1024, dtype=F32),
            big(8, 1024, dtype=F32), big(2, 16, 256, dtype=F32),
            big(2, 8, 256, dtype=F32), big(32, 1024), big(512, 128),
            big(512, 128, dtype=F32), big(512, 128), big(512, 128),
            big(512, 128, dtype=F32), big(8, 1024, dtype=F32), big(512, 128),
            big(8, 72, 128, dtype=F32), big(3, 72, 128, dtype=F32),
            dma((24,)), dma((5, 2, 4, 2)), dma((5, 2, 4, 2)), dma((6, 2, 7)), dma((6, 2, 7)),
            dma((7,)), dma((7,)), dma, dma, dma, dma, dma((3,)), dma((3,)),
            dma((2, 3)), dma((2, 3)), dma((2, 3)), dma((2, 3)),
            dma((4, 3, 2)), dma((4, 3, 2)), dma((2,)), dma((2,)), dma, dma,
            dma((3, 2, 4)), dma((3, 2, 3)), dma((3, 2)), dma((3, 2)),
            dma((3, 2)), dma((3, 2)), dma((7,)), dma((7,)), dma((2,)), dma((2,)), dma((9,)),
            regular, regular, regular,
        ],
        compiler_params=pltpu.CompilerParams(
            collective_id=0, has_side_effects=True, vmem_limit_bytes=VMEM_BYTES
        ),
        name="layer",
    )(
        layer_in.reshape(512, width), cotangent.reshape(512, width),
        own_in, w_out.reshape(8, 2, 64, 128), tap_cols, own_gate, own_up,
        w_down.reshape(8, 4, 144, 128), gains, ids,
    )
    lo, gi, od, og, ou, oi, oo, small = outs
    back = lambda a: a.astype(F32)
    grad_in = back(oi).reshape(2, 3, 64, width).transpose(3, 1, 0, 2).reshape(width, 384)
    grad_out = back(oo).reshape(2, 8, 64, 128).transpose(1, 0, 2, 3).reshape(width, 128)
    grad_gate = back(og).reshape(576, width).T
    grad_up = back(ou).reshape(576, width).T
    grad_down = back(od).reshape(4, 8, 144, 128).transpose(1, 0, 2, 3).reshape(4608, 128)
    grad_taps = small[:, 0:64, 0:3].reshape(128, 3).T
    return (
        lo.reshape(2, 256, width), gi.reshape(2, 256, width),
        grad_in, grad_out, grad_gate, grad_up, grad_down, grad_taps,
        small[0, 64] + small[1, 64], small[0, 65] + small[1, 65],
    )


def solution(mesh):
    grouped = mesh.shape["rep"] == 4 and mesh.shape["fsdp"] == 8
    return jax.shard_map(
        grouped_device if grouped else per_device,
        mesh=mesh,
        in_specs=(
            P(None, ("rep", "fsdp"), None),
            P(None, ("rep", "fsdp")),
            P(None, "fsdp"),
            P(None, "fsdp"),
            P(None, "fsdp"),
            P(None, "fsdp"),
            P(None, "fsdp"),
            P(None, "fsdp"),
            P("fsdp"),
            P("fsdp"),
            P(None, ("rep", "fsdp"), None),
        ),
        out_specs=(
            P(None, ("rep", "fsdp"), None),
            P(None, ("rep", "fsdp"), None),
            P(None, "fsdp"),
            P(None, "fsdp"),
            P(None, "fsdp"),
            P(None, "fsdp"),
            P(None, "fsdp"),
            P(None, "fsdp"),
            P("fsdp"),
            P("fsdp"),
        ),
        check_vma=False,
    )
```

```python
import jax
import jax.numpy as jnp
from jax import lax
from jax.experimental import pallas as pl
from jax.experimental.pallas import tpu as pltpu
from jax.sharding import PartitionSpec as P

epsilon = 1e-05
VMEM_BYTES = 65000 << 10


def shifted(block, axis, distance):
    devices = range(lax.axis_size(axis))
    route = [(i - distance, i) for i in devices if i - distance in devices]
    return lax.ppermute(block, axis, route)


def rms_scale(values):
    return lax.rsqrt(jnp.mean(values * values, axis=-1, keepdims=True) + epsilon)


def matmul(left_side, right_side):
    return jnp.dot(left_side, right_side, preferred_element_type=jnp.float32)


def contract_rows(left_side, right_side):
    return lax.dot_general(
        left_side, right_side, (((0,), (0,)), ((), ())), preferred_element_type=jnp.float32
    )


def against_rows(left_side, right_side):
    return lax.dot_general(
        left_side, right_side, (((1,), (1,)), ((), ())), preferred_element_type=jnp.float32
    )


def forward_pass(layer_rows, doc_rows, weights):
    w_in, w_out, w_gate, w_up, w_down, conv_taps, gain_one, gain_two = weights
    residual = layer_rows.astype(jnp.float32)
    model_width = residual.shape[1]
    seq_rows = residual.shape[0]
    tap_values = conv_taps.astype(jnp.float32)
    scale_one = rms_scale(residual)
    normed_one = (residual * scale_one * gain_one.astype(jnp.float32)).astype(jnp.bfloat16)
    projected = matmul(normed_one, w_in)
    b_part = projected[:, :model_width]
    c_part = projected[:, model_width : 2 * model_width]
    x_part = projected[:, 2 * model_width :]
    product_bx = b_part * x_part
    doc_float = doc_rows.astype(jnp.float32)
    rim_values, rim_ids = shifted((product_bx[-2:], doc_float[-2:]), "fsdp", 1)
    extended = jnp.concatenate([rim_values, product_bx], 0)
    extended_ids = jnp.concatenate([rim_ids, doc_float], 0)
    conv_out = tap_values[0] * product_bx
    doc_masks = []
    for offset in (1, 2):
        matching = (extended_ids[2 - offset : 2 - offset + seq_rows] == doc_float).astype(
            jnp.float32
        )[:, None]
        doc_masks.append(matching)
        conv_out = (
            conv_out + tap_values[offset] * matching * extended[2 - offset : 2 - offset + seq_rows]
        )
    gated_rows = (c_part * conv_out).astype(jnp.bfloat16)
    middle = residual + matmul(gated_rows, w_out)
    scale_two = rms_scale(middle)
    normed_two = (middle * scale_two * gain_two.astype(jnp.float32)).astype(jnp.bfloat16)
    gate_pre = matmul(normed_two, w_gate)
    up_pre = matmul(normed_two, w_up)
    hidden = (jax.nn.silu(gate_pre) * up_pre).astype(jnp.bfloat16)
    output = middle + matmul(hidden, w_down)
    saved_state = (
        residual,
        scale_one,
        normed_one,
        projected,
        extended,
        doc_masks,
        conv_out,
        gated_rows,
        middle,
        scale_two,
        normed_two,
        gate_pre,
        up_pre,
        hidden,
    )
    return (output, saved_state)


def backward_pass(cotan_rows, weights, saved_state):
    w_in, w_out, w_gate, w_up, w_down, conv_taps, gain_one, gain_two = weights
    (
        residual,
        scale_one,
        normed_one,
        projected,
        extended,
        doc_masks,
        conv_out,
        gated_rows,
        middle,
        scale_two,
        normed_two,
        gate_pre,
        up_pre,
        hidden,
    ) = saved_state
    model_width = residual.shape[1]
    seq_rows = residual.shape[0]
    tap_values = conv_taps.astype(jnp.float32)
    b_part = projected[:, :model_width]
    c_part = projected[:, model_width : 2 * model_width]
    x_part = projected[:, 2 * model_width :]
    grad_out = cotan_rows.astype(jnp.float32)
    grad_down = contract_rows(hidden, cotan_rows)
    grad_hidden = against_rows(cotan_rows, w_down)
    gate_prob = jax.nn.sigmoid(gate_pre)
    grad_gate = (grad_hidden * up_pre * gate_prob * (1.0 + gate_pre * (1.0 - gate_prob))).astype(
        jnp.bfloat16
    )
    grad_up = (grad_hidden * gate_pre * gate_prob).astype(jnp.bfloat16)
    grad_wgate = contract_rows(normed_two, grad_gate)
    grad_wup = contract_rows(normed_two, grad_up)
    grad_normed_two = against_rows(grad_gate, w_gate) + against_rows(grad_up, w_up)
    grad_gtwo = jnp.sum(grad_normed_two * middle * scale_two, axis=0)
    weighted = grad_normed_two * gain_two.astype(jnp.float32)
    grad_middle = (
        grad_out
        + scale_two * weighted
        - middle * scale_two**3 * jnp.mean(weighted * middle, axis=-1, keepdims=True)
    )
    grad_branch = grad_middle.astype(jnp.bfloat16)
    grad_wout = contract_rows(gated_rows, grad_branch)
    grad_gated = against_rows(grad_branch, w_out)
    grad_c = grad_gated * conv_out
    grad_conv = grad_gated * c_part
    grad_ext = jnp.pad(tap_values[0] * grad_conv, ((2, 0), (0, 0)))
    tap_rows = [jnp.sum(grad_conv * extended[2:], axis=0)]
    for offset, matching in zip((1, 2), doc_masks):
        masked_grad = matching * grad_conv
        grad_ext = grad_ext + jnp.pad(
            tap_values[offset] * masked_grad, ((2 - offset, offset), (0, 0))
        )
        tap_rows.append(jnp.sum(masked_grad * extended[2 - offset : 2 - offset + seq_rows], axis=0))
    rim_back = shifted(grad_ext[:2], "fsdp", -1)
    grad_bx = grad_ext[2:] + jnp.pad(rim_back, ((seq_rows - 2, 0), (0, 0)))
    grad_taps = jnp.stack(tap_rows)
    grad_proj = jnp.concatenate([grad_bx * x_part, grad_c, grad_bx * b_part], 1).astype(
        jnp.bfloat16
    )
    grad_win = contract_rows(normed_one, grad_proj)
    grad_normed_one = against_rows(grad_proj, w_in)
    grad_gone = jnp.sum(grad_normed_one * residual * scale_one, axis=0)
    weighted_one = grad_normed_one * gain_one.astype(jnp.float32)
    grad_input = (
        grad_middle
        + scale_one * weighted_one
        - residual * scale_one**3 * jnp.mean(weighted_one * residual, axis=-1, keepdims=True)
    )
    local_grads = (
        grad_win,
        grad_wout,
        grad_wgate,
        grad_wup,
        grad_down,
        grad_taps,
        grad_gone,
        grad_gtwo,
    )
    return (grad_input, local_grads)


def per_device(
    layer_in, segments, w_in, w_out, w_gate, w_up, w_down, conv_taps, gain_one, gain_two, cotangent
):
    outputs = []
    input_grads = []
    totals = None
    owned_grads = None
    for batch_index in range(layer_in.shape[0]):
        weights_now = (
            lax.all_gather(w_in, "fsdp", axis=1, tiled=True),
            lax.all_gather(w_out, "fsdp", axis=1, tiled=True),
            lax.all_gather(w_gate, "fsdp", axis=1, tiled=True),
            lax.all_gather(w_up, "fsdp", axis=1, tiled=True),
            lax.all_gather(w_down, "fsdp", axis=1, tiled=True),
            lax.all_gather(conv_taps, "fsdp", axis=1, tiled=True),
            lax.all_gather(gain_one, "fsdp", axis=0, tiled=True),
            lax.all_gather(gain_two, "fsdp", axis=0, tiled=True),
        )
        output, saved_state = forward_pass(
            layer_in[batch_index], segments[batch_index], weights_now
        )
        outputs.append(output)
        grad_input, local_grads = backward_pass(cotangent[batch_index], weights_now, saved_state)
        input_grads.append(grad_input)
        totals = local_grads if batch_index == 0 else jax.tree.map(jnp.add, totals, local_grads)
    owned_grads = tuple(
        lax.psum_scatter(
            total.astype(jnp.bfloat16), "fsdp", scatter_dimension=total.ndim - 1, tiled=True
        )
        for total in totals
    )
    summed = (
        lax.psum(owned_grads[0].astype(jnp.bfloat16), "rep").astype(jnp.float32),
        lax.psum(owned_grads[1].astype(jnp.bfloat16), "rep").astype(jnp.float32),
        lax.psum(owned_grads[2].astype(jnp.bfloat16), "rep").astype(jnp.float32),
        lax.psum(owned_grads[3].astype(jnp.bfloat16), "rep").astype(jnp.float32),
        lax.psum(owned_grads[4].astype(jnp.bfloat16), "rep").astype(jnp.float32),
        lax.psum(owned_grads[5].astype(jnp.bfloat16), "rep").astype(jnp.float32),
        lax.psum(owned_grads[6].astype(jnp.bfloat16), "rep").astype(jnp.float32),
        lax.psum(owned_grads[7].astype(jnp.bfloat16), "rep").astype(jnp.float32),
    )
    return (
        jnp.stack(outputs),
        jnp.stack(input_grads),
        summed[0],
        summed[1],
        summed[2],
        summed[3],
        summed[4],
        summed[5],
        summed[6],
        summed[7],
    )


MESH_ID = pl.DeviceIdType.MESH
BF16 = jnp.bfloat16
F32 = jnp.float32
CW, CCW = 0, 1
OUT, GN2, DOWN, GN1 = range(4)
WIN, WO, WG, WU, WD, WIN2 = range(6)


def dot_nn(a, b):
    return lax.dot_general(a, b, (((1,), (0,)), ((), ())), preferred_element_type=F32)


def dot_nt(a, b):
    return lax.dot_general(a, b, (((1,), (1,)), ((), ())), preferred_element_type=F32)


def dot_tn(a, b):
    return lax.dot_general(a, b, (((0,), (0,)), ((), ())), preferred_element_type=F32)


def span(start, size, step):
    return pl.ds(pl.multiple_of(start, step), size)


def layer_kernel(
    li, cot_in, win_in, wo_in, taps_in, wg_in, wu_in, wd_in, gains_in, ids_in,
    o_lo, o_gi, o_d, o_g, o_u, o_i, o_o, o_s,
    win, wo, wg, wu, wd, n1, n2, cot, proj, gated, gate, up, hidden, dwd,
    slots_d, slots_g, slots_u, part, rsib, rxn, middle, gmid,
    gains, masks, ids, hal, taps, hbx, halo_out, halo_in, dtap, dgain, mix_o, small_r, small_x,
    loc_sem, side_s, side_r, ag_s, ag_r, rs_s, rs_r, gain_s, gain_r, mask_s, mask_r, n1_s, n1_r,
    rim_s, rim_r, cot_s, cot_r, n2_s, n2_r, ex_s, ex_r, gb_s, gb_r, halo_s, halo_r, fin_s, fin_r, mx_s, mx_r,
    ms_s, ms_r, sm_s, sm_r, sx_s, sx_r, out_sem, sib_credit, xn_credit, oi_ready,
):
    r = lax.axis_index("rep")
    f = lax.axis_index("fsdp")
    x = lax.div(r, 2)
    c = lax.rem(r, 2)
    oc = 1 - c
    sib = 2 * x + oc
    xn = 2 * (1 - x) + c
    far = 2 * (1 - x) + oc
    y = lax.rem(f, 2)
    z = lax.div(f, 2)
    p = z + y * (7 - 2 * z)

    def f_at(place):
        place = lax.rem(place + 16, 8)
        yy = lax.div(place, 4)
        return 2 * (place + yy * (7 - 2 * place)) + yy

    right, left = f_at(p + 1), f_at(p - 1)
    toward = (right, left)

    def remote(src, dst, send, recv, device):
        return pltpu.make_async_remote_copy(
            src_ref=src, dst_ref=dst, send_sem=send, recv_sem=recv, device_id=device,
            device_id_type=MESH_ID,
        )

    def weight_slot(k, g):
        if k == WIN:
            return win.at[span(g * 192, 192, 64), :]
        if k == WO:
            return wo.at[:, span(g * 128, 128, 128)]
        if k == WG:
            return wg.at[span(g * 144, 144, 16), :]
        if k == WU:
            return wu.at[span(g * 144, 144, 16), :]
        return wd.at[:, span(g * 128, 128, 128)]

    def weight_part(k, g, h):
        if k == WIN:
            return win.at[span(g * 192 + 64 * x, 128, 64), pl.ds(512 * h, 512)]
        if k == WO:
            return wo.at[span(192 * x + 192 * h, 192, 192), span(g * 128, 128, 128)]
        if k == WG:
            return wg.at[span(g * 144, 144, 16), pl.ds(512 * h, 512)]
        if k == WU:
            return wu.at[span(g * 144, 144, 16), pl.ds(512 * h, 512)]
        return wd.at[pl.ds(576 * h, 576), span(g * 128, 128, 128)]

    reach = {WIN: (4, 3), WO: (3, 4), WG: (3, 4), WU: (3, 4), WD: (4, 3)}

    def ag_copy(k, s, way, g, h):
        view = weight_part(k, g, h)
        return remote(
            view, view, ag_s.at[k, way, s, h], ag_r.at[k, way, s, h], (r, toward[way])
        )

    def ag_send(k, s, way, h):
        ag_copy(k, s, way, f_at(p - s) if way == CW else f_at(p + s), h).start()

    def side_copy(k, s, way, half):
        g = f_at(p - 1 - s) if way == CW else f_at(p + 1 + s)
        if k == WIN:
            view = win.at[span(g * 192 + 128 * half, 64, 64), :]
        else:
            view = wo.at[span(384 * half, 192, 192), span(g * 128, 128, 128)]
        return remote(view, view, side_s.at[k, way, s], side_r.at[k, way, s], (xn, f))

    def ag_start(k):
        for h in (0, 1):
            for way in (CW, CCW):
                ag_send(k, 0, way, h)

    def ag_event(k, s):
        for h in (0, 1):
            for way in (CW, CCW):
                if s < reach[k][way]:
                    g = f_at(p - 1 - s) if way == CW else f_at(p + 1 + s)
                    ag_copy(k, s, way, g, h).wait_recv()
                    if s + 1 < reach[k][way]:
                        ag_send(k, s + 1, way, h)
                    if h and k in (WIN, WO):
                        side_copy(k, s, way, x).start()

    def side_arrive(k):
        for way in (CW, CCW):
            for s in range(reach[k][way]):
                side_copy(k, s, way, 1 - x).wait_recv()

    def side_drain(k):
        for way in (CW, CCW):
            for s in range(reach[k][way]):
                side_copy(k, s, way, x).wait_send()

    def ag_drain(k):
        for way in (CW, CCW):
            for s in range(reach[k][way]):
                for h in (0, 1):
                    ag_copy(k, s, way, f, h).wait_send()

    def grad_piece(k, g, way):
        if k == WD:
            return dwd.at[pl.ds(576 * way, 576), span(g * 128, 128, 128)]
        if k == WG:
            return cot.at[span(g * 144, 144, 16), pl.ds(512 * way, 512)]
        if k == WU:
            return wu.at[span(g * 144, 144, 16), pl.ds(512 * way, 512)]
        if k == WO:
            return gate.at[pl.ds(512 + 256 * way, 256), span(1024 + g * 128, 128, 128)]
        return gate.at[
            span(192 * lax.rem(g, 6), 192, 64), span(1024 * lax.div(g, 6) + 512 * way + 256 * (k == WIN2), 256, 128)
        ]

    def sum_slot(k, way, s):
        if k == WD:
            return slots_d.at[way, s]
        if k == WG:
            return slots_g.at[way, s]
        if k == WU:
            return slots_u.at[way, s]
        i = way * 7 + s
        if k == WO:
            return up.at[pl.ds(768, 256), pl.ds(128 * i, 128)]
        return up.at[pl.ds(192 * (i // 4), 192), pl.ds(512 * (i % 4) + 256 * (k == WIN2), 256)]

    def rs_copy(k, way, s):
        src = sum_slot(k, way, s - 1) if s else grad_piece(
            k, f_at(p - 1) if way == CW else f_at(p + 1), way
        )
        return remote(
            src, sum_slot(k, way, s), rs_s.at[k, way, s], rs_r.at[k, way, s], (r, toward[way])
        )

    def rs_start(k):
        rs_copy(k, CW, 0).start()
        rs_copy(k, CCW, 0).start()

    def rs_event(k, s):
        for way in (CW, CCW):
            g = f_at(p - 2 - s) if way == CW else f_at(p + 2 + s)
            rs_copy(k, way, s).wait_recv()
            slot = sum_slot(k, way, s)
            slot[...] = (slot[...].astype(F32) + grad_piece(k, g, way)[...].astype(F32)).astype(BF16)
            if s < 6:
                rs_copy(k, way, s + 1).start()

    def rs_drain(k):
        for way in (CW, CCW):
            for s in range(7):
                rs_copy(k, way, s).wait_send()

    ffn_out = {WD: (0, o_d), WG: (1, o_g), WU: (2, o_u)}
    peers = (sib, xn, far)

    def final_view(k, owner, way):
        out = ffn_out[k][1]
        if k == WD:
            return out.at[owner, pl.ds(576 * way, 576), :]
        return out.at[owner, :, pl.ds(512 * way, 512)]

    def final_copy(k, way, j):
        i = ffn_out[k][0]
        src = final_view(k, xn, way) if j == 2 else sum_slot(k, way, 6)
        dst = final_view(k, xn if j == 2 else r, way)
        if j == 3:
            return pltpu.make_async_copy(src, dst, fin_s.at[i, way, 3])
        return remote(
            src, dst, fin_s.at[i, way, j], fin_r.at[i, way, j], (xn if j == 1 else sib, f)
        )

    def final_start(k):
        for way in (CW, CCW):
            for j in (1, 0, 3):
                final_copy(k, way, j).start()

    def final_arrive(k, way, j):
        i = ffn_out[k][0]
        view = final_view(k, peers[j], way)
        remote(view, view, fin_s.at[i, way, j], fin_r.at[i, way, j], (sib, f)).wait_recv()

    def final_forward(k):
        for way in (CW, CCW):
            final_arrive(k, way, 1)
            final_copy(k, way, 2).start()

    def final_drain(k):
        for way in (CW, CCW):
            final_copy(k, way, 3).wait()
            for j in range(3):
                final_copy(k, way, j).wait_send()
            final_arrive(k, way, 0)
            final_arrive(k, way, 2)

    loads = [
        pltpu.make_async_copy(win_in, weight_slot(WIN, f), loc_sem.at[0]),
        pltpu.make_async_copy(
            taps_in, wo.at[pl.ds(512, 64), span(f * 128, 128, 128)], loc_sem.at[1]
        ),
        pltpu.make_async_copy(li, part.at[0], loc_sem.at[2]),
        pltpu.make_async_copy(cot_in, cot.at[span(r * 512, 512, 512), :], loc_sem.at[3]),
        pltpu.make_async_copy(wg_in, weight_slot(WG, f), loc_sem.at[4]),
        pltpu.make_async_copy(wu_in, weight_slot(WU, f), loc_sem.at[5]),
        pltpu.make_async_copy(ids_in, ids.at[0], loc_sem.at[6]),
        pltpu.make_async_copy(gains_in, gains.at[:, span(f * 128, 128, 128)], loc_sem.at[7]),
    ]
    loads_out = [
        pltpu.make_async_copy(
            wo_in.at[g, c], wo.at[pl.ds(64 * g, 64), span(f * 128, 128, 128)], loc_sem.at[8 + g]
        )
        for g in range(8)
    ]
    loads_down = [
        pltpu.make_async_copy(
            wd_in.at[g, r], wd.at[pl.ds(144 * g, 144), span(f * 128, 128, 128)], loc_sem.at[16 + g]
        )
        for g in range(8)
    ]
    for load in loads[:2] + loads_out + loads[2:] + loads_down:
        load.start()
    barrier = pltpu.get_barrier_semaphore()
    for j in range(1, 8):
        pl.semaphore_signal(
            barrier, inc=1, device_id=(r, lax.rem(f + j, 8)), device_id_type=MESH_ID
        )
    for peer in peers:
        pl.semaphore_signal(barrier, inc=1, device_id=(peer, f), device_id_type=MESH_ID)
    dtap[...] = jnp.zeros_like(dtap)
    dgain[...] = jnp.zeros_like(dgain)
    pl.semaphore_wait(barrier, 10)

    def gain_copy(j):
        return remote(
            gains_in, gains.at[:, span(f * 128, 128, 128)], gain_s.at[j - 1], gain_r.at[j - 1],
            (r, lax.rem(f + j, 8)),
        )

    def cot_copy(m, j):
        rows = span((xn if j == 2 else r) * 512 + m * 256, 256, 256)
        return remote(
            cot.at[rows, :], cot.at[rows, :], cot_s.at[m, j], cot_r.at[m, j],
            (xn if j == 1 else sib, f),
        )

    def cot_arrive(m, j):
        rows = span((sib, xn, far)[j] * 512 + m * 256, 256, 256)
        remote(
            cot.at[rows, :], cot.at[rows, :], cot_s.at[m, j], cot_r.at[m, j], (sib, f)
        ).wait_recv()

    def n2_copy(m, j):
        rows = span((xn if j == 2 else r) * 512 + m * 256, 256, 256)
        return remote(
            n2.at[rows, :], n2.at[rows, :], n2_s.at[m, j], n2_r.at[m, j],
            (xn if j == 1 else sib, f),
        )

    def n2_arrive(m, j):
        rows = span((sib, xn, far)[j] * 512 + m * 256, 256, 256)
        remote(
            n2.at[rows, :], n2.at[rows, :], n2_s.at[m, j], n2_r.at[m, j], (sib, f)
        ).wait_recv()

    def rim_copy(j):
        if j == 2:
            src, dst = ids_in, ids.at[1]
        else:
            src, dst = li.at[pl.ds(240 + 256 * j, 16), :], hal.at[pl.ds(16 * j, 16), :]
        return remote(src, dst, rim_s.at[j], rim_r.at[j], (r, lax.rem(f + 1, 8)))

    for j in range(1, 8):
        gain_copy(j).start()
    for j in range(3):
        rim_copy(j).start()
    for load in loads[:2] + loads_out:
        load.wait()
    ag_start(WIN)
    ag_start(WO)
    loads[3].wait()
    cot_copy(0, 0).start()
    cot_copy(0, 1).start()
    loads[2].wait()
    loads[7].wait()
    for j in range(1, 8):
        gain_copy(j).wait_recv()

    gain_one = gains[0:1, :]
    gain_two = gains[1:2, :]

    def norm_rows(rows):
        rows = rows.astype(F32)
        scale = lax.rsqrt(jnp.mean(rows * rows, axis=1, keepdims=True) + epsilon)
        return (rows * scale * gain_one).astype(BF16)

    def norm_step(i, carry):
        rows = span(i * 64, 64, 64)
        n1[c, rows, :] = norm_rows(part[0, rows, :])
        return carry

    lax.fori_loop(0, 8, norm_step, 0)
    for j in range(3):
        rim_copy(j).wait_recv()
    started = jnp.where(f > 0, 1.0, 0.0).astype(F32)
    n1[c, 512:544, :] = norm_rows(hal[...].astype(F32) * started)
    n1_copy = remote(n1.at[c], n1.at[c], n1_s, n1_r, (sib, f))
    n1_copy.start()
    loads[6].wait()
    here, before = ids[0], ids[1]
    lane_ids = lax.broadcasted_iota(jnp.int32, (8, 256), 1)
    last = before[:, 255:256]
    prev = jnp.where(lane_ids == 0, last, pltpu.roll(here, 1, 1))
    masks[c, 0:8, :] = jnp.where(prev == here, 1.0, 0.0)
    prev = jnp.where(
        lane_ids == 0, before[:, 254:255], jnp.where(lane_ids == 1, last, pltpu.roll(here, 2, 1))
    )
    masks[c, 8:16, :] = jnp.where(prev == here, 1.0, 0.0)
    mask_copy = remote(masks.at[c], masks.at[c], mask_s, mask_r, (sib, f))
    mask_copy.start()

    for s in (0, 1):
        ag_event(WIN, s)
        ag_event(WO, s)
    for load in loads[4:6] + loads_down:
        load.wait()
    ag_event(WIN, 2)
    ag_event(WO, 2)
    ag_start(WG)
    cot_arrive(0, 1)
    cot_copy(0, 2).start()
    ag_event(WIN, 3)
    ag_event(WO, 3)
    ag_start(WU)
    ag_event(WG, 0)
    side_arrive(WIN)
    side_arrive(WO)

    for g in range(8):
        taps[64 * g : 64 * g + 64, :] = wo[512:576, 128 * g : 128 * g + 128]
    remote(n1.at[oc], n1.at[oc], n1_s, n1_r, (sib, f)).wait_recv()
    remote(masks.at[oc], masks.at[oc], mask_s, mask_r, (sib, f)).wait_recv()
    lane256 = lax.broadcasted_iota(jnp.int32, (64, 256), 1)

    def halo_product(qc):
        rows = n1[qc, 512:544, :]
        return dot_nt(win[0:512, :], rows) * dot_nt(win[1024:1536, :], rows)

    hbx[:, 0:32] = halo_product(0)
    hbx[:, 32:64] = halo_product(1)

    def earlier(bx, qc, rows, m):
        held = hbx[rows, 0:64]
        place = 32 * qc + 16 * m
        spot = lax.broadcasted_iota(jnp.int32, (64, 64), 1) - place
        one = jnp.sum(jnp.where(spot == 15, held, 0.0), axis=1, keepdims=True)
        two = jnp.sum(jnp.where(spot == 14, held, 0.0), axis=1, keepdims=True)
        prev_one = jnp.where(lane256 == 0, one, pltpu.roll(bx, 1, 1))
        prev_two = jnp.where(
            lane256 == 0, two, jnp.where(lane256 == 1, one, pltpu.roll(bx, 2, 1))
        )
        return prev_one, prev_two

    def tap_columns(rows):
        held = taps[rows, :].astype(F32)
        return held[:, 0:1], held[:, 1:2], held[:, 2:3]

    def mix_fwd(qc, m):
        tokens = n1[qc, 256 * m : 256 * m + 256, :]
        lanes = span(qc * 512 + m * 256, 256, 256)
        mask_one = masks[qc, m : m + 1, :]
        mask_two = masks[qc, 8 + m : 9 + m, :]
        for i in range(3):
            gmid[:, 256 * i : 256 * i + 256] = dot_nt(win[512 * i : 512 * i + 512, :], tokens)

        def step(i, carry):
            rows = span(64 * i, 64, 64)
            b, cc, xx = gmid[rows, 0:256], gmid[rows, 256:512], gmid[rows, 512:768]
            proj[rows, lanes] = b.astype(BF16)
            proj[span(512 + 64 * i, 64, 64), lanes] = cc.astype(BF16)
            proj[span(1024 + 64 * i, 64, 64), lanes] = xx.astype(BF16)
            bx = b * xx
            prev_one, prev_two = earlier(bx, qc, rows, m)
            t0, t1, t2 = tap_columns(rows)
            conv = (
                t0 * bx + t1 * (mask_one * prev_one) + t2 * (mask_two * prev_two)
            )
            gated[rows, lanes] = (cc * conv).astype(BF16)
            return carry

        lax.fori_loop(0, 8, step, 0)
        return dot_tn(gated[:, lanes], wo[0:512, :])

    def ex_copy(op, kind, m):
        rows = span(256 * m, 256, 256)
        src = part.at[{0: 1, 1: 0, 2: 2}[kind], rows, :]
        if op == DOWN and kind == 2:
            src = cot.at[span(1152 + 256 * m, 256, 128), :]
        dst = rxn.at[rows, :] if kind == 2 else rsib.at[kind, rows, :]
        return remote(
            src, dst, ex_s.at[op, kind, m], ex_r.at[op, kind, m], (xn if kind == 2 else sib, f)
        )

    for m in (0, 1):
        part[1, 256 * m : 256 * m + 256, :] = mix_fwd(oc, m).astype(BF16)
        ex_copy(OUT, 0, m).start()
        if m:
            ag_event(WU, 0)
        middle[256 * m : 256 * m + 256, :] = mix_fwd(c, m)
        if m == 0:
            ag_event(WG, 1)
        ex_copy(OUT, 0, m).wait_recv()

        def norm_two_step(i, carry):
            rows = span(256 * m + i * 64, 64, 64)
            mid = middle[rows, :] + rsib[0, rows, :].astype(F32) + part[0, rows, :].astype(F32)
            middle[rows, :] = mid
            scale = lax.rsqrt(jnp.mean(mid * mid, axis=1, keepdims=True) + epsilon)
            n2[span(r * 512 + 256 * m + i * 64, 64, 64), :] = (mid * scale * gain_two).astype(BF16)
            return carry

        lax.fori_loop(0, 4, norm_two_step, 0)
        n2_copy(m, 1).start()
        n2_copy(m, 0).start()
        if m:
            cot_copy(1, 1).start()
            cot_copy(1, 0).start()
    pl.semaphore_signal(sib_credit, inc=1, device_id=(sib, f), device_id_type=MESH_ID)
    mid_copy = pltpu.make_async_copy(middle, o_lo, out_sem.at[0])
    mid_copy.start()
    for m in (0, 1):
        ex_copy(OUT, 0, m).wait_send()
    ag_event(WG, 2)
    ag_event(WU, 1)
    ag_start(WD)
    ag_event(WG, 3)

    def gate_half(q):
        def step(i, carry):
            rows = span(lax.rem(i, 3) * 384, 384, 128)
            tokens = span(q * 512 + lax.div(i, 3) * 256, 256, 256)
            gate[rows, tokens] = dot_nt(wg[rows, :], n2[tokens, :]).astype(BF16)
            return carry

        lax.fori_loop(0, 6, step, 0)

    def up_half(q):
        def step(i, carry):
            rows = span(lax.rem(i, 3) * 384, 384, 128)
            tokens = span(q * 512 + lax.div(i, 3) * 256, 256, 256)
            u = dot_nt(wu[rows, :], n2[tokens, :])
            g = gate[rows, tokens].astype(F32)
            up[rows, tokens] = u.astype(BF16)
            hidden[rows, tokens] = (g * jax.nn.sigmoid(g) * u).astype(BF16)
            return carry

        lax.fori_loop(0, 6, step, 0)

    gate_half(r)
    ag_event(WU, 2)
    for m in (0, 1):
        n2_arrive(m, 0)
    gate_half(sib)
    for m in (0, 1):
        n2_arrive(m, 1)
        n2_copy(m, 2).start()
    ag_event(WD, 0)
    gate_half(xn)
    for m in (0, 1):
        n2_arrive(m, 2)
    gate_half(far)
    cot_arrive(1, 1)
    cot_copy(1, 2).start()
    ag_event(WU, 3)
    up_half(r)
    up_half(sib)
    ag_event(WD, 1)
    up_half(xn)
    up_half(far)
    ag_event(WD, 2)
    for m in (0, 1):
        cot_arrive(m, 0)
        cot_arrive(m, 2)

    def dwd_step(i, carry):
        rows = span(i * 384, 384, 128)
        for n in (0, 512):
            dwd[rows, n : n + 512] = dot_nn(hidden[rows, :], cot[:, n : n + 512]).astype(BF16)
        return carry

    lax.fori_loop(0, 3, dwd_step, 0)
    rs_start(WD)
    ag_event(WD, 3)

    def ring(*events):
        for k, s in events:
            rs_event(k, s)

    def grad_hidden(q):
        def step(i, carry):
            rows = span(lax.rem(i, 3) * 384, 384, 128)
            tokens = span(q * 512 + lax.div(i, 3) * 256, 256, 256)
            gh = dot_nt(wd[rows, :], cot[tokens, :])
            g = gate[rows, tokens].astype(F32)
            u = up[rows, tokens].astype(F32)
            s = jax.nn.sigmoid(g)
            gate[rows, tokens] = (gh * u * s * (1.0 + g * (1.0 - s))).astype(BF16)
            up[rows, tokens] = (gh * g * s).astype(BF16)
            return carry

        lax.fori_loop(0, 6, step, 0)

    for i, q in enumerate((r, sib, xn, far)):
        grad_hidden(q)
        if i % 2:
            ring((WD, i // 2))
    for m in (0, 1):
        for j in range(3):
            cot_copy(m, j).wait_send()
            n2_copy(m, j).wait_send()
    ag_drain(WG)
    ag_drain(WU)

    def dwg_step(i, carry):
        rows = span(i * 384, 384, 128)
        for n in (0, 512):
            cot[rows, n : n + 512] = dot_nn(gate[rows, :], n2[:, n : n + 512]).astype(BF16)
        return carry


    def gn2_part(q, m):
        tokens = span(q * 512 + m * 256, 256, 256)
        return dot_tn(gate[:, tokens], wg[...]) + dot_tn(up[:, tokens], wu[...])

    def down_part(q, m):
        return dot_tn(hidden[:, span(q * 512 + m * 256, 256, 256)], wd[...])

    def to_part(partial, q, dst, op=None, kind=None):
        def step(m, carry):
            dst(m)[...] = partial(q, m).astype(BF16)
            if op is not None:
                ex_copy(op, kind, m).start()
            return carry

        lax.fori_loop(0, 2, step, 0)

    def part_rows(slot):
        return lambda m: part.at[slot, span(256 * m, 256, 256), :]

    def core_sum(op, dst, halves=(0, 1)):
        for m in halves:
            ex_copy(op, 1, m).wait_recv()

            def add_step(i, carry):
                rows = span(256 * m + i * 64, 64, 64)
                view = dst(256 * m + i * 64)
                view[...] = (view[...].astype(F32) + rsib[1, rows, :].astype(F32)).astype(BF16)
                return carry

            lax.fori_loop(0, 4, add_step, 0)
            ex_copy(op, 2, m).start()

    lax.fori_loop(0, 3, dwg_step, 0)
    rs_start(WG)
    ring((WD, 2))
    pl.semaphore_wait(sib_credit, 1)
    for m in (0, 1):
        part[0, 256 * m : 256 * m + 256, :] = gn2_part(far, m).astype(BF16)
        ex_copy(GN2, 1, m).start()
        part[2, 256 * m : 256 * m + 256, :] = gn2_part(xn, m).astype(BF16)
        core_sum(GN2, lambda at: part.at[2, span(at, 64, 64), :], (m,))
    ring((WD, 3), (WG, 0))

    def own_step(m, carry):
        gmid[span(256 * m, 256, 256), :] = gn2_part(r, m)
        return carry

    lax.fori_loop(0, 2, own_step, 0)
    to_part(gn2_part, sib, part_rows(1))
    for m in (0, 1):
        ex_copy(GN2, 0, m).start()
    ring((WD, 4), (WG, 1))
    cot_again = pltpu.make_async_copy(
        cot_in, gate.at[pl.ds(0, 512), pl.ds(0, 1024)], loc_sem.at[3]
    )
    cot_again.start()

    def dwu_step(i, carry):
        rows = span(i * 384, 384, 128)
        for n in (0, 512):
            wu[rows, n : n + 512] = dot_nn(up[rows, :], n2[:, n : n + 512]).astype(BF16)
        return carry

    gb_copies = []

    def grad_middle(m):
        ex_copy(GN2, 0, m).wait_recv()
        ex_copy(GN2, 2, m).wait_recv()

        def grad_middle_step(i, carry):
            rows = span(256 * m + i * 64, 64, 64)
            gn = gmid[rows, :] + rsib[0, rows, :].astype(F32) + rxn[rows, :].astype(F32)
            mid = middle[rows, :]
            scale = lax.rsqrt(jnp.mean(mid * mid, axis=1, keepdims=True) + epsilon)
            dgain[1:2, :] += jnp.sum(gn * (mid * scale), axis=0, keepdims=True)
            weighted = gn * gain_two
            inner = jnp.mean(weighted * mid, axis=1, keepdims=True)
            gm = (
                gate[rows, 0:1024].astype(F32)
                + scale * weighted
                - mid * (scale * scale * scale * inner)
            )
            gmid[rows, :] = gm
            wg[span(c * 512 + 256 * m + i * 64, 64, 64), :] = gm.astype(BF16)
            return carry

        lax.fori_loop(0, 4, grad_middle_step, 0)
        rows = span(c * 512 + 256 * m, 256, 256)
        copy = remote(wg.at[rows, :], wg.at[rows, :], gb_s.at[m], gb_r.at[m], (sib, f))
        copy.start()
        gb_copies.append(copy)

    lax.fori_loop(0, 3, dwu_step, 0)
    rs_start(WU)
    pl.semaphore_signal(oi_ready, inc=1, device_id=(r, right), device_id_type=MESH_ID)
    pl.semaphore_signal(oi_ready, inc=1, device_id=(r, left), device_id_type=MESH_ID)
    cot_again.wait()
    grad_middle(0)
    ring((WD, 5), (WG, 2))
    grad_middle(1)
    pl.semaphore_signal(sib_credit, inc=1, device_id=(sib, f), device_id_type=MESH_ID)
    pl.semaphore_signal(xn_credit, inc=1, device_id=(xn, f), device_id_type=MESH_ID)
    mid_copy.wait()
    for m in (0, 1):
        rows = span(oc * 512 + 256 * m, 256, 256)
        remote(wg.at[rows, :], wg.at[rows, :], gb_s.at[m], gb_r.at[m], (sib, f)).wait_recv()

    mix_place = {WIN: 0, WIN2: 1, WO: 2}

    def mix_sum(k, way):
        if k == WO:
            return mix_o.at[pl.ds(256 * way, 256), :]
        return cot.at[pl.ds(1664, 192), pl.ds(512 * way + 256 * (k == WIN2), 256)]

    def mx_copy(k, way):
        i = mix_place[k]
        return remote(
            sum_slot(k, way, 6), mix_sum(k, way), mx_s.at[i, way], mx_r.at[i, way], (xn, f)
        )

    def mix_start(k):
        for way in (CW, CCW):
            mx_copy(k, way).start()

    def mix_view(k, owner, way):
        if k == WO:
            return o_o.at[owner, pl.ds(256 * way, 256), :]
        return o_i.at[owner, :, pl.ds(512 * way + 256 * (k == WIN2), 256)]

    def mix_copies(k, way):
        i = mix_place[k]
        dst = mix_sum(k, way)
        return (
            remote(dst, mix_view(k, c, way), ms_s.at[i, way], ms_r.at[i, way], (sib, f)),
            pltpu.make_async_copy(dst, mix_view(k, c, way), out_sem.at[3 + 2 * i + way]),
        )

    lane128 = lax.broadcasted_iota(jnp.int32, (512, 128), 1)
    rim = jnp.zeros((512, 128), F32)
    taps_one, taps_two = tap_columns(slice(None))[1:]
    for qc in (0, 1):
        for m in (0, 1):
            at = qc * 512 + m * 256
            gg = dot_nt(wo[0:512, :], wg[at : at + 16, :])
            gc = gg * proj[512:1024, at : at + 128].astype(F32)[:, 0:16]
            masked_one = masks[qc, m : m + 1, 0:16] * gc
            masked_two = masks[qc, 8 + m : 9 + m, 0:16] * gc
            first = taps_two * masked_two[:, 0:1]
            second = taps_one * masked_one[:, 0:1] + taps_two * masked_two[:, 1:2]
            b = 2 * (2 * qc + m)
            rim = jnp.where(lane128 == b, first, jnp.where(lane128 == b + 1, second, rim))
    halo_out[...] = rim.astype(BF16)
    halo_copy = remote(halo_out, halo_in, halo_s, halo_r, (r, lax.rem(f + 7, 8)))
    halo_copy.start()

    for n in (0, 512):
        gate[512:1024, 1024 + n : 1536 + n] = dot_nn(gated[...], wg[0:1024, n : n + 512]).astype(BF16)
    pl.semaphore_wait(oi_ready, 2)
    rs_start(WO)
    ring((WD, 6), (WG, 3), (WU, 0))
    halo_copy.wait_recv()
    inside = jnp.where(f < 7, 1.0, 0.0).astype(F32)
    lane_tap = lax.broadcasted_iota(jnp.int32, (64, 128), 1)

    def mix_bwd(qc, m):
        lanes = pl.ds(qc * 512 + m * 256, 256)
        tokens = wg[qc * 512 + m * 256 : qc * 512 + m * 256 + 256, :]
        mask_one = masks[qc, m : m + 1, :]
        mask_two = masks[qc, 8 + m : 9 + m, :]
        b2 = 2 * (2 * qc + m)
        middle[:, 0:256] = dot_nt(wo[0:512, :], tokens)

        def step(i, carry):
            rows = span(64 * i, 64, 64)
            c_rows, x_rows = span(512 + 64 * i, 64, 64), span(1024 + 64 * i, 64, 64)
            gg = middle[rows, 0:256]
            b = proj[rows, lanes].astype(F32)
            cc = proj[c_rows, lanes].astype(F32)
            xx = proj[x_rows, lanes].astype(F32)
            bx = b * xx
            prev_one, prev_two = earlier(bx, qc, rows, m)
            prev_one = mask_one * prev_one
            prev_two = mask_two * prev_two
            t0, t1, t2 = tap_columns(rows)
            conv = t0 * bx + t1 * prev_one + t2 * prev_two
            gc = gg * cc
            sum0 = jnp.sum(gc * bx, axis=1, keepdims=True)
            sum1 = jnp.sum(gc * prev_one, axis=1, keepdims=True)
            sum2 = jnp.sum(gc * prev_two, axis=1, keepdims=True)
            dtap[rows, :] += jnp.where(
                lane_tap == 0, sum0, jnp.where(lane_tap == 1, sum1, jnp.where(lane_tap == 2, sum2, 0.0))
            )
            back_one = jnp.where(lane256 < 255, pltpu.roll(mask_one * gc, 255, 1), 0.0)
            back_two = jnp.where(lane256 < 254, pltpu.roll(mask_two * gc, 254, 1), 0.0)
            edge = halo_in[rows, :].astype(F32) * inside
            back = jnp.where(
                lane256 == 254, edge[:, b2 : b2 + 1],
                jnp.where(lane256 == 255, edge[:, b2 + 1 : b2 + 2], 0.0),
            )
            gbx = t0 * gc + t1 * back_one + t2 * back_two + back
            proj[rows, lanes] = (gbx * xx).astype(BF16)
            proj[c_rows, lanes] = (gg * conv).astype(BF16)
            proj[x_rows, lanes] = (gbx * b).astype(BF16)
            return carry

        lax.fori_loop(0, 8, step, 0)

    for qc in (0, 1):
        for m in (0, 1):
            mix_bwd(qc, m)
        if qc == 0:
            ring((WG, 4), (WU, 1), (WO, 0))
    ring((WG, 5), (WU, 2), (WO, 1))

    def dwin(t, n):
        rows = span(384 * t, 384, 128)
        return (
            dot_nn(proj[rows, 0:512], n1[0, 0:512, n : n + 512])
            + dot_nn(proj[rows, 512:1024], n1[1, 0:512, n : n + 512])
        ).astype(BF16)

    def dwin_step(t, carry):
        for n in (0, 512):
            gate[span(384 * t, 384, 128), n : n + 512] = dwin(t, n)
        return carry

    lax.fori_loop(0, 3, dwin_step, 0)
    for n in (0, 512):
        gate[0:384, 1024 + n : 1536 + n] = dwin(3, n)
    rs_start(WIN)
    rs_start(WIN2)

    for m in (0, 1):
        ex_copy(GN2, 0, m).wait_send()
        ex_copy(GN2, 1, m).wait_send()
        ex_copy(GN2, 2, m).wait_send()
    pl.semaphore_wait(sib_credit, 1)
    to_part(down_part, far, part_rows(0), DOWN, 1)
    to_part(down_part, xn, lambda m: cot.at[span(1152 + 256 * m, 256, 128), :])
    pl.semaphore_wait(xn_credit, 1)
    core_sum(DOWN, lambda at: cot.at[span(1152 + at, 64, 64), :])
    pl.semaphore_signal(sib_credit, inc=1, device_id=(sib, f), device_id_type=MESH_ID)
    ring((WG, 6), (WU, 3), (WO, 2), (WIN, 0), (WIN2, 0))
    final_start(WD)
    final_start(WG)
    to_part(down_part, sib, part_rows(1), DOWN, 0)

    def gn1_part(qc, m):
        return dot_tn(proj[:, span(qc * 512 + m * 256, 256, 256)], win[...])

    pl.semaphore_wait(sib_credit, 1)
    for m in (0, 1):
        ex_copy(DOWN, 0, m).wait_send()
        ex_copy(DOWN, 1, m).wait_send()
    li_again = pltpu.make_async_copy(li, part.at[1], loc_sem.at[2])
    li_again.start()
    to_part(gn1_part, oc, part_rows(0), GN1, 1)
    ring((WU, 4), (WO, 3), (WIN, 1), (WIN2, 1))
    for m in (0, 1):
        middle[256 * m : 256 * m + 256, :] = gn1_part(c, m)
    ring((WU, 5), (WO, 4), (WIN, 2), (WIN2, 2))
    li_again.wait()
    for m in (0, 1):
        ex_copy(GN1, 1, m).wait_recv()

        def grad_in_step(i, carry):
            rows = span(256 * m + i * 64, 64, 64)
            gn = middle[rows, :] + rsib[1, rows, :].astype(F32)
            res = part[1, rows, :].astype(F32)
            scale = lax.rsqrt(jnp.mean(res * res, axis=1, keepdims=True) + epsilon)
            dgain[0:1, :] += jnp.sum(gn * (res * scale), axis=0, keepdims=True)
            weighted = gn * gain_one
            inner = jnp.mean(weighted * res, axis=1, keepdims=True)
            middle[rows, :] = gmid[rows, :] + scale * weighted - res * (scale * scale * scale * inner)
            return carry

        lax.fori_loop(0, 4, grad_in_step, 0)
    gi_copy = pltpu.make_async_copy(middle, o_gi, out_sem.at[1])
    gi_copy.start()
    for m in (0, 1):
        ex_copy(GN1, 1, m).wait_send()

    for g in range(8):
        gmid[0:64, 128 * g : 128 * g + 128] = dtap[64 * g : 64 * g + 64, :]
        gmid[64:72, 128 * g : 128 * g + 128] = dgain[:, 128 * g : 128 * g + 128]

    def small_p(g):
        return gmid.at[pl.ds(0, 72), span(g * 128, 128, 128)]

    def small_copy(j):
        g = lax.rem(f + j, 8)
        return remote(small_p(g), small_r.at[j], sm_s.at[j - 1], sm_r.at[j - 1], (r, g))

    for j in range(1, 8):
        small_copy(j).start()
    ring((WU, 6), (WO, 5), (WIN, 3), (WIN2, 3))
    final_start(WU)
    total = small_p(f)[...]
    for j in range(1, 8):
        small_copy(j).wait_recv()
        total = total + small_r[j]
    small_x[0] = total
    sx_copy = remote(small_x.at[0], small_x.at[1], sx_s.at[0], sx_r.at[0], (xn, f))
    sx_copy.start()
    gi_copy.wait()
    mid_again = pltpu.make_async_copy(o_lo, middle, out_sem.at[0])
    mid_again.start()
    ring((WO, 6), (WIN, 4), (WIN2, 4))
    final_forward(WD)
    sx_copy.wait_recv()
    small_x[2] = small_x[0] + small_x[1]
    ss_copy = remote(small_x.at[2], o_s.at[c], sx_s.at[1], sx_r.at[1], (sib, f))
    ss_copy.start()
    so_copy = pltpu.make_async_copy(small_x.at[2], o_s.at[c], out_sem.at[2])
    so_copy.start()
    for way in (CW, CCW):
        mx_copy(WO, way).start()

    mid_again.wait()
    for m in (0, 1):
        ex_copy(DOWN, 0, m).wait_recv()
        ex_copy(DOWN, 2, m).wait_recv()
        middle[256 * m : 256 * m + 256, :] += down_part(r, m)

        def out_step(i, carry):
            rows = span(256 * m + i * 64, 64, 64)
            middle[rows, :] += rsib[0, rows, :].astype(F32) + rxn[rows, :].astype(F32)
            return carry

        lax.fori_loop(0, 4, out_step, 0)
        if m == 0:
            ring((WIN, 5), (WIN2, 5))
    lo_copy = pltpu.make_async_copy(middle, o_lo, out_sem.at[0])
    lo_copy.start()
    final_forward(WG)
    ring((WIN, 6))
    mix_start(WIN)
    ring((WIN2, 6))
    mix_start(WIN2)
    final_forward(WU)

    for k in (WO, WIN, WIN2):
        for way in (CW, CCW):
            mx_copy(k, way).wait_recv()
            dst = mix_sum(k, way)
            dst[...] = (dst[...].astype(F32) + sum_slot(k, way, 6)[...].astype(F32)).astype(BF16)
            for out in mix_copies(k, way):
                out.start()

    for k in (WIN, WO, WD):
        ag_drain(k)
    for k in (WIN, WO):
        side_drain(k)
    for k in range(6):
        rs_drain(k)
    for k in (WD, WG, WU):
        final_drain(k)
    for j in range(1, 8):
        gain_copy(j).wait_send()
        small_copy(j).wait_send()
    mask_copy.wait_send()
    for j in range(3):
        rim_copy(j).wait_send()
    n1_copy.wait_send()
    for m in (0, 1):
        gb_copies[m].wait_send()
    halo_copy.wait_send()
    lo_copy.wait()
    so_copy.wait()
    for m in (0, 1):
        ex_copy(DOWN, 2, m).wait_send()
    sx_copy.wait_send()
    ss_copy.wait_send()
    other = o_s.at[oc]
    remote(other, other, sx_s.at[1], sx_r.at[1], (sib, f)).wait_recv()
    for k in (WO, WIN, WIN2):
        i = mix_place[k]
        for way in (CW, CCW):
            mx_copy(k, way).wait_send()
            out, local = mix_copies(k, way)
            out.wait_send()
            local.wait()
            view = mix_view(k, oc, way)
            remote(view, view, ms_s.at[i, way], ms_r.at[i, way], (sib, f)).wait_recv()


def grouped_device(
    layer_in, segments, w_in, w_out, w_gate, w_up, w_down, conv_taps, gain_one, gain_two, cotangent
):
    r = lax.axis_index("rep")
    c = lax.rem(r, 2)
    width = layer_in.shape[2]

    def pick(array, axis, index):
        return lax.dynamic_index_in_dim(array, index, axis, keepdims=False)

    ids = jnp.pad(segments.astype(F32), ((0, 6), (0, 0)))
    own_in = pick(w_in.reshape(width, 3, 2, 64), 2, c).reshape(width, 192).T
    tap_half = pick(conv_taps.reshape(3, 2, 64), 1, c)
    tap_cols = jnp.pad(tap_half.T, ((0, 0), (0, 125)))
    own_gate = pick(w_gate.reshape(width, 4, 144), 1, r).T
    own_up = pick(w_up.reshape(width, 4, 144), 1, r).T
    gains = jnp.pad(jnp.stack([gain_one, gain_two]).astype(F32), ((0, 6), (0, 0)))

    hbm = pl.BlockSpec(memory_space=pl.ANY)
    dma = pltpu.SemaphoreType.DMA
    regular = pltpu.SemaphoreType.REGULAR

    def big(*shape, dtype=BF16):
        return pltpu.VMEM(shape, dtype)

    outs = pl.pallas_call(
        layer_kernel,
        out_shape=(
            jax.ShapeDtypeStruct((512, 1024), F32),
            jax.ShapeDtypeStruct((512, 1024), F32),
            jax.ShapeDtypeStruct((4, 1152, 128), BF16),
            jax.ShapeDtypeStruct((4, 144, 1024), BF16),
            jax.ShapeDtypeStruct((4, 144, 1024), BF16),
            jax.ShapeDtypeStruct((2, 192, 1024), BF16),
            jax.ShapeDtypeStruct((2, 512, 128), BF16),
            jax.ShapeDtypeStruct((2, 72, 128), F32),
        ),
        in_specs=[hbm] * 10,
        out_specs=[hbm] * 8,
        scratch_shapes=[
            big(1536, 1024), big(576, 1024), big(1152, 1024), big(1152, 1024), big(1152, 1024),
            big(2, 544, 1024), big(2048, 1024), big(2048, 1024), big(1536, 1024), big(512, 1024),
            big(1152, 2048), big(1152, 2048), big(1152, 2048), big(1152, 1024),
            big(2, 7, 576, 128), big(2, 7, 144, 512), big(2, 7, 144, 512),
            big(3, 512, 1024), big(2, 512, 1024), big(512, 1024),
            big(512, 1024, dtype=F32), big(512, 1024, dtype=F32),
            big(8, 1024, dtype=F32), big(2, 16, 256, dtype=F32),
            big(2, 8, 256, dtype=F32), big(32, 1024), big(512, 128),
            big(512, 128, dtype=F32), big(512, 128), big(512, 128),
            big(512, 128, dtype=F32), big(8, 1024, dtype=F32), big(512, 128),
            big(8, 72, 128, dtype=F32), big(3, 72, 128, dtype=F32),
            dma((24,)), dma((2, 2, 4)), dma((2, 2, 4)), dma((5, 2, 4, 2)), dma((5, 2, 4, 2)), dma((6, 2, 7)), dma((6, 2, 7)),
            dma((7,)), dma((7,)), dma, dma, dma, dma, dma((3,)), dma((3,)),
            dma((2, 3)), dma((2, 3)), dma((2, 3)), dma((2, 3)),
            dma((4, 3, 2)), dma((4, 3, 2)), dma((2,)), dma((2,)), dma, dma,
            dma((3, 2, 4)), dma((3, 2, 3)), dma((3, 2)), dma((3, 2)),
            dma((3, 2)), dma((3, 2)), dma((7,)), dma((7,)), dma((2,)), dma((2,)), dma((9,)),
            regular, regular, regular,
        ],
        compiler_params=pltpu.CompilerParams(
            collective_id=0, has_side_effects=True, vmem_limit_bytes=VMEM_BYTES
        ),
        name="layer",
    )(
        layer_in.reshape(512, width), cotangent.reshape(512, width),
        own_in, w_out.reshape(8, 2, 64, 128), tap_cols, own_gate, own_up,
        w_down.reshape(8, 4, 144, 128), gains, ids,
    )
    lo, gi, od, og, ou, oi, oo, small = outs
    back = lambda a: a.astype(F32)
    grad_in = back(oi).reshape(2, 3, 64, width).transpose(3, 1, 0, 2).reshape(width, 384)
    grad_out = back(oo).reshape(2, 8, 64, 128).transpose(1, 0, 2, 3).reshape(width, 128)
    grad_gate = back(og).reshape(576, width).T
    grad_up = back(ou).reshape(576, width).T
    grad_down = back(od).reshape(4, 8, 144, 128).transpose(1, 0, 2, 3).reshape(4608, 128)
    grad_taps = small[:, 0:64, 0:3].reshape(128, 3).T
    return (
        lo.reshape(2, 256, width), gi.reshape(2, 256, width),
        grad_in, grad_out, grad_gate, grad_up, grad_down, grad_taps,
        small[0, 64] + small[1, 64], small[0, 65] + small[1, 65],
    )


def solution(mesh):
    grouped = mesh.shape["rep"] == 4 and mesh.shape["fsdp"] == 8
    return jax.shard_map(
        grouped_device if grouped else per_device,
        mesh=mesh,
        in_specs=(
            P(None, ("rep", "fsdp"), None),
            P(None, ("rep", "fsdp")),
            P(None, "fsdp"),
            P(None, "fsdp"),
            P(None, "fsdp"),
            P(None, "fsdp"),
            P(None, "fsdp"),
            P(None, "fsdp"),
            P("fsdp"),
            P("fsdp"),
            P(None, ("rep", "fsdp"), None),
        ),
        out_specs=(
            P(None, ("rep", "fsdp"), None),
            P(None, ("rep", "fsdp"), None),
            P(None, "fsdp"),
            P(None, "fsdp"),
            P(None, "fsdp"),
            P(None, "fsdp"),
            P(None, "fsdp"),
            P(None, "fsdp"),
            P("fsdp"),
            P("fsdp"),
        ),
        check_vma=False,
    )
```

```python
import jax
import jax.numpy as jnp
from jax import lax
from jax.experimental import pallas as pl
from jax.experimental.pallas import tpu as pltpu
from jax.sharding import PartitionSpec as P

epsilon = 1e-05
VMEM_BYTES = 65000 << 10


def shifted(block, axis, distance):
    devices = range(lax.axis_size(axis))
    route = [(i - distance, i) for i in devices if i - distance in devices]
    return lax.ppermute(block, axis, route)


def rms_scale(values):
    return lax.rsqrt(jnp.mean(values * values, axis=-1, keepdims=True) + epsilon)


def matmul(left_side, right_side):
    return jnp.dot(left_side, right_side, preferred_element_type=jnp.float32)


def contract_rows(left_side, right_side):
    return lax.dot_general(
        left_side, right_side, (((0,), (0,)), ((), ())), preferred_element_type=jnp.float32
    )


def against_rows(left_side, right_side):
    return lax.dot_general(
        left_side, right_side, (((1,), (1,)), ((), ())), preferred_element_type=jnp.float32
    )


def forward_pass(layer_rows, doc_rows, weights):
    w_in, w_out, w_gate, w_up, w_down, conv_taps, gain_one, gain_two = weights
    residual = layer_rows.astype(jnp.float32)
    model_width = residual.shape[1]
    seq_rows = residual.shape[0]
    tap_values = conv_taps.astype(jnp.float32)
    scale_one = rms_scale(residual)
    normed_one = (residual * scale_one * gain_one.astype(jnp.float32)).astype(jnp.bfloat16)
    projected = matmul(normed_one, w_in)
    b_part = projected[:, :model_width]
    c_part = projected[:, model_width : 2 * model_width]
    x_part = projected[:, 2 * model_width :]
    product_bx = b_part * x_part
    doc_float = doc_rows.astype(jnp.float32)
    rim_values, rim_ids = shifted((product_bx[-2:], doc_float[-2:]), "fsdp", 1)
    extended = jnp.concatenate([rim_values, product_bx], 0)
    extended_ids = jnp.concatenate([rim_ids, doc_float], 0)
    conv_out = tap_values[0] * product_bx
    doc_masks = []
    for offset in (1, 2):
        matching = (extended_ids[2 - offset : 2 - offset + seq_rows] == doc_float).astype(
            jnp.float32
        )[:, None]
        doc_masks.append(matching)
        conv_out = (
            conv_out + tap_values[offset] * matching * extended[2 - offset : 2 - offset + seq_rows]
        )
    gated_rows = (c_part * conv_out).astype(jnp.bfloat16)
    middle = residual + matmul(gated_rows, w_out)
    scale_two = rms_scale(middle)
    normed_two = (middle * scale_two * gain_two.astype(jnp.float32)).astype(jnp.bfloat16)
    gate_pre = matmul(normed_two, w_gate)
    up_pre = matmul(normed_two, w_up)
    hidden = (jax.nn.silu(gate_pre) * up_pre).astype(jnp.bfloat16)
    output = middle + matmul(hidden, w_down)
    saved_state = (
        residual,
        scale_one,
        normed_one,
        projected,
        extended,
        doc_masks,
        conv_out,
        gated_rows,
        middle,
        scale_two,
        normed_two,
        gate_pre,
        up_pre,
        hidden,
    )
    return (output, saved_state)


def backward_pass(cotan_rows, weights, saved_state):
    w_in, w_out, w_gate, w_up, w_down, conv_taps, gain_one, gain_two = weights
    (
        residual,
        scale_one,
        normed_one,
        projected,
        extended,
        doc_masks,
        conv_out,
        gated_rows,
        middle,
        scale_two,
        normed_two,
        gate_pre,
        up_pre,
        hidden,
    ) = saved_state
    model_width = residual.shape[1]
    seq_rows = residual.shape[0]
    tap_values = conv_taps.astype(jnp.float32)
    b_part = projected[:, :model_width]
    c_part = projected[:, model_width : 2 * model_width]
    x_part = projected[:, 2 * model_width :]
    grad_out = cotan_rows.astype(jnp.float32)
    grad_down = contract_rows(hidden, cotan_rows)
    grad_hidden = against_rows(cotan_rows, w_down)
    gate_prob = jax.nn.sigmoid(gate_pre)
    grad_gate = (grad_hidden * up_pre * gate_prob * (1.0 + gate_pre * (1.0 - gate_prob))).astype(
        jnp.bfloat16
    )
    grad_up = (grad_hidden * gate_pre * gate_prob).astype(jnp.bfloat16)
    grad_wgate = contract_rows(normed_two, grad_gate)
    grad_wup = contract_rows(normed_two, grad_up)
    grad_normed_two = against_rows(grad_gate, w_gate) + against_rows(grad_up, w_up)
    grad_gtwo = jnp.sum(grad_normed_two * middle * scale_two, axis=0)
    weighted = grad_normed_two * gain_two.astype(jnp.float32)
    grad_middle = (
        grad_out
        + scale_two * weighted
        - middle * scale_two**3 * jnp.mean(weighted * middle, axis=-1, keepdims=True)
    )
    grad_branch = grad_middle.astype(jnp.bfloat16)
    grad_wout = contract_rows(gated_rows, grad_branch)
    grad_gated = against_rows(grad_branch, w_out)
    grad_c = grad_gated * conv_out
    grad_conv = grad_gated * c_part
    grad_ext = jnp.pad(tap_values[0] * grad_conv, ((2, 0), (0, 0)))
    tap_rows = [jnp.sum(grad_conv * extended[2:], axis=0)]
    for offset, matching in zip((1, 2), doc_masks):
        masked_grad = matching * grad_conv
        grad_ext = grad_ext + jnp.pad(
            tap_values[offset] * masked_grad, ((2 - offset, offset), (0, 0))
        )
        tap_rows.append(jnp.sum(masked_grad * extended[2 - offset : 2 - offset + seq_rows], axis=0))
    rim_back = shifted(grad_ext[:2], "fsdp", -1)
    grad_bx = grad_ext[2:] + jnp.pad(rim_back, ((seq_rows - 2, 0), (0, 0)))
    grad_taps = jnp.stack(tap_rows)
    grad_proj = jnp.concatenate([grad_bx * x_part, grad_c, grad_bx * b_part], 1).astype(
        jnp.bfloat16
    )
    grad_win = contract_rows(normed_one, grad_proj)
    grad_normed_one = against_rows(grad_proj, w_in)
    grad_gone = jnp.sum(grad_normed_one * residual * scale_one, axis=0)
    weighted_one = grad_normed_one * gain_one.astype(jnp.float32)
    grad_input = (
        grad_middle
        + scale_one * weighted_one
        - residual * scale_one**3 * jnp.mean(weighted_one * residual, axis=-1, keepdims=True)
    )
    local_grads = (
        grad_win,
        grad_wout,
        grad_wgate,
        grad_wup,
        grad_down,
        grad_taps,
        grad_gone,
        grad_gtwo,
    )
    return (grad_input, local_grads)


def per_device(
    layer_in, segments, w_in, w_out, w_gate, w_up, w_down, conv_taps, gain_one, gain_two, cotangent
):
    outputs = []
    input_grads = []
    totals = None
    owned_grads = None
    for batch_index in range(layer_in.shape[0]):
        weights_now = (
            lax.all_gather(w_in, "fsdp", axis=1, tiled=True),
            lax.all_gather(w_out, "fsdp", axis=1, tiled=True),
            lax.all_gather(w_gate, "fsdp", axis=1, tiled=True),
            lax.all_gather(w_up, "fsdp", axis=1, tiled=True),
            lax.all_gather(w_down, "fsdp", axis=1, tiled=True),
            lax.all_gather(conv_taps, "fsdp", axis=1, tiled=True),
            lax.all_gather(gain_one, "fsdp", axis=0, tiled=True),
            lax.all_gather(gain_two, "fsdp", axis=0, tiled=True),
        )
        output, saved_state = forward_pass(
            layer_in[batch_index], segments[batch_index], weights_now
        )
        outputs.append(output)
        grad_input, local_grads = backward_pass(cotangent[batch_index], weights_now, saved_state)
        input_grads.append(grad_input)
        totals = local_grads if batch_index == 0 else jax.tree.map(jnp.add, totals, local_grads)
    owned_grads = tuple(
        lax.psum_scatter(
            total.astype(jnp.bfloat16), "fsdp", scatter_dimension=total.ndim - 1, tiled=True
        )
        for total in totals
    )
    summed = (
        lax.psum(owned_grads[0].astype(jnp.bfloat16), "rep").astype(jnp.float32),
        lax.psum(owned_grads[1].astype(jnp.bfloat16), "rep").astype(jnp.float32),
        lax.psum(owned_grads[2].astype(jnp.bfloat16), "rep").astype(jnp.float32),
        lax.psum(owned_grads[3].astype(jnp.bfloat16), "rep").astype(jnp.float32),
        lax.psum(owned_grads[4].astype(jnp.bfloat16), "rep").astype(jnp.float32),
        lax.psum(owned_grads[5].astype(jnp.bfloat16), "rep").astype(jnp.float32),
        lax.psum(owned_grads[6].astype(jnp.bfloat16), "rep").astype(jnp.float32),
        lax.psum(owned_grads[7].astype(jnp.bfloat16), "rep").astype(jnp.float32),
    )
    return (
        jnp.stack(outputs),
        jnp.stack(input_grads),
        summed[0],
        summed[1],
        summed[2],
        summed[3],
        summed[4],
        summed[5],
        summed[6],
        summed[7],
    )


MESH_ID = pl.DeviceIdType.MESH
BF16 = jnp.bfloat16
F32 = jnp.float32
CW, CCW = 0, 1
OUT, GN2, DOWN, GN1 = range(4)
WIN, WO, WG, WU, WD, WIN2 = range(6)


def dot_nn(a, b):
    return lax.dot_general(a, b, (((1,), (0,)), ((), ())), preferred_element_type=F32)


def dot_nt(a, b):
    return lax.dot_general(a, b, (((1,), (1,)), ((), ())), preferred_element_type=F32)


def dot_tn(a, b):
    return lax.dot_general(a, b, (((0,), (0,)), ((), ())), preferred_element_type=F32)


def span(start, size, step):
    return pl.ds(pl.multiple_of(start, step), size)


def layer_kernel(
    li, cot_in, win_in, wo_in, taps_in, wg_in, wu_in, wd_in, gains_in, ids_in,
    o_lo, o_gi, o_d, o_g, o_u, o_i, o_o, o_s,
    win, wo, wg, wu, wd, n1, n2, cot, proj, gated, gate, up, hidden, dwd,
    slots_d, slots_g, slots_u, part, rsib, rxn, middle, gmid,
    gains, masks, ids, hal, taps, hbx, halo_out, halo_in, dtap, dgain, mix_o, small_r, small_x,
    loc_sem, side_s, side_r, ag_s, ag_r, rs_s, rs_r, gain_s, gain_r, mask_s, mask_r, n1_s, n1_r,
    rim_s, rim_r, cot_s, cot_r, n2_s, n2_r, ex_s, ex_r, gb_s, gb_r, halo_s, halo_r, fin_s, fin_r, mx_s, mx_r,
    ms_s, ms_r, sm_s, sm_r, sx_s, sx_r, out_sem, sib_credit, xn_credit, oi_ready,
):
    r = lax.axis_index("rep")
    f = lax.axis_index("fsdp")
    x = lax.div(r, 2)
    c = lax.rem(r, 2)
    oc = 1 - c
    sib = 2 * x + oc
    xn = 2 * (1 - x) + c
    far = 2 * (1 - x) + oc
    y = lax.rem(f, 2)
    z = lax.div(f, 2)
    p = z + y * (7 - 2 * z)

    def f_at(place):
        place = lax.rem(place + 16, 8)
        yy = lax.div(place, 4)
        return 2 * (place + yy * (7 - 2 * place)) + yy

    right, left = f_at(p + 1), f_at(p - 1)
    toward = (right, left)

    def remote(src, dst, send, recv, device):
        return pltpu.make_async_remote_copy(
            src_ref=src, dst_ref=dst, send_sem=send, recv_sem=recv, device_id=device,
            device_id_type=MESH_ID,
        )

    def weight_slot(k, g):
        if k == WIN:
            return win.at[span(g * 192, 192, 64), :]
        if k == WO:
            return wo.at[:, span(g * 128, 128, 128)]
        if k == WG:
            return wg.at[span(g * 144, 144, 16), :]
        if k == WU:
            return wu.at[span(g * 144, 144, 16), :]
        return wd.at[:, span(g * 128, 128, 128)]

    def weight_part(k, g, h):
        if k == WIN:
            return win.at[span(g * 192 + 64 * x, 128, 64), pl.ds(512 * h, 512)]
        if k == WO:
            return wo.at[span(192 * x + 192 * h, 192, 192), span(g * 128, 128, 128)]
        if k == WG:
            return wg.at[span(g * 144, 144, 16), pl.ds(512 * h, 512)]
        if k == WU:
            return wu.at[span(g * 144, 144, 16), pl.ds(512 * h, 512)]
        return wd.at[pl.ds(576 * h, 576), span(g * 128, 128, 128)]

    reach = {WIN: (4, 3), WO: (3, 4), WG: (3, 4), WU: (3, 4), WD: (4, 3)}

    def ag_copy(k, s, way, g, h):
        view = weight_part(k, g, h)
        return remote(
            view, view, ag_s.at[k, way, s, h], ag_r.at[k, way, s, h], (r, toward[way])
        )

    def ag_send(k, s, way, h):
        ag_copy(k, s, way, f_at(p - s) if way == CW else f_at(p + s), h).start()

    def side_copy(k, s, way, half):
        g = f_at(p - 1 - s) if way == CW else f_at(p + 1 + s)
        if k == WIN:
            view = win.at[span(g * 192 + 128 * half, 64, 64), :]
        else:
            view = wo.at[span(384 * half, 192, 192), span(g * 128, 128, 128)]
        return remote(view, view, side_s.at[k, way, s], side_r.at[k, way, s], (xn, f))

    def ag_start(k):
        for h in (0, 1):
            for way in (CW, CCW):
                ag_send(k, 0, way, h)

    def ag_event(k, s):
        for h in (0, 1):
            for way in (CW, CCW):
                if s < reach[k][way]:
                    g = f_at(p - 1 - s) if way == CW else f_at(p + 1 + s)
                    ag_copy(k, s, way, g, h).wait_recv()
                    if s + 1 < reach[k][way]:
                        ag_send(k, s + 1, way, h)
                    if h and k in (WIN, WO):
                        side_copy(k, s, way, x).start()

    def side_arrive(k):
        for way in (CW, CCW):
            for s in range(reach[k][way]):
                side_copy(k, s, way, 1 - x).wait_recv()

    def side_drain(k):
        for way in (CW, CCW):
            for s in range(reach[k][way]):
                side_copy(k, s, way, x).wait_send()

    def ag_drain(k):
        for way in (CW, CCW):
            for s in range(reach[k][way]):
                for h in (0, 1):
                    ag_copy(k, s, way, f, h).wait_send()

    def grad_piece(k, g, way):
        if k == WD:
            return dwd.at[pl.ds(576 * way, 576), span(g * 128, 128, 128)]
        if k == WG:
            return cot.at[span(g * 144, 144, 16), pl.ds(512 * way, 512)]
        if k == WU:
            return wu.at[span(g * 144, 144, 16), pl.ds(512 * way, 512)]
        if k == WO:
            return gate.at[pl.ds(512 + 256 * way, 256), span(1024 + g * 128, 128, 128)]
        return gate.at[
            span(192 * lax.rem(g, 6), 192, 64), span(1024 * lax.div(g, 6) + 512 * way + 256 * (k == WIN2), 256, 128)
        ]

    def sum_slot(k, way, s):
        if k == WD:
            return slots_d.at[way, s]
        if k == WG:
            return slots_g.at[way, s]
        if k == WU:
            return slots_u.at[way, s]
        i = way * 7 + s
        if k == WO:
            return up.at[pl.ds(768, 256), pl.ds(128 * i, 128)]
        return up.at[pl.ds(192 * (i // 4), 192), pl.ds(512 * (i % 4) + 256 * (k == WIN2), 256)]

    def rs_copy(k, way, s):
        src = sum_slot(k, way, s - 1) if s else grad_piece(
            k, f_at(p - 1) if way == CW else f_at(p + 1), way
        )
        return remote(
            src, sum_slot(k, way, s), rs_s.at[k, way, s], rs_r.at[k, way, s], (r, toward[way])
        )

    def rs_start(k):
        rs_copy(k, CW, 0).start()
        rs_copy(k, CCW, 0).start()

    def rs_event(k, s):
        for way in (CW, CCW):
            g = f_at(p - 2 - s) if way == CW else f_at(p + 2 + s)
            rs_copy(k, way, s).wait_recv()
            slot = sum_slot(k, way, s)
            slot[...] = (slot[...].astype(F32) + grad_piece(k, g, way)[...].astype(F32)).astype(BF16)
            if s < 6:
                rs_copy(k, way, s + 1).start()

    def rs_drain(k):
        for way in (CW, CCW):
            for s in range(7):
                rs_copy(k, way, s).wait_send()

    ffn_out = {WD: (0, o_d), WG: (1, o_g), WU: (2, o_u)}
    peers = (sib, xn, far)

    def final_view(k, owner, way):
        out = ffn_out[k][1]
        if k == WD:
            return out.at[owner, pl.ds(576 * way, 576), :]
        return out.at[owner, :, pl.ds(512 * way, 512)]

    def final_copy(k, way, j):
        i = ffn_out[k][0]
        src = final_view(k, xn, way) if j == 2 else sum_slot(k, way, 6)
        dst = final_view(k, xn if j == 2 else r, way)
        if j == 3:
            return pltpu.make_async_copy(src, dst, fin_s.at[i, way, 3])
        return remote(
            src, dst, fin_s.at[i, way, j], fin_r.at[i, way, j], (xn if j == 1 else sib, f)
        )

    def final_start(k):
        for way in (CW, CCW):
            for j in (1, 0, 3):
                final_copy(k, way, j).start()

    def final_arrive(k, way, j):
        i = ffn_out[k][0]
        view = final_view(k, peers[j], way)
        remote(view, view, fin_s.at[i, way, j], fin_r.at[i, way, j], (sib, f)).wait_recv()

    def final_forward(k):
        for way in (CW, CCW):
            final_arrive(k, way, 1)
            final_copy(k, way, 2).start()

    def final_drain(k):
        for way in (CW, CCW):
            final_copy(k, way, 3).wait()
            for j in range(3):
                final_copy(k, way, j).wait_send()
            final_arrive(k, way, 0)
            final_arrive(k, way, 2)

    loads = [
        pltpu.make_async_copy(win_in, weight_slot(WIN, f), loc_sem.at[0]),
        pltpu.make_async_copy(
            taps_in, wo.at[pl.ds(512, 64), span(f * 128, 128, 128)], loc_sem.at[1]
        ),
        pltpu.make_async_copy(li, part.at[0], loc_sem.at[2]),
        pltpu.make_async_copy(cot_in, cot.at[span(r * 512, 512, 512), :], loc_sem.at[3]),
        pltpu.make_async_copy(wg_in, weight_slot(WG, f), loc_sem.at[4]),
        pltpu.make_async_copy(wu_in, weight_slot(WU, f), loc_sem.at[5]),
        pltpu.make_async_copy(ids_in, ids.at[0], loc_sem.at[6]),
        pltpu.make_async_copy(gains_in, gains.at[:, span(f * 128, 128, 128)], loc_sem.at[7]),
    ]
    loads_out = [
        pltpu.make_async_copy(
            wo_in.at[g, c], wo.at[pl.ds(64 * g, 64), span(f * 128, 128, 128)], loc_sem.at[8 + g]
        )
        for g in range(8)
    ]
    loads_down = [
        pltpu.make_async_copy(
            wd_in.at[g, r], wd.at[pl.ds(144 * g, 144), span(f * 128, 128, 128)], loc_sem.at[16 + g]
        )
        for g in range(8)
    ]
    for load in loads[:2] + loads_out + loads[2:] + loads_down:
        load.start()
    barrier = pltpu.get_barrier_semaphore()
    for j in range(1, 8):
        pl.semaphore_signal(
            barrier, inc=1, device_id=(r, lax.rem(f + j, 8)), device_id_type=MESH_ID
        )
    for peer in peers:
        pl.semaphore_signal(barrier, inc=1, device_id=(peer, f), device_id_type=MESH_ID)
    dtap[...] = jnp.zeros_like(dtap)
    dgain[...] = jnp.zeros_like(dgain)
    pl.semaphore_wait(barrier, 10)

    def gain_copy(j):
        return remote(
            gains_in, gains.at[:, span(f * 128, 128, 128)], gain_s.at[j - 1], gain_r.at[j - 1],
            (r, lax.rem(f + j, 8)),
        )

    def cot_copy(m, j):
        rows = span((xn if j == 2 else r) * 512 + m * 256, 256, 256)
        return remote(
            cot.at[rows, :], cot.at[rows, :], cot_s.at[m, j], cot_r.at[m, j],
            (xn if j == 1 else sib, f),
        )

    def cot_arrive(m, j):
        rows = span((sib, xn, far)[j] * 512 + m * 256, 256, 256)
        remote(
            cot.at[rows, :], cot.at[rows, :], cot_s.at[m, j], cot_r.at[m, j], (sib, f)
        ).wait_recv()

    def n2_copy(m, j):
        rows = span((xn if j == 2 else r) * 512 + m * 256, 256, 256)
        return remote(
            n2.at[rows, :], n2.at[rows, :], n2_s.at[m, j], n2_r.at[m, j],
            (xn if j == 1 else sib, f),
        )

    def n2_arrive(m, j):
        rows = span((sib, xn, far)[j] * 512 + m * 256, 256, 256)
        remote(
            n2.at[rows, :], n2.at[rows, :], n2_s.at[m, j], n2_r.at[m, j], (sib, f)
        ).wait_recv()

    def rim_copy(j):
        if j == 2:
            src, dst = ids_in, ids.at[1]
        else:
            src, dst = li.at[pl.ds(240 + 256 * j, 16), :], hal.at[pl.ds(16 * j, 16), :]
        return remote(src, dst, rim_s.at[j], rim_r.at[j], (r, lax.rem(f + 1, 8)))

    for j in range(1, 8):
        gain_copy(j).start()
    for j in range(3):
        rim_copy(j).start()
    for load in loads[:2] + loads_out:
        load.wait()
    ag_start(WIN)
    ag_start(WO)
    loads[3].wait()
    cot_copy(0, 0).start()
    cot_copy(0, 1).start()
    loads[2].wait()
    loads[7].wait()
    for j in range(1, 8):
        gain_copy(j).wait_recv()

    gain_one = gains[0:1, :]
    gain_two = gains[1:2, :]

    def norm_rows(rows):
        rows = rows.astype(F32)
        scale = lax.rsqrt(jnp.mean(rows * rows, axis=1, keepdims=True) + epsilon)
        return (rows * scale * gain_one).astype(BF16)

    def norm_step(i, carry):
        rows = span(i * 64, 64, 64)
        n1[c, rows, :] = norm_rows(part[0, rows, :])
        return carry

    lax.fori_loop(0, 8, norm_step, 0)
    for j in range(3):
        rim_copy(j).wait_recv()
    started = jnp.where(f > 0, 1.0, 0.0).astype(F32)
    n1[c, 512:544, :] = norm_rows(hal[...].astype(F32) * started)
    n1_copy = remote(n1.at[c], n1.at[c], n1_s, n1_r, (sib, f))
    n1_copy.start()
    loads[6].wait()
    here, before = ids[0], ids[1]
    lane_ids = lax.broadcasted_iota(jnp.int32, (8, 256), 1)
    last = before[:, 255:256]
    prev = jnp.where(lane_ids == 0, last, pltpu.roll(here, 1, 1))
    masks[c, 0:8, :] = jnp.where(prev == here, 1.0, 0.0)
    prev = jnp.where(
        lane_ids == 0, before[:, 254:255], jnp.where(lane_ids == 1, last, pltpu.roll(here, 2, 1))
    )
    masks[c, 8:16, :] = jnp.where(prev == here, 1.0, 0.0)
    mask_copy = remote(masks.at[c], masks.at[c], mask_s, mask_r, (sib, f))
    mask_copy.start()

    for s in (0, 1):
        ag_event(WIN, s)
        ag_event(WO, s)
    for load in loads[4:6] + loads_down:
        load.wait()
    ag_event(WIN, 2)
    ag_event(WO, 2)
    ag_start(WG)
    cot_arrive(0, 1)
    cot_copy(0, 2).start()
    ag_event(WIN, 3)
    ag_event(WO, 3)
    ag_start(WU)
    ag_event(WG, 0)
    side_arrive(WIN)
    side_arrive(WO)

    for g in range(8):
        taps[64 * g : 64 * g + 64, :] = wo[512:576, 128 * g : 128 * g + 128]
    remote(n1.at[oc], n1.at[oc], n1_s, n1_r, (sib, f)).wait_recv()
    remote(masks.at[oc], masks.at[oc], mask_s, mask_r, (sib, f)).wait_recv()
    lane256 = lax.broadcasted_iota(jnp.int32, (64, 256), 1)

    def halo_product(qc):
        rows = n1[qc, 512:544, :]
        return dot_nt(win[0:512, :], rows) * dot_nt(win[1024:1536, :], rows)

    hbx[:, 0:32] = halo_product(0)
    hbx[:, 32:64] = halo_product(1)

    def earlier(bx, qc, rows, m):
        held = hbx[rows, 0:64]
        place = 32 * qc + 16 * m
        spot = lax.broadcasted_iota(jnp.int32, (64, 64), 1) - place
        one = jnp.sum(jnp.where(spot == 15, held, 0.0), axis=1, keepdims=True)
        two = jnp.sum(jnp.where(spot == 14, held, 0.0), axis=1, keepdims=True)
        prev_one = jnp.where(lane256 == 0, one, pltpu.roll(bx, 1, 1))
        prev_two = jnp.where(
            lane256 == 0, two, jnp.where(lane256 == 1, one, pltpu.roll(bx, 2, 1))
        )
        return prev_one, prev_two

    def tap_columns(rows):
        held = taps[rows, :].astype(F32)
        return held[:, 0:1], held[:, 1:2], held[:, 2:3]

    def mix_fwd(qc, m):
        tokens = n1[qc, 256 * m : 256 * m + 256, :]
        lanes = span(qc * 512 + m * 256, 256, 256)
        mask_one = masks[qc, m : m + 1, :]
        mask_two = masks[qc, 8 + m : 9 + m, :]
        for i in range(3):
            gmid[:, 256 * i : 256 * i + 256] = dot_nt(win[512 * i : 512 * i + 512, :], tokens)

        def step(i, carry):
            rows = span(64 * i, 64, 64)
            b, cc, xx = gmid[rows, 0:256], gmid[rows, 256:512], gmid[rows, 512:768]
            proj[rows, lanes] = b.astype(BF16)
            proj[span(512 + 64 * i, 64, 64), lanes] = cc.astype(BF16)
            proj[span(1024 + 64 * i, 64, 64), lanes] = xx.astype(BF16)
            bx = b * xx
            prev_one, prev_two = earlier(bx, qc, rows, m)
            t0, t1, t2 = tap_columns(rows)
            conv = (
                t0 * bx + t1 * (mask_one * prev_one) + t2 * (mask_two * prev_two)
            )
            gated[rows, lanes] = (cc * conv).astype(BF16)
            return carry

        lax.fori_loop(0, 8, step, 0)
        return dot_tn(gated[:, lanes], wo[0:512, :])

    def ex_copy(op, kind, m):
        rows = span(256 * m, 256, 256)
        src = part.at[{0: 1, 1: 0, 2: 2}[kind], rows, :]
        if op == DOWN and kind == 2:
            src = cot.at[span(1152 + 256 * m, 256, 128), :]
        dst = rxn.at[rows, :] if kind == 2 else rsib.at[kind, rows, :]
        return remote(
            src, dst, ex_s.at[op, kind, m], ex_r.at[op, kind, m], (xn if kind == 2 else sib, f)
        )

    for m in (0, 1):
        part[1, 256 * m : 256 * m + 256, :] = mix_fwd(oc, m).astype(BF16)
        ex_copy(OUT, 0, m).start()
        if m:
            ag_event(WU, 0)
        middle[256 * m : 256 * m + 256, :] = mix_fwd(c, m)
        if m == 0:
            ag_event(WG, 1)
        ex_copy(OUT, 0, m).wait_recv()

        def norm_two_step(i, carry):
            rows = span(256 * m + i * 64, 64, 64)
            mid = middle[rows, :] + rsib[0, rows, :].astype(F32) + part[0, rows, :].astype(F32)
            middle[rows, :] = mid
            scale = lax.rsqrt(jnp.mean(mid * mid, axis=1, keepdims=True) + epsilon)
            n2[span(r * 512 + 256 * m + i * 64, 64, 64), :] = (mid * scale * gain_two).astype(BF16)
            return carry

        lax.fori_loop(0, 4, norm_two_step, 0)
        n2_copy(m, 1).start()
        n2_copy(m, 0).start()
        if m:
            cot_copy(1, 1).start()
            cot_copy(1, 0).start()
    pl.semaphore_signal(sib_credit, inc=1, device_id=(sib, f), device_id_type=MESH_ID)
    mid_copy = pltpu.make_async_copy(middle, o_lo, out_sem.at[0])
    mid_copy.start()
    for m in (0, 1):
        ex_copy(OUT, 0, m).wait_send()
    ag_event(WG, 2)
    ag_event(WU, 1)
    ag_start(WD)
    ag_event(WG, 3)

    def gate_half(q):
        def step(i, carry):
            rows = span(lax.rem(i, 3) * 384, 384, 128)
            tokens = span(q * 512 + lax.div(i, 3) * 256, 256, 256)
            gate[rows, tokens] = dot_nt(wg[rows, :], n2[tokens, :]).astype(BF16)
            return carry

        lax.fori_loop(0, 6, step, 0)

    def up_half(q):
        def step(i, carry):
            rows = span(lax.rem(i, 3) * 384, 384, 128)
            tokens = span(q * 512 + lax.div(i, 3) * 256, 256, 256)
            u = dot_nt(wu[rows, :], n2[tokens, :])
            g = gate[rows, tokens].astype(F32)
            up[rows, tokens] = u.astype(BF16)
            hidden[rows, tokens] = (g * jax.nn.sigmoid(g) * u).astype(BF16)
            return carry

        lax.fori_loop(0, 6, step, 0)

    gate_half(r)
    ag_event(WU, 2)
    for m in (0, 1):
        n2_arrive(m, 0)
    gate_half(sib)
    for m in (0, 1):
        n2_arrive(m, 1)
        n2_copy(m, 2).start()
    ag_event(WD, 0)
    gate_half(xn)
    for m in (0, 1):
        n2_arrive(m, 2)
    gate_half(far)
    cot_arrive(1, 1)
    cot_copy(1, 2).start()
    ag_event(WU, 3)
    up_half(r)
    up_half(sib)
    ag_event(WD, 1)
    up_half(xn)
    up_half(far)
    ag_event(WD, 2)
    for m in (0, 1):
        cot_arrive(m, 0)
        cot_arrive(m, 2)

    def dwd_step(i, carry):
        rows = span(i * 384, 384, 128)
        for n in (0, 512):
            dwd[rows, n : n + 512] = dot_nn(hidden[rows, :], cot[:, n : n + 512]).astype(BF16)
        return carry

    lax.fori_loop(0, 3, dwd_step, 0)
    rs_start(WD)
    ag_event(WD, 3)

    def ring(*events):
        for k, s in events:
            rs_event(k, s)

    def grad_hidden(q):
        def step(i, carry):
            rows = span(lax.rem(i, 3) * 384, 384, 128)
            tokens = span(q * 512 + lax.div(i, 3) * 256, 256, 256)
            gh = dot_nt(wd[rows, :], cot[tokens, :])
            g = gate[rows, tokens].astype(F32)
            u = up[rows, tokens].astype(F32)
            s = jax.nn.sigmoid(g)
            gate[rows, tokens] = (gh * u * s * (1.0 + g * (1.0 - s))).astype(BF16)
            up[rows, tokens] = (gh * g * s).astype(BF16)
            return carry

        lax.fori_loop(0, 6, step, 0)

    for i, q in enumerate((r, sib, xn, far)):
        grad_hidden(q)
        if i % 2:
            ring((WD, i // 2))
    for m in (0, 1):
        for j in range(3):
            cot_copy(m, j).wait_send()
            n2_copy(m, j).wait_send()
    ag_drain(WG)
    ag_drain(WU)

    def dwg_step(i, carry):
        rows = span(i * 384, 384, 128)
        for n in (0, 512):
            cot[rows, n : n + 512] = dot_nn(gate[rows, :], n2[:, n : n + 512]).astype(BF16)
        return carry


    def gn2_part(q, m):
        tokens = span(q * 512 + m * 256, 256, 256)
        return dot_tn(gate[:, tokens], wg[...]) + dot_tn(up[:, tokens], wu[...])

    def down_part(q, m):
        return dot_tn(hidden[:, span(q * 512 + m * 256, 256, 256)], wd[...])

    def to_part(partial, q, dst, op=None, kind=None):
        def step(m, carry):
            dst(m)[...] = partial(q, m).astype(BF16)
            if op is not None:
                ex_copy(op, kind, m).start()
            return carry

        lax.fori_loop(0, 2, step, 0)

    def part_rows(slot):
        return lambda m: part.at[slot, span(256 * m, 256, 256), :]

    def core_sum(op, dst, halves=(0, 1)):
        for m in halves:
            ex_copy(op, 1, m).wait_recv()

            def add_step(i, carry):
                rows = span(256 * m + i * 64, 64, 64)
                view = dst(256 * m + i * 64)
                view[...] = (view[...].astype(F32) + rsib[1, rows, :].astype(F32)).astype(BF16)
                return carry

            lax.fori_loop(0, 4, add_step, 0)
            ex_copy(op, 2, m).start()

    lax.fori_loop(0, 3, dwg_step, 0)
    rs_start(WG)
    ring((WD, 2))
    pl.semaphore_wait(sib_credit, 1)
    for m in (0, 1):
        part[0, 256 * m : 256 * m + 256, :] = gn2_part(far, m).astype(BF16)
        ex_copy(GN2, 1, m).start()
        part[2, 256 * m : 256 * m + 256, :] = gn2_part(xn, m).astype(BF16)
        core_sum(GN2, lambda at: part.at[2, span(at, 64, 64), :], (m,))
    ring((WD, 3), (WG, 0))

    def own_step(m, carry):
        gmid[span(256 * m, 256, 256), :] = gn2_part(r, m)
        return carry

    lax.fori_loop(0, 2, own_step, 0)
    to_part(gn2_part, sib, part_rows(1))
    for m in (0, 1):
        ex_copy(GN2, 0, m).start()
    ring((WD, 4), (WG, 1))
    cot_again = pltpu.make_async_copy(
        cot_in, gate.at[pl.ds(0, 512), pl.ds(0, 1024)], loc_sem.at[3]
    )
    cot_again.start()

    def dwu_step(i, carry):
        rows = span(i * 384, 384, 128)
        for n in (0, 512):
            wu[rows, n : n + 512] = dot_nn(up[rows, :], n2[:, n : n + 512]).astype(BF16)
        return carry

    gb_copies = []

    def grad_middle(m):
        ex_copy(GN2, 0, m).wait_recv()
        ex_copy(GN2, 2, m).wait_recv()

        def grad_middle_step(i, carry):
            rows = span(256 * m + i * 64, 64, 64)
            gn = gmid[rows, :] + rsib[0, rows, :].astype(F32) + rxn[rows, :].astype(F32)
            mid = middle[rows, :]
            scale = lax.rsqrt(jnp.mean(mid * mid, axis=1, keepdims=True) + epsilon)
            dgain[1:2, :] += jnp.sum(gn * (mid * scale), axis=0, keepdims=True)
            weighted = gn * gain_two
            inner = jnp.mean(weighted * mid, axis=1, keepdims=True)
            gm = (
                gate[rows, 0:1024].astype(F32)
                + scale * weighted
                - mid * (scale * scale * scale * inner)
            )
            gmid[rows, :] = gm
            wg[span(c * 512 + 256 * m + i * 64, 64, 64), :] = gm.astype(BF16)
            return carry

        lax.fori_loop(0, 4, grad_middle_step, 0)
        rows = span(c * 512 + 256 * m, 256, 256)
        copy = remote(wg.at[rows, :], wg.at[rows, :], gb_s.at[m], gb_r.at[m], (sib, f))
        copy.start()
        gb_copies.append(copy)

    lax.fori_loop(0, 3, dwu_step, 0)
    rs_start(WU)
    pl.semaphore_signal(oi_ready, inc=1, device_id=(r, right), device_id_type=MESH_ID)
    pl.semaphore_signal(oi_ready, inc=1, device_id=(r, left), device_id_type=MESH_ID)
    cot_again.wait()
    grad_middle(0)
    ring((WD, 5), (WG, 2))
    grad_middle(1)
    ring((WD, 6), (WG, 3))
    pl.semaphore_signal(sib_credit, inc=1, device_id=(sib, f), device_id_type=MESH_ID)
    pl.semaphore_signal(xn_credit, inc=1, device_id=(xn, f), device_id_type=MESH_ID)
    mid_copy.wait()
    for m in (0, 1):
        rows = span(oc * 512 + 256 * m, 256, 256)
        remote(wg.at[rows, :], wg.at[rows, :], gb_s.at[m], gb_r.at[m], (sib, f)).wait_recv()

    mix_place = {WIN: 0, WIN2: 1, WO: 2}

    def mix_sum(k, way):
        if k == WO:
            return mix_o.at[pl.ds(256 * way, 256), :]
        return cot.at[pl.ds(1664, 192), pl.ds(512 * way + 256 * (k == WIN2), 256)]

    def mx_copy(k, way):
        i = mix_place[k]
        return remote(
            sum_slot(k, way, 6), mix_sum(k, way), mx_s.at[i, way], mx_r.at[i, way], (xn, f)
        )

    def mix_start(k):
        for way in (CW, CCW):
            mx_copy(k, way).start()

    def mix_view(k, owner, way):
        if k == WO:
            return o_o.at[owner, pl.ds(256 * way, 256), :]
        return o_i.at[owner, :, pl.ds(512 * way + 256 * (k == WIN2), 256)]

    def mix_copies(k, way):
        i = mix_place[k]
        dst = mix_sum(k, way)
        return (
            remote(dst, mix_view(k, c, way), ms_s.at[i, way], ms_r.at[i, way], (sib, f)),
            pltpu.make_async_copy(dst, mix_view(k, c, way), out_sem.at[3 + 2 * i + way]),
        )

    lane128 = lax.broadcasted_iota(jnp.int32, (512, 128), 1)
    rim = jnp.zeros((512, 128), F32)
    taps_one, taps_two = tap_columns(slice(None))[1:]
    for qc in (0, 1):
        for m in (0, 1):
            at = qc * 512 + m * 256
            gg = dot_nt(wo[0:512, :], wg[at : at + 16, :])
            gc = gg * proj[512:1024, at : at + 128].astype(F32)[:, 0:16]
            masked_one = masks[qc, m : m + 1, 0:16] * gc
            masked_two = masks[qc, 8 + m : 9 + m, 0:16] * gc
            first = taps_two * masked_two[:, 0:1]
            second = taps_one * masked_one[:, 0:1] + taps_two * masked_two[:, 1:2]
            b = 2 * (2 * qc + m)
            rim = jnp.where(lane128 == b, first, jnp.where(lane128 == b + 1, second, rim))
    halo_out[...] = rim.astype(BF16)
    halo_copy = remote(halo_out, halo_in, halo_s, halo_r, (r, lax.rem(f + 7, 8)))
    halo_copy.start()

    for n in (0, 512):
        gate[512:1024, 1024 + n : 1536 + n] = dot_nn(gated[...], wg[0:1024, n : n + 512]).astype(BF16)
    pl.semaphore_wait(oi_ready, 2)
    rs_start(WO)
    ring((WG, 4), (WU, 0))
    halo_copy.wait_recv()
    inside = jnp.where(f < 7, 1.0, 0.0).astype(F32)
    lane_tap = lax.broadcasted_iota(jnp.int32, (64, 128), 1)

    def mix_bwd(qc, m):
        lanes = pl.ds(qc * 512 + m * 256, 256)
        tokens = wg[qc * 512 + m * 256 : qc * 512 + m * 256 + 256, :]
        mask_one = masks[qc, m : m + 1, :]
        mask_two = masks[qc, 8 + m : 9 + m, :]
        b2 = 2 * (2 * qc + m)
        middle[:, 0:256] = dot_nt(wo[0:512, :], tokens)

        def step(i, carry):
            rows = span(64 * i, 64, 64)
            c_rows, x_rows = span(512 + 64 * i, 64, 64), span(1024 + 64 * i, 64, 64)
            gg = middle[rows, 0:256]
            b = proj[rows, lanes].astype(F32)
            cc = proj[c_rows, lanes].astype(F32)
            xx = proj[x_rows, lanes].astype(F32)
            bx = b * xx
            prev_one, prev_two = earlier(bx, qc, rows, m)
            prev_one = mask_one * prev_one
            prev_two = mask_two * prev_two
            t0, t1, t2 = tap_columns(rows)
            conv = t0 * bx + t1 * prev_one + t2 * prev_two
            gc = gg * cc
            sum0 = jnp.sum(gc * bx, axis=1, keepdims=True)
            sum1 = jnp.sum(gc * prev_one, axis=1, keepdims=True)
            sum2 = jnp.sum(gc * prev_two, axis=1, keepdims=True)
            dtap[rows, :] += jnp.where(
                lane_tap == 0, sum0, jnp.where(lane_tap == 1, sum1, jnp.where(lane_tap == 2, sum2, 0.0))
            )
            back_one = jnp.where(lane256 < 255, pltpu.roll(mask_one * gc, 255, 1), 0.0)
            back_two = jnp.where(lane256 < 254, pltpu.roll(mask_two * gc, 254, 1), 0.0)
            edge = halo_in[rows, :].astype(F32) * inside
            back = jnp.where(
                lane256 == 254, edge[:, b2 : b2 + 1],
                jnp.where(lane256 == 255, edge[:, b2 + 1 : b2 + 2], 0.0),
            )
            gbx = t0 * gc + t1 * back_one + t2 * back_two + back
            proj[rows, lanes] = (gbx * xx).astype(BF16)
            proj[c_rows, lanes] = (gg * conv).astype(BF16)
            proj[x_rows, lanes] = (gbx * b).astype(BF16)
            return carry

        lax.fori_loop(0, 8, step, 0)

    for qc in (0, 1):
        for m in (0, 1):
            mix_bwd(qc, m)
        if qc == 0:
            ring((WG, 5), (WU, 1), (WO, 0))
    ring((WG, 6), (WU, 2), (WO, 1))

    def dwin(t, n):
        rows = span(384 * t, 384, 128)
        return (
            dot_nn(proj[rows, 0:512], n1[0, 0:512, n : n + 512])
            + dot_nn(proj[rows, 512:1024], n1[1, 0:512, n : n + 512])
        ).astype(BF16)

    def dwin_step(t, carry):
        for n in (0, 512):
            gate[span(384 * t, 384, 128), n : n + 512] = dwin(t, n)
        return carry

    lax.fori_loop(0, 3, dwin_step, 0)
    for n in (0, 512):
        gate[0:384, 1024 + n : 1536 + n] = dwin(3, n)
    rs_start(WIN)
    rs_start(WIN2)

    for m in (0, 1):
        ex_copy(GN2, 0, m).wait_send()
        ex_copy(GN2, 1, m).wait_send()
        ex_copy(GN2, 2, m).wait_send()
    pl.semaphore_wait(sib_credit, 1)
    to_part(down_part, far, part_rows(0), DOWN, 1)
    to_part(down_part, xn, lambda m: cot.at[span(1152 + 256 * m, 256, 128), :])
    pl.semaphore_wait(xn_credit, 1)
    core_sum(DOWN, lambda at: cot.at[span(1152 + at, 64, 64), :])
    pl.semaphore_signal(sib_credit, inc=1, device_id=(sib, f), device_id_type=MESH_ID)
    ring((WU, 3), (WO, 2), (WIN, 0), (WIN2, 0))
    final_start(WD)
    final_start(WG)
    to_part(down_part, sib, part_rows(1), DOWN, 0)

    def gn1_part(qc, m):
        return dot_tn(proj[:, span(qc * 512 + m * 256, 256, 256)], win[...])

    pl.semaphore_wait(sib_credit, 1)
    for m in (0, 1):
        ex_copy(DOWN, 0, m).wait_send()
        ex_copy(DOWN, 1, m).wait_send()
    li_again = pltpu.make_async_copy(li, part.at[1], loc_sem.at[2])
    li_again.start()
    to_part(gn1_part, oc, part_rows(0), GN1, 1)
    ring((WU, 4), (WO, 3), (WIN, 1), (WIN2, 1))
    for m in (0, 1):
        middle[256 * m : 256 * m + 256, :] = gn1_part(c, m)
    ring((WU, 5), (WO, 4), (WIN, 2), (WIN2, 2))
    li_again.wait()
    for m in (0, 1):
        ex_copy(GN1, 1, m).wait_recv()

        def grad_in_step(i, carry):
            rows = span(256 * m + i * 64, 64, 64)
            gn = middle[rows, :] + rsib[1, rows, :].astype(F32)
            res = part[1, rows, :].astype(F32)
            scale = lax.rsqrt(jnp.mean(res * res, axis=1, keepdims=True) + epsilon)
            dgain[0:1, :] += jnp.sum(gn * (res * scale), axis=0, keepdims=True)
            weighted = gn * gain_one
            inner = jnp.mean(weighted * res, axis=1, keepdims=True)
            middle[rows, :] = gmid[rows, :] + scale * weighted - res * (scale * scale * scale * inner)
            return carry

        lax.fori_loop(0, 4, grad_in_step, 0)
    gi_copy = pltpu.make_async_copy(middle, o_gi, out_sem.at[1])
    gi_copy.start()
    for m in (0, 1):
        ex_copy(GN1, 1, m).wait_send()

    for g in range(8):
        gmid[0:64, 128 * g : 128 * g + 128] = dtap[64 * g : 64 * g + 64, :]
        gmid[64:72, 128 * g : 128 * g + 128] = dgain[:, 128 * g : 128 * g + 128]

    def small_p(g):
        return gmid.at[pl.ds(0, 72), span(g * 128, 128, 128)]

    def small_copy(j):
        g = lax.rem(f + j, 8)
        return remote(small_p(g), small_r.at[j], sm_s.at[j - 1], sm_r.at[j - 1], (r, g))

    for j in range(1, 8):
        small_copy(j).start()
    ring((WU, 6), (WO, 5), (WIN, 3), (WIN2, 3))
    final_start(WU)
    total = small_p(f)[...]
    for j in range(1, 8):
        small_copy(j).wait_recv()
        total = total + small_r[j]
    small_x[0] = total
    sx_copy = remote(small_x.at[0], small_x.at[1], sx_s.at[0], sx_r.at[0], (xn, f))
    sx_copy.start()
    gi_copy.wait()
    mid_again = pltpu.make_async_copy(o_lo, middle, out_sem.at[0])
    mid_again.start()
    ring((WO, 6), (WIN, 4), (WIN2, 4))
    final_forward(WD)
    sx_copy.wait_recv()
    small_x[2] = small_x[0] + small_x[1]
    ss_copy = remote(small_x.at[2], o_s.at[c], sx_s.at[1], sx_r.at[1], (sib, f))
    ss_copy.start()
    so_copy = pltpu.make_async_copy(small_x.at[2], o_s.at[c], out_sem.at[2])
    so_copy.start()
    for way in (CW, CCW):
        mx_copy(WO, way).start()

    mid_again.wait()
    for m in (0, 1):
        ex_copy(DOWN, 0, m).wait_recv()
        ex_copy(DOWN, 2, m).wait_recv()
        middle[256 * m : 256 * m + 256, :] += down_part(r, m)

        def out_step(i, carry):
            rows = span(256 * m + i * 64, 64, 64)
            middle[rows, :] += rsib[0, rows, :].astype(F32) + rxn[rows, :].astype(F32)
            return carry

        lax.fori_loop(0, 4, out_step, 0)
        if m == 0:
            ring((WIN, 5), (WIN2, 5))
    lo_copy = pltpu.make_async_copy(middle, o_lo, out_sem.at[0])
    lo_copy.start()
    final_forward(WG)
    ring((WIN, 6))
    mix_start(WIN)
    ring((WIN2, 6))
    mix_start(WIN2)
    final_forward(WU)

    for k in (WO, WIN, WIN2):
        for way in (CW, CCW):
            mx_copy(k, way).wait_recv()
            dst = mix_sum(k, way)
            dst[...] = (dst[...].astype(F32) + sum_slot(k, way, 6)[...].astype(F32)).astype(BF16)
            for out in mix_copies(k, way):
                out.start()

    for k in (WIN, WO, WD):
        ag_drain(k)
    for k in (WIN, WO):
        side_drain(k)
    for k in range(6):
        rs_drain(k)
    for k in (WD, WG, WU):
        final_drain(k)
    for j in range(1, 8):
        gain_copy(j).wait_send()
        small_copy(j).wait_send()
    mask_copy.wait_send()
    for j in range(3):
        rim_copy(j).wait_send()
    n1_copy.wait_send()
    for m in (0, 1):
        gb_copies[m].wait_send()
    halo_copy.wait_send()
    lo_copy.wait()
    so_copy.wait()
    for m in (0, 1):
        ex_copy(DOWN, 2, m).wait_send()
    sx_copy.wait_send()
    ss_copy.wait_send()
    other = o_s.at[oc]
    remote(other, other, sx_s.at[1], sx_r.at[1], (sib, f)).wait_recv()
    for k in (WO, WIN, WIN2):
        i = mix_place[k]
        for way in (CW, CCW):
            mx_copy(k, way).wait_send()
            out, local = mix_copies(k, way)
            out.wait_send()
            local.wait()
            view = mix_view(k, oc, way)
            remote(view, view, ms_s.at[i, way], ms_r.at[i, way], (sib, f)).wait_recv()


def grouped_device(
    layer_in, segments, w_in, w_out, w_gate, w_up, w_down, conv_taps, gain_one, gain_two, cotangent
):
    r = lax.axis_index("rep")
    c = lax.rem(r, 2)
    width = layer_in.shape[2]

    def pick(array, axis, index):
        return lax.dynamic_index_in_dim(array, index, axis, keepdims=False)

    ids = jnp.pad(segments.astype(F32), ((0, 6), (0, 0)))
    own_in = pick(w_in.reshape(width, 3, 2, 64), 2, c).reshape(width, 192).T
    tap_half = pick(conv_taps.reshape(3, 2, 64), 1, c)
    tap_cols = jnp.pad(tap_half.T, ((0, 0), (0, 125)))
    own_gate = pick(w_gate.reshape(width, 4, 144), 1, r).T
    own_up = pick(w_up.reshape(width, 4, 144), 1, r).T
    gains = jnp.pad(jnp.stack([gain_one, gain_two]).astype(F32), ((0, 6), (0, 0)))

    hbm = pl.BlockSpec(memory_space=pl.ANY)
    dma = pltpu.SemaphoreType.DMA
    regular = pltpu.SemaphoreType.REGULAR

    def big(*shape, dtype=BF16):
        return pltpu.VMEM(shape, dtype)

    outs = pl.pallas_call(
        layer_kernel,
        out_shape=(
            jax.ShapeDtypeStruct((512, 1024), F32),
            jax.ShapeDtypeStruct((512, 1024), F32),
            jax.ShapeDtypeStruct((4, 1152, 128), BF16),
            jax.ShapeDtypeStruct((4, 144, 1024), BF16),
            jax.ShapeDtypeStruct((4, 144, 1024), BF16),
            jax.ShapeDtypeStruct((2, 192, 1024), BF16),
            jax.ShapeDtypeStruct((2, 512, 128), BF16),
            jax.ShapeDtypeStruct((2, 72, 128), F32),
        ),
        in_specs=[hbm] * 10,
        out_specs=[hbm] * 8,
        scratch_shapes=[
            big(1536, 1024), big(576, 1024), big(1152, 1024), big(1152, 1024), big(1152, 1024),
            big(2, 544, 1024), big(2048, 1024), big(2048, 1024), big(1536, 1024), big(512, 1024),
            big(1152, 2048), big(1152, 2048), big(1152, 2048), big(1152, 1024),
            big(2, 7, 576, 128), big(2, 7, 144, 512), big(2, 7, 144, 512),
            big(3, 512, 1024), big(2, 512, 1024), big(512, 1024),
            big(512, 1024, dtype=F32), big(512, 1024, dtype=F32),
            big(8, 1024, dtype=F32), big(2, 16, 256, dtype=F32),
            big(2, 8, 256, dtype=F32), big(32, 1024), big(512, 128),
            big(512, 128, dtype=F32), big(512, 128), big(512, 128),
            big(512, 128, dtype=F32), big(8, 1024, dtype=F32), big(512, 128),
            big(8, 72, 128, dtype=F32), big(3, 72, 128, dtype=F32),
            dma((24,)), dma((2, 2, 4)), dma((2, 2, 4)), dma((5, 2, 4, 2)), dma((5, 2, 4, 2)), dma((6, 2, 7)), dma((6, 2, 7)),
            dma((7,)), dma((7,)), dma, dma, dma, dma, dma((3,)), dma((3,)),
            dma((2, 3)), dma((2, 3)), dma((2, 3)), dma((2, 3)),
            dma((4, 3, 2)), dma((4, 3, 2)), dma((2,)), dma((2,)), dma, dma,
            dma((3, 2, 4)), dma((3, 2, 3)), dma((3, 2)), dma((3, 2)),
            dma((3, 2)), dma((3, 2)), dma((7,)), dma((7,)), dma((2,)), dma((2,)), dma((9,)),
            regular, regular, regular,
        ],
        compiler_params=pltpu.CompilerParams(
            collective_id=0, has_side_effects=True, vmem_limit_bytes=VMEM_BYTES
        ),
        name="layer",
    )(
        layer_in.reshape(512, width), cotangent.reshape(512, width),
        own_in, w_out.reshape(8, 2, 64, 128), tap_cols, own_gate, own_up,
        w_down.reshape(8, 4, 144, 128), gains, ids,
    )
    lo, gi, od, og, ou, oi, oo, small = outs
    back = lambda a: a.astype(F32)
    grad_in = back(oi).reshape(2, 3, 64, width).transpose(3, 1, 0, 2).reshape(width, 384)
    grad_out = back(oo).reshape(2, 8, 64, 128).transpose(1, 0, 2, 3).reshape(width, 128)
    grad_gate = back(og).reshape(576, width).T
    grad_up = back(ou).reshape(576, width).T
    grad_down = back(od).reshape(4, 8, 144, 128).transpose(1, 0, 2, 3).reshape(4608, 128)
    grad_taps = small[:, 0:64, 0:3].reshape(128, 3).T
    return (
        lo.reshape(2, 256, width), gi.reshape(2, 256, width),
        grad_in, grad_out, grad_gate, grad_up, grad_down, grad_taps,
        small[0, 64] + small[1, 64], small[0, 65] + small[1, 65],
    )


def solution(mesh):
    grouped = mesh.shape["rep"] == 4 and mesh.shape["fsdp"] == 8
    return jax.shard_map(
        grouped_device if grouped else per_device,
        mesh=mesh,
        in_specs=(
            P(None, ("rep", "fsdp"), None),
            P(None, ("rep", "fsdp")),
            P(None, "fsdp"),
            P(None, "fsdp"),
            P(None, "fsdp"),
            P(None, "fsdp"),
            P(None, "fsdp"),
            P(None, "fsdp"),
            P("fsdp"),
            P("fsdp"),
            P(None, ("rep", "fsdp"), None),
        ),
        out_specs=(
            P(None, ("rep", "fsdp"), None),
            P(None, ("rep", "fsdp"), None),
            P(None, "fsdp"),
            P(None, "fsdp"),
            P(None, "fsdp"),
            P(None, "fsdp"),
            P(None, "fsdp"),
            P(None, "fsdp"),
            P("fsdp"),
            P("fsdp"),
        ),
        check_vma=False,
    )
```
